128 devices in a mesh: seq: 16 (over x_hi, y, core), tp: 8 (over z, x_lo).
Axes of the slice: x: 4 (x_hi: 2, x_lo: 2; x = x_hi * 2 + x_lo), y: 4, z: 4, core: 2. Of those that a mesh axis runs over, the one named last changes fastest.
Arguments:
- fine_stream: bfloat16 [16384, 2048], P(('seq', 'tp')), may hold values from -20 to 20
- queries: bfloat16 [16384, 1024], P(('seq', 'tp')), may hold values from -80 to 80
- keys: bfloat16 [16384, 1024], P(('seq', 'tp')), may hold values from -8 to 8
- values: bfloat16 [16384, 1024], P(('seq', 'tp')), may hold values from -6 to 6
- out_weight: bfloat16 [1024, 2048], replicated, may hold values from -0.1875 to 0.1875
- norm_gain: float32 [2048], replicated, may hold values from 0.25 to 1.75
- gate_weight: bfloat16 [2048, 5632], P(None, 'tp'), may hold values from -0.125 to 0.125
- up_weight: bfloat16 [2048, 5632], P(None, 'tp'), may hold values from -0.125 to 0.125
- down_weight: bfloat16 [5632, 2048], P('tp'), may hold values from -0.078125 to 0.078125
- cotangent: bfloat16 [16384, 2048], P(('seq', 'tp')), may hold values from -12 to 12
Outputs:
- section_out: bfloat16 [16384, 2048], P(('seq', 'tp'))
- stream_grad: bfloat16 [16384, 2048], P(('seq', 'tp'))
- gate_grad: float32 [2048, 5632], P('seq', 'tp')
- up_grad: float32 [2048, 5632], P('seq', 'tp')
- down_grad: float32 [5632, 2048], P('tp', 'seq')
- gain_grad: float32 [2048], replicated
The draws below stay inside these ranges and needn't reach their ends.
All inputs are finite; a program needn't handle non-finite values.
Results may differ from the reference program's by a relative error of at most 0.02.
Values may be sent and summed in bfloat16 or wider, within the bound.
A program may use at most 128 MiB of HBM per device.

```python
import jax
import jax.numpy as jnp
from jax import lax

D = 2048
HEADS = 8
HEAD = 128
FF = 5632
SHORTEN = 8
TOKENS = 16384
CROWS = 2048


def head_pair(key):
    scale = 1.64
    keys_base = jnp.clip(jax.random.normal(jax.random.fold_in(key, 101), (TOKENS, HEADS * HEAD)), -4.0, 4.0) * scale
    queries_base = jnp.clip(jax.random.normal(jax.random.fold_in(key, 102), (TOKENS, HEADS * HEAD)), -4.0, 4.0) * scale
    return (keys_base, queries_base)


def draw_keys(key, part):
    keys_base, queries_base = head_pair(key)
    return keys_base.astype(jnp.bfloat16)


def draw_queries(key, part):
    keys_base, queries_base = head_pair(key)
    return queries_base.astype(jnp.bfloat16)


def draw_fine_stream(key, part):
    key = jax.random.fold_in(key, 7)
    row_scale = 10.0 ** jax.random.uniform(jax.random.fold_in(key, 1), (TOKENS, 1), minval=-0.5, maxval=0.5)
    col_scale = 10.0 ** jax.random.uniform(jax.random.fold_in(key, 2), (1, D), minval=-0.5, maxval=0.5)
    core = jnp.clip(jax.random.normal(jax.random.fold_in(key, 3), (TOKENS, D)), -4.0, 4.0)
    return (0.5 * core * row_scale * col_scale).astype(jnp.bfloat16)


def draw_cotangent(key, part):
    key = jax.random.fold_in(key, 9)
    rising = 1.0 + 2.0 * jnp.arange(TOKENS, dtype=jnp.float32)[:, None] / (TOKENS - 1)
    core = jnp.clip(jax.random.normal(jax.random.fold_in(key, 1), (TOKENS, D)), -4.0, 4.0)
    return (core * rising).astype(jnp.bfloat16)


def levels(key, dims, split, smallest, largest):
    gain = 1.0
    for dim, shards_of in split:
        heights = jax.random.uniform(jax.random.fold_in(jax.random.fold_in(key, 6), dim), (shards_of,), jnp.float32, smallest / len(split), largest / len(split))
        gain = gain * jnp.repeat(jnp.exp(heights), dims[dim] // shards_of).reshape((-1,) + (1,) * (len(dims) - 1 - dim))
    return gain


def centred(rng, dims, spread, most, split=(), kind=jnp.bfloat16):
    entries = jax.random.normal(rng, dims, jnp.float32) * spread
    if len(split) > 0:
        entries = levels(rng, dims, split, -0.22, 0.18) * entries
    return jnp.clip(entries, min=-most, max=most).astype(kind)


def setup_inputs(seed: int = 0) -> dict:
    splits = jax.random.split(jax.random.key(seed), 11)
    return {
        "fine_stream": draw_fine_stream(jax.random.fold_in(splits[10], 71), 0),
        "queries": draw_queries(jax.random.fold_in(splits[10], 71), 0),
        "keys": draw_keys(jax.random.fold_in(splits[10], 71), 0),
        "values": centred(splits[3], (TOKENS, HEADS * HEAD), 1.0, 6.0, ((0, 128),)),
        "out_weight": centred(splits[4], (HEADS * HEAD, D), (HEADS * HEAD) ** -0.5, 0.1875),
        "norm_gain": jnp.clip(1.0 + 0.15 * jax.random.normal(splits[5], (D,), jnp.float32), 0.25, 1.75),
        "gate_weight": centred(splits[6], (D, FF), D ** -0.5, 0.125, ((1, 8),)),
        "up_weight": centred(splits[7], (D, FF), D ** -0.5, 0.125, ((1, 8),)),
        "down_weight": centred(splits[8], (FF, D), FF ** -0.5, 0.078125, ((0, 8),)),
        "cotangent": draw_cotangent(jax.random.fold_in(splits[10], 71), 0),
    }


def attend(queries, keys, values):
    block = min(512, TOKENS)
    count = TOKENS // block
    key_all = keys.astype(jnp.float32).reshape(TOKENS, HEADS, HEAD)
    value_all = values.astype(jnp.float32).reshape(TOKENS, HEADS, HEAD)
    positions = jnp.arange(TOKENS, dtype=jnp.int32)
    query_blocks = queries.reshape(count, block, HEADS, HEAD)
    starts = (jnp.arange(count, dtype=jnp.int32) * block).astype(jnp.int32)

    def one_block(pair):
        query_block, start = pair
        scores = jnp.einsum('qhd,khd->hqk', query_block.astype(jnp.float32), key_all) * HEAD ** (-0.5)
        visible = (start + jnp.arange(block, dtype=jnp.int32))[:, None] >= positions[None, :]
        scores = jnp.where(visible[None], scores, -jnp.inf)
        top = lax.optimization_barrier(jnp.max(scores, axis=-1, keepdims=True))
        weights = jnp.exp(scores - top)
        totals = lax.optimization_barrier(jnp.sum(weights, axis=-1))
        rounded = lax.optimization_barrier(weights.astype(jnp.bfloat16))
        mixed = jnp.einsum('hqk,khd->qhd', rounded.astype(jnp.float32), value_all)
        return (mixed / totals.T[..., None]).astype(jnp.bfloat16)
    result = lax.map(one_block, (query_blocks, starts))
    return result.reshape(TOKENS, HEADS * HEAD)

def reference(fine_stream, queries, keys, values, out_weight, norm_gain, gate_weight, up_weight, down_weight, cotangent):
    attention = attend(queries, keys, values)
    stream = (fine_stream.astype(jnp.float32) + jnp.dot(attention, out_weight, preferred_element_type=jnp.float32)).astype(jnp.bfloat16)
    padded = jnp.concatenate([jnp.zeros((SHORTEN - 1, D), jnp.bfloat16), stream], 0)[:TOKENS]
    coarse = padded.astype(jnp.float32).reshape(CROWS, SHORTEN, D).sum(1) / SHORTEN
    rstd = lax.rsqrt(lax.optimization_barrier(jnp.mean(coarse * coarse, axis=-1, keepdims=True)) + 1e-05)
    base = coarse * rstd
    normed = (base * norm_gain).astype(jnp.bfloat16)
    gate = jnp.dot(normed, gate_weight, preferred_element_type=jnp.float32)
    up = jnp.dot(normed, up_weight, preferred_element_type=jnp.float32)
    sig = jax.nn.sigmoid(gate)
    hidden = (gate * sig * up).astype(jnp.bfloat16)
    coarse_out = coarse + jnp.dot(hidden, down_weight, preferred_element_type=jnp.float32)
    section_out = (stream.astype(jnp.float32).reshape(CROWS, SHORTEN, D) + coarse_out[:, None, :]).reshape(TOKENS, D).astype(jnp.bfloat16)
    grad = cotangent.astype(jnp.float32)
    coarse_grad = grad.reshape(CROWS, SHORTEN, D).sum(1)
    coarse_grad_b = coarse_grad.astype(jnp.bfloat16)
    contract_last = (((1,), (1,)), ((), ()))
    contract_first = (((0,), (0,)), ((), ()))
    hidden_grad = lax.dot_general(coarse_grad_b, down_weight, contract_last, preferred_element_type=jnp.float32)
    gate_delta = (hidden_grad * up * sig * (1.0 + gate * (1.0 - sig))).astype(jnp.bfloat16)
    up_delta = (hidden_grad * gate * sig).astype(jnp.bfloat16)
    normed_grad = lax.dot_general(gate_delta, gate_weight, contract_last, preferred_element_type=jnp.float32) + lax.dot_general(up_delta, up_weight, contract_last, preferred_element_type=jnp.float32)
    gain_grad = lax.optimization_barrier(jnp.sum(normed_grad * base, axis=0))
    scaled = normed_grad * norm_gain
    coarse_total = coarse_grad + rstd * (scaled - base * lax.optimization_barrier(jnp.mean(scaled * base, axis=-1, keepdims=True)))
    extended = jnp.concatenate([coarse_total, jnp.zeros((1, D), jnp.float32)], 0)
    index = ((jnp.arange(TOKENS, dtype=jnp.int32) + (SHORTEN - 1)) // SHORTEN).astype(jnp.int32)
    stream_grad = (grad + jnp.take(extended, index, axis=0) / SHORTEN).astype(jnp.bfloat16)
    gate_grad = lax.dot_general(normed, gate_delta, contract_first, preferred_element_type=jnp.float32)
    up_grad = lax.dot_general(normed, up_delta, contract_first, preferred_element_type=jnp.float32)
    down_grad = lax.dot_general(hidden, coarse_grad_b, contract_first, preferred_element_type=jnp.float32)
    return (section_out, stream_grad, gate_grad, up_grad, down_grad, gain_grad)
```

```python
import math

import jax
import jax.numpy as jnp
from jax import lax
from jax.experimental import pallas as pl
from jax.experimental.pallas import tpu as pltpu
from jax.sharding import PartitionSpec as P

D = 2048
HEAD = 128
SHORTEN = 8
MESH = pl.DeviceIdType.MESH
TP = 8

contract_last = (((1,), (1,)), ((), ()))
contract_first = (((0,), (0,)), ((), ()))
very_low = -1e30
POWER = math.log2(math.e) * HEAD ** (-0.5)
TILE = 256


def places():
    s, t = lax.axis_index("seq"), lax.axis_index("tp")
    half, block = s // 8, lax.rem(s, 8)
    y, core = block // 2, lax.rem(block, 2)
    sib = half * 8 + y * 2 + (1 - core)
    up = half * 8 + lax.rem(y + 1, 4) * 2 + core
    down = half * 8 + lax.rem(y + 3, 4) * 2 + core
    partner = (1 - half) * 8 + block
    return s, t, half, block, y, core, sib, up, down, partner


def attend_kernel(
    q_ref, k_ref, v_ref, att_ref,
    vt_src, q_own, q_far, k_all, vt_all, m_ref, l_ref, acc_ref, far_m, far_l, far_acc,
    o_out, o_in, stat_out, stat_in, o_rows, att, send, recv, local_sem,
):
    s, t, half, block, y, core, sib, up, down, partner = places()
    rows = q_ref.shape[0]

    barrier = pltpu.get_barrier_semaphore()
    peers = [(s, lax.rem(t + off, TP)) for off in range(1, TP)]
    peers += [(sib, t), (up, t), (down, t), (partner, t)]
    for peer in peers:
        pl.semaphore_signal(barrier, inc=1, device_id=peer, device_id_type=MESH)
    pl.semaphore_wait(barrier, len(peers))

    def remote(kind, src, dst, device):
        return pltpu.make_async_remote_copy(
            src_ref=src, dst_ref=dst, send_sem=send.at[kind], recv_sem=recv.at[kind],
            device_id=device, device_id_type=MESH,
        )

    def lanes(index):
        return pl.ds(pl.multiple_of(index * HEAD, HEAD), HEAD)

    def band(index):
        return pl.ds(pl.multiple_of(index * rows, rows), rows)

    q_copies, k_copies, v_copies = [], [], []
    for off in range(1, TP):
        peer = lax.rem(t + off, TP)
        cp = remote(off - 1, q_ref.at[:, lanes(peer)], q_own.at[band(t), :], (s, peer))
        cp.start()
        q_copies.append(cp)
    for off in range(1, TP):
        peer = lax.rem(t + off, TP)
        cp = remote(6 + off, k_ref.at[:, lanes(peer)], k_all.at[block, band(t), :], (s, peer))
        cp.start()
        k_copies.append(cp)
    for h in range(TP):
        vt_src[h] = v_ref[:, h * HEAD : (h + 1) * HEAD].astype(jnp.float32).T.astype(jnp.bfloat16)
    for off in range(1, TP):
        peer = lax.rem(t + off, TP)
        cp = remote(13 + off, vt_src.at[peer], vt_all.at[block, :, band(t)], (s, peer))
        cp.start()
        v_copies.append(cp)
    own = [
        pltpu.make_async_copy(q_ref.at[:, lanes(t)], q_own.at[band(t), :], local_sem.at[0]),
        pltpu.make_async_copy(k_ref.at[:, lanes(t)], k_all.at[block, band(t), :], local_sem.at[1]),
        pltpu.make_async_copy(vt_src.at[t], vt_all.at[block, :, band(t)], local_sem.at[2]),
    ]
    for cp in own:
        cp.start()

    for ref, value in ((m_ref, very_low), (l_ref, 0.0), (acc_ref, 0.0),
                       (far_m, very_low), (far_l, 0.0), (far_acc, 0.0)):
        ref[...] = jnp.full(ref.shape, value, jnp.float32)

    for cp in own:
        cp.wait()
    for cp in q_copies:
        cp.wait_recv()
    q_over = remote(35, q_own, q_far, (partner, t))

    @pl.when(half == 1)
    def _():
        q_over.start()

    k_mine, v_mine = k_all.at[block], vt_all.at[block]
    gather = [
        remote(21, k_mine, k_mine, (up, t)), remote(22, k_mine, k_mine, (down, t)),
        remote(23, k_mine, k_mine, (sib, t)),
        remote(24, v_mine, v_mine, (up, t)), remote(25, v_mine, v_mine, (down, t)),
        remote(26, v_mine, v_mine, (sib, t)),
    ]
    for cp in k_copies:
        cp.wait_recv()
    for cp in gather[:3]:
        cp.start()
    for cp in v_copies:
        cp.wait_recv()
    for cp in gather[3:]:
        cp.start()

    def block_of(step):
        j = step // 2
        dy = j + (j // 2) * (5 - 2 * j)
        return lax.rem(y + dy, 4) * 2 + lax.rem(core + step, 2)

    def fold(q_all, m_all, l_all, acc_all, key_block, tile, diagonal):
        span = pl.ds(pl.multiple_of(tile * (2 * TILE), 2 * TILE), 2 * TILE)
        keys = k_all[key_block]
        scores = [
            lax.dot_general(
                keys, q_all[pl.ds(pl.multiple_of((2 * tile + u) * TILE, TILE), TILE), :],
                contract_last, preferred_element_type=jnp.float32,
            )
            for u in range(2)
        ]
        values = vt_all[key_block]
        for u in range(2):
            cols = pl.ds(pl.multiple_of((2 * tile + u) * TILE, TILE), TILE)
            st = scores[u]
            if diagonal:
                key_pos = lax.broadcasted_iota(jnp.int32, st.shape, 0)
                query_pos = lax.broadcasted_iota(jnp.int32, st.shape, 1) + (2 * tile + u) * TILE
                st = jnp.where(key_pos <= query_pos, st, very_low)
            before = m_all[:, cols]
            fresh = jnp.maximum(before, jnp.max(st, axis=0, keepdims=True))
            weights = jnp.exp2((st - fresh) * POWER)
            factor = jnp.exp2((before - fresh) * POWER)
            m_all[:, cols] = fresh
            l_all[:, cols] = l_all[:, cols] * factor + jnp.sum(weights, axis=0, keepdims=True)
            acc_all[:, cols] = acc_all[:, cols] * factor + jnp.dot(
                values, weights.astype(jnp.bfloat16), preferred_element_type=jnp.float32
            )

    tiles = q_own.shape[0] // (2 * TILE)

    def own_steps(first, last):
        @pl.loop(first, last)
        def _(step):
            key_block = block_of(step)

            @pl.when(key_block < block)
            def _():
                @pl.loop(0, tiles)
                def _(tile):
                    fold(q_own, m_ref, l_ref, acc_ref, key_block, tile, False)

    def far_steps(first, last):
        @pl.when(half == 0)
        def _():
            @pl.loop(first, last)
            def _(step):
                @pl.loop(0, tiles)
                def _(tile):
                    fold(q_far, far_m, far_l, far_acc, block_of(step), tile, False)

    @pl.loop(0, tiles)
    def _(tile):
        fold(q_own, m_ref, l_ref, acc_ref, block, tile, True)

    gather[2].wait_recv()
    gather[5].wait_recv()

    @pl.when(half == 0)
    def _():
        q_over.wait_recv()

    far_steps(0, 2)
    k_below, v_below = k_all.at[block_of(4)], vt_all.at[block_of(4)]
    k_above, v_above = k_all.at[block_of(2)], vt_all.at[block_of(2)]
    k_across, v_across = k_all.at[block_of(6)], vt_all.at[block_of(6)]
    passed = [
        remote(27, k_below, k_below, (up, t)), remote(28, v_above, v_above, (down, t)),
        remote(29, k_above, k_above, (sib, t)), remote(30, v_above, v_above, (sib, t)),
        remote(31, k_below, k_below, (sib, t)), remote(32, v_below, v_below, (sib, t)),
        remote(33, k_across, k_across, (sib, t)), remote(34, v_across, v_across, (sib, t)),
    ]
    gather[0].wait_recv()
    passed[0].start()
    passed[4].start()
    gather[1].wait_recv()
    passed[2].start()
    gather[4].wait_recv()
    passed[1].start()
    passed[3].start()
    gather[3].wait_recv()
    passed[5].start()
    far_steps(2, 3)
    for cp in passed[2:4]:
        cp.wait_recv()
    far_steps(3, 5)
    for cp in passed[4:6]:
        cp.wait_recv()
    passed[0].wait_recv()
    passed[6].start()
    passed[1].wait_recv()
    passed[7].start()
    far_steps(5, 7)
    for cp in passed[6:8]:
        cp.wait_recv()
    far_steps(7, 8)

    o_over = remote(36, o_out, o_in, (partner, t))
    stat_over = remote(37, stat_out, stat_in, (partner, t))

    @pl.when(half == 0)
    def _():
        o_out[...] = (far_acc[...] / far_l[...]).astype(jnp.bfloat16)
        stat_out[0:1] = far_m[...]
        stat_out[1:2] = far_l[...]
        o_over.start()
        stat_over.start()
        o_in[...] = jnp.zeros(o_in.shape, o_in.dtype)
        stat_in[0:1] = jnp.full(far_m.shape, very_low, jnp.float32)
        stat_in[1:2] = jnp.zeros(far_l.shape, jnp.float32)

    own_steps(1, 8)

    @pl.when(half == 1)
    def _():
        o_over.wait_recv()
        stat_over.wait_recv()

    other_m, other_l = stat_in[0:1], stat_in[1:2]
    top = jnp.maximum(m_ref[...], other_m)
    mine = jnp.exp2((m_ref[...] - top) * POWER)
    other = other_l * jnp.exp2((other_m - top) * POWER)
    total = l_ref[...] * mine + other
    mine, other = mine / total, other / total
    back = []
    for h in range(TP):
        cols = slice(h * rows, (h + 1) * rows)
        mixed = acc_ref[:, cols] * mine[:, cols] + o_in[:, cols].astype(jnp.float32) * other[:, cols]
        o_rows[h] = mixed.T.astype(jnp.bfloat16)
    for off in range(1, TP):
        peer = lax.rem(t + off, TP)
        cp = remote(37 + off, o_rows.at[peer], att.at[:, lanes(t)], (s, peer))
        cp.start()
        back.append(cp)
    own_back = pltpu.make_async_copy(o_rows.at[t], att.at[:, lanes(t)], local_sem.at[3])
    own_back.start()
    own_back.wait()
    for cp in back:
        cp.wait_recv()
    att_ref[...] = att[...]

    for cp in q_copies + k_copies + v_copies + gather + passed + back:
        cp.wait_send()

    @pl.when(half == 1)
    def _():
        q_over.wait_send()

    @pl.when(half == 0)
    def _():
        o_over.wait_send()
        stat_over.wait_send()


def attention_of(queries, keys, values):
    rows, width = queries.shape
    group = rows * TP
    f32, bf16 = jnp.float32, jnp.bfloat16
    vmem = pl.BlockSpec(memory_space=pltpu.VMEM)
    return pl.pallas_call(
        attend_kernel,
        out_shape=jax.ShapeDtypeStruct((rows, width), bf16),
        in_specs=[vmem] * 3,
        out_specs=vmem,
        scratch_shapes=[
            pltpu.VMEM((TP, HEAD, rows), bf16),
            pltpu.VMEM((group, HEAD), bf16),
            pltpu.VMEM((group, HEAD), bf16),
            pltpu.VMEM((8, group, HEAD), bf16),
            pltpu.VMEM((8, HEAD, group), bf16),
            pltpu.VMEM((1, group), f32),
            pltpu.VMEM((1, group), f32),
            pltpu.VMEM((HEAD, group), f32),
            pltpu.VMEM((1, group), f32),
            pltpu.VMEM((1, group), f32),
            pltpu.VMEM((HEAD, group), f32),
            pltpu.VMEM((HEAD, group), bf16),
            pltpu.VMEM((HEAD, group), bf16),
            pltpu.VMEM((8, group), f32),
            pltpu.VMEM((8, group), f32),
            pltpu.VMEM((TP, rows, HEAD), bf16),
            pltpu.VMEM((rows, width), bf16),
            pltpu.SemaphoreType.DMA((45,)),
            pltpu.SemaphoreType.DMA((45,)),
            pltpu.SemaphoreType.DMA((4,)),
        ],
        compiler_params=pltpu.CompilerParams(
            collective_id=0, has_side_effects=True, vmem_limit_bytes=48 * 1024 * 1024
        ),
        name="attention",
    )(queries, keys, values)


def shifted(value, axis, steps):
    count = lax.axis_size(axis)
    leading, last = (max(0, -steps), min(count, count - steps))
    return lax.ppermute(value, axis, [(source, source + steps) for source in range(leading, last)])


def on_device(
    fine_stream,
    queries,
    keys,
    values,
    out_weight,
    norm_gain,
    gate_weight,
    up_weight,
    down_weight,
    cotangent,
):
    tok = fine_stream.shape[0]
    attention = attention_of(queries, keys, values)
    projected = jnp.dot(attention, out_weight, preferred_element_type=jnp.float32)
    stream = (fine_stream.astype(jnp.float32) + projected).astype(jnp.bfloat16)
    crows = tok // SHORTEN
    border = shifted(stream[tok - SHORTEN :], ("seq", "tp"), 1)
    extended = jnp.concatenate([border[1:], stream], 0)[:tok]
    coarse = extended.astype(jnp.float32).reshape(crows, SHORTEN, D).sum(1) / SHORTEN
    rstd = lax.rsqrt(jnp.mean(coarse * coarse, axis=-1, keepdims=True) + 1e-05)
    base = coarse * rstd
    normed = (base * norm_gain).astype(jnp.bfloat16)
    normed_group = lax.all_gather(normed, "tp", axis=0, tiled=True)
    gate = jnp.dot(normed_group, gate_weight, preferred_element_type=jnp.float32)
    up = jnp.dot(normed_group, up_weight, preferred_element_type=jnp.float32)
    sig = jax.nn.sigmoid(gate)
    hidden = (gate * sig * up).astype(jnp.bfloat16)
    coarse_out = coarse + lax.psum_scatter(
        jnp.dot(hidden, down_weight, preferred_element_type=jnp.float32).astype(jnp.bfloat16),
        "tp",
        scatter_dimension=0,
        tiled=True,
    ).astype(jnp.float32)
    section_out = (
        (stream.astype(jnp.float32).reshape(crows, SHORTEN, D) + coarse_out[:, None, :])
        .reshape(tok, D)
        .astype(jnp.bfloat16)
    )
    grad = cotangent.astype(jnp.float32)
    coarse_grad = grad.reshape(crows, SHORTEN, D).sum(1)
    coarse_grad_b = coarse_grad.astype(jnp.bfloat16)
    grad_group = lax.all_gather(coarse_grad_b, "tp", axis=0, tiled=True)
    hidden_grad = lax.dot_general(
        grad_group, down_weight, contract_last, preferred_element_type=jnp.float32
    )
    gate_delta = (hidden_grad * up * sig * (1.0 + gate * (1.0 - sig))).astype(jnp.bfloat16)
    up_delta = (hidden_grad * gate * sig).astype(jnp.bfloat16)
    normed_grad = lax.psum_scatter(
        (
            lax.dot_general(
                gate_delta, gate_weight, contract_last, preferred_element_type=jnp.float32
            )
            + lax.dot_general(
                up_delta, up_weight, contract_last, preferred_element_type=jnp.float32
            )
        ).astype(jnp.bfloat16),
        "tp",
        scatter_dimension=0,
        tiled=True,
    ).astype(jnp.float32)
    gain_grad = lax.psum(jnp.sum(normed_grad * base, axis=0), ("seq", "tp"))
    scaled = normed_grad * norm_gain
    coarse_total = coarse_grad + rstd * (
        scaled - base * jnp.mean(scaled * base, axis=-1, keepdims=True)
    )
    following = shifted(coarse_total[:1], ("seq", "tp"), -1)
    ahead = jnp.concatenate([coarse_total[1:], following], 0)
    spread = jnp.broadcast_to(ahead[:, None, :], (crows, SHORTEN, D)).reshape(tok, D)
    contrib = jnp.concatenate([coarse_total[:1], spread[: tok - 1]], 0)
    stream_grad = (grad + contrib / SHORTEN).astype(jnp.bfloat16)
    gate_local = lax.dot_general(
        normed_group, gate_delta, contract_first, preferred_element_type=jnp.float32
    )
    up_local = lax.dot_general(
        normed_group, up_delta, contract_first, preferred_element_type=jnp.float32
    )
    gate_grad, up_grad = (
        lax.psum_scatter(
            gate_local.astype(jnp.bfloat16), "seq", scatter_dimension=0, tiled=True
        ).astype(jnp.float32),
        lax.psum_scatter(
            up_local.astype(jnp.bfloat16), "seq", scatter_dimension=0, tiled=True
        ).astype(jnp.float32),
    )
    down_local = lax.dot_general(
        hidden, grad_group, contract_first, preferred_element_type=jnp.float32
    )
    down_grad = lax.psum_scatter(
        down_local.astype(jnp.bfloat16), "seq", scatter_dimension=1, tiled=True
    ).astype(jnp.float32)
    return (section_out, stream_grad, gate_grad, up_grad, down_grad, gain_grad)


def solution(mesh):
    return jax.shard_map(
        on_device,
        mesh=mesh,
        in_specs=(
            P(("seq", "tp"), None),
            P(("seq", "tp"), None),
            P(("seq", "tp"), None),
            P(("seq", "tp"), None),
            P(),
            P(),
            P(None, "tp"),
            P(None, "tp"),
            P("tp", None),
            P(("seq", "tp"), None),
        ),
        out_specs=(
            P(("seq", "tp"), None),
            P(("seq", "tp"), None),
            P("seq", "tp"),
            P("seq", "tp"),
            P("tp", "seq"),
            P(),
        ),
        check_vma=False,
    )
```

```python
import math

import jax
import jax.numpy as jnp
from jax import lax
from jax.experimental import pallas as pl
from jax.experimental.pallas import tpu as pltpu
from jax.sharding import PartitionSpec as P

D = 2048
HEAD = 128
SHORTEN = 8
MESH = pl.DeviceIdType.MESH
TP = 8

contract_last = (((1,), (1,)), ((), ()))
contract_first = (((0,), (0,)), ((), ()))
very_low = -1e30
POWER = math.log2(math.e) * HEAD ** (-0.5)
TILE = 256


def places():
    s, t = lax.axis_index("seq"), lax.axis_index("tp")
    half, block = s // 8, lax.rem(s, 8)
    y, core = block // 2, lax.rem(block, 2)
    sib = half * 8 + y * 2 + (1 - core)
    up = half * 8 + lax.rem(y + 1, 4) * 2 + core
    down = half * 8 + lax.rem(y + 3, 4) * 2 + core
    partner = (1 - half) * 8 + block
    return s, t, half, block, y, core, sib, up, down, partner


def attend_kernel(
    q_ref, k_ref, v_ref, att_ref,
    vt_src, q_own, q_far, k_all, vt_all, m_ref, l_ref, acc_ref, far_m, far_l, far_acc,
    o_out, o_in, stat_out, stat_in, o_rows, att, send, recv, local_sem,
):
    s, t, half, block, y, core, sib, up, down, partner = places()
    rows = q_ref.shape[0]

    barrier = pltpu.get_barrier_semaphore()
    peers = [(s, lax.rem(t + off, TP)) for off in range(1, TP)]
    peers += [(sib, t), (up, t), (down, t), (partner, t)]
    for peer in peers:
        pl.semaphore_signal(barrier, inc=1, device_id=peer, device_id_type=MESH)
    pl.semaphore_wait(barrier, len(peers))

    def remote(kind, src, dst, device):
        return pltpu.make_async_remote_copy(
            src_ref=src, dst_ref=dst, send_sem=send.at[kind], recv_sem=recv.at[kind],
            device_id=device, device_id_type=MESH,
        )

    def lanes(index):
        return pl.ds(pl.multiple_of(index * HEAD, HEAD), HEAD)

    def band(index):
        return pl.ds(pl.multiple_of(index * rows, rows), rows)

    q_copies, k_copies, v_copies = [], [], []
    for off in range(1, TP):
        peer = lax.rem(t + off, TP)
        cp = remote(off - 1, q_ref.at[:, lanes(peer)], q_own.at[band(t), :], (s, peer))
        cp.start()
        q_copies.append(cp)
    for off in range(1, TP):
        peer = lax.rem(t + off, TP)
        cp = remote(6 + off, k_ref.at[:, lanes(peer)], k_all.at[block, band(t), :], (s, peer))
        cp.start()
        k_copies.append(cp)
    for h in range(TP):
        vt_src[h] = v_ref[:, h * HEAD : (h + 1) * HEAD].astype(jnp.float32).T.astype(jnp.bfloat16)
    for off in range(1, TP):
        peer = lax.rem(t + off, TP)
        cp = remote(13 + off, vt_src.at[peer], vt_all.at[block, :, band(t)], (s, peer))
        cp.start()
        v_copies.append(cp)
    own = [
        pltpu.make_async_copy(q_ref.at[:, lanes(t)], q_own.at[band(t), :], local_sem.at[0]),
        pltpu.make_async_copy(k_ref.at[:, lanes(t)], k_all.at[block, band(t), :], local_sem.at[1]),
        pltpu.make_async_copy(vt_src.at[t], vt_all.at[block, :, band(t)], local_sem.at[2]),
    ]
    for cp in own:
        cp.start()

    for ref, value in ((m_ref, very_low), (l_ref, 0.0), (acc_ref, 0.0),
                       (far_m, very_low), (far_l, 0.0), (far_acc, 0.0)):
        ref[...] = jnp.full(ref.shape, value, jnp.float32)

    for cp in own:
        cp.wait()
    for cp in q_copies:
        cp.wait_recv()
    q_over = remote(35, q_own, q_far, (partner, t))

    @pl.when(half == 1)
    def _():
        q_over.start()

    k_mine, v_mine = k_all.at[block], vt_all.at[block]
    gather = [
        remote(21, k_mine, k_mine, (up, t)), remote(22, k_mine, k_mine, (down, t)),
        remote(23, k_mine, k_mine, (sib, t)),
        remote(24, v_mine, v_mine, (up, t)), remote(25, v_mine, v_mine, (down, t)),
        remote(26, v_mine, v_mine, (sib, t)),
    ]
    for cp in k_copies:
        cp.wait_recv()
    for cp in gather[:3]:
        cp.start()
    for cp in v_copies:
        cp.wait_recv()
    for cp in gather[3:]:
        cp.start()

    def block_of(step):
        j = step // 2
        dy = j + (j // 2) * (5 - 2 * j)
        return lax.rem(y + dy, 4) * 2 + lax.rem(core + step, 2)

    def fold(q_all, m_all, l_all, acc_all, key_block, tile, diagonal):
        span = pl.ds(pl.multiple_of(tile * (2 * TILE), 2 * TILE), 2 * TILE)
        keys = k_all[key_block]
        scores = [
            lax.dot_general(
                keys, q_all[pl.ds(pl.multiple_of((2 * tile + u) * TILE, TILE), TILE), :],
                contract_last, preferred_element_type=jnp.float32,
            )
            for u in range(2)
        ]
        values = vt_all[key_block]
        for u in range(2):
            cols = pl.ds(pl.multiple_of((2 * tile + u) * TILE, TILE), TILE)
            st = scores[u]
            if diagonal:
                key_pos = lax.broadcasted_iota(jnp.int32, st.shape, 0)
                query_pos = lax.broadcasted_iota(jnp.int32, st.shape, 1) + (2 * tile + u) * TILE
                st = jnp.where(key_pos <= query_pos, st, very_low)
            before = m_all[:, cols]
            fresh = jnp.maximum(before, jnp.max(st, axis=0, keepdims=True))
            weights = jnp.exp2((st - fresh) * POWER)
            factor = jnp.exp2((before - fresh) * POWER)
            m_all[:, cols] = fresh
            l_all[:, cols] = l_all[:, cols] * factor + jnp.sum(weights, axis=0, keepdims=True)
            acc_all[:, cols] = acc_all[:, cols] * factor + jnp.dot(
                values, weights.astype(jnp.bfloat16), preferred_element_type=jnp.float32
            )

    tiles = q_own.shape[0] // (2 * TILE)

    def own_steps(first, last):
        @pl.loop(first, last)
        def _(step):
            key_block = block_of(step)

            @pl.when(key_block < block)
            def _():
                @pl.loop(0, tiles)
                def _(tile):
                    fold(q_own, m_ref, l_ref, acc_ref, key_block, tile, False)

    def far_steps(first, last):
        @pl.when(half == 0)
        def _():
            @pl.loop(first, last)
            def _(step):
                @pl.loop(0, tiles)
                def _(tile):
                    fold(q_far, far_m, far_l, far_acc, block_of(step), tile, False)

    @pl.loop(0, tiles)
    def _(tile):
        fold(q_own, m_ref, l_ref, acc_ref, block, tile, True)

    gather[2].wait_recv()
    gather[5].wait_recv()

    @pl.when(half == 0)
    def _():
        q_over.wait_recv()

    far_steps(0, 2)
    k_below, v_below = k_all.at[block_of(4)], vt_all.at[block_of(4)]
    k_above, v_above = k_all.at[block_of(2)], vt_all.at[block_of(2)]
    k_across, v_across = k_all.at[block_of(6)], vt_all.at[block_of(6)]
    passed = [
        remote(27, k_below, k_below, (up, t)), remote(28, v_above, v_above, (down, t)),
        remote(29, k_above, k_above, (sib, t)), remote(30, v_above, v_above, (sib, t)),
        remote(31, k_below, k_below, (sib, t)), remote(32, v_below, v_below, (sib, t)),
        remote(33, k_across, k_across, (sib, t)), remote(34, v_across, v_across, (sib, t)),
    ]
    gather[0].wait_recv()
    passed[0].start()
    passed[4].start()
    gather[1].wait_recv()
    passed[2].start()
    gather[4].wait_recv()
    passed[1].start()
    passed[3].start()
    gather[3].wait_recv()
    passed[5].start()
    far_steps(2, 3)
    for cp in passed[2:4]:
        cp.wait_recv()
    far_steps(3, 5)
    for cp in passed[4:6]:
        cp.wait_recv()
    passed[0].wait_recv()
    passed[6].start()
    passed[1].wait_recv()
    passed[7].start()
    far_steps(5, 7)
    for cp in passed[6:8]:
        cp.wait_recv()
    far_steps(7, 8)

    o_over = remote(36, o_out, o_in, (partner, t))
    stat_over = remote(37, stat_out, stat_in, (partner, t))

    @pl.when(half == 0)
    def _():
        o_out[...] = (far_acc[...] / far_l[...]).astype(jnp.bfloat16)
        stat_out[0:1] = far_m[...]
        stat_out[1:2] = far_l[...]
        o_over.start()
        stat_over.start()
        o_in[...] = jnp.zeros(o_in.shape, o_in.dtype)
        stat_in[0:1] = jnp.full(far_m.shape, very_low, jnp.float32)
        stat_in[1:2] = jnp.zeros(far_l.shape, jnp.float32)

    own_steps(1, 8)

    @pl.when(half == 1)
    def _():
        o_over.wait_recv()
        stat_over.wait_recv()

    other_m, other_l = stat_in[0:1], stat_in[1:2]
    top = jnp.maximum(m_ref[...], other_m)
    mine = jnp.exp2((m_ref[...] - top) * POWER)
    other = other_l * jnp.exp2((other_m - top) * POWER)
    total = l_ref[...] * mine + other
    mine, other = mine / total, other / total
    back = []
    for h in range(TP):
        cols = slice(h * rows, (h + 1) * rows)
        mixed = acc_ref[:, cols] * mine[:, cols] + o_in[:, cols].astype(jnp.float32) * other[:, cols]
        o_rows[h] = mixed.T.astype(jnp.bfloat16)
    for off in range(1, TP):
        peer = lax.rem(t + off, TP)
        cp = remote(37 + off, o_rows.at[peer], att.at[:, lanes(t)], (s, peer))
        cp.start()
        back.append(cp)
    own_back = pltpu.make_async_copy(o_rows.at[t], att.at[:, lanes(t)], local_sem.at[3])
    own_back.start()
    own_back.wait()
    for cp in back:
        cp.wait_recv()
    att_ref[...] = att[...]

    for cp in q_copies + k_copies + v_copies + gather + passed + back:
        cp.wait_send()

    @pl.when(half == 1)
    def _():
        q_over.wait_send()

    @pl.when(half == 0)
    def _():
        o_over.wait_send()
        stat_over.wait_send()


def attention_of(queries, keys, values):
    rows, width = queries.shape
    group = rows * TP
    f32, bf16 = jnp.float32, jnp.bfloat16
    vmem = pl.BlockSpec(memory_space=pltpu.VMEM)
    return pl.pallas_call(
        attend_kernel,
        out_shape=jax.ShapeDtypeStruct((rows, width), bf16),
        in_specs=[vmem] * 3,
        out_specs=vmem,
        scratch_shapes=[
            pltpu.VMEM((TP, HEAD, rows), bf16),
            pltpu.VMEM((group, HEAD), bf16),
            pltpu.VMEM((group, HEAD), bf16),
            pltpu.VMEM((8, group, HEAD), bf16),
            pltpu.VMEM((8, HEAD, group), bf16),
            pltpu.VMEM((1, group), f32),
            pltpu.VMEM((1, group), f32),
            pltpu.VMEM((HEAD, group), f32),
            pltpu.VMEM((1, group), f32),
            pltpu.VMEM((1, group), f32),
            pltpu.VMEM((HEAD, group), f32),
            pltpu.VMEM((HEAD, group), bf16),
            pltpu.VMEM((HEAD, group), bf16),
            pltpu.VMEM((8, group), f32),
            pltpu.VMEM((8, group), f32),
            pltpu.VMEM((TP, rows, HEAD), bf16),
            pltpu.VMEM((rows, width), bf16),
            pltpu.SemaphoreType.DMA((45,)),
            pltpu.SemaphoreType.DMA((45,)),
            pltpu.SemaphoreType.DMA((4,)),
        ],
        compiler_params=pltpu.CompilerParams(
            collective_id=0, has_side_effects=True, vmem_limit_bytes=48 * 1024 * 1024
        ),
        name="attention",
    )(queries, keys, values)


def section_kernel(
    att_ref, fine_ref, cot_ref, gain_ref, out_hbm, gate_hbm, up_hbm, down_hbm,
    section_ref, stream_grad_ref, gate_grad_ref, up_grad_ref, down_grad_ref, gain_grad_ref,
    out_w, gate_w, up_w, down_w, stream, border, coarse_b, coarse_grad_b, ng, gg, hidden_grad,
    ng_t, gg_t, ng_all, gg_all, hgu, down_out, down_in, norm_out, norm_in, follow_out, follow_in,
    gain_out, gain_in, gain_mid, gain_half, gain_far_out, gain_far_in, term_out, term_in,
    send, recv, local_sem,
):
    s, t, half, block, y, core, sib, up, down, partner = places()
    f32, bf16 = jnp.float32, jnp.bfloat16
    tok = fine_ref.shape[0]
    crows = tok // SHORTEN
    group = crows * TP
    hid = gate_w.shape[1]
    number = lax.axis_size("seq") * TP
    flat = s * TP + t
    after, before = lax.rem(flat + 1, number), lax.rem(flat + number - 1, number)
    after, before = (after // TP, lax.rem(after, TP)), (before // TP, lax.rem(before, TP))

    weights = [
        pltpu.make_async_copy(src, dst, local_sem.at[i])
        for i, (src, dst) in enumerate(
            ((out_hbm, out_w), (down_hbm, down_w), (gate_hbm, gate_w), (up_hbm, up_w))
        )
    ]
    for cp in weights:
        cp.start()

    barrier = pltpu.get_barrier_semaphore()
    peers = [(s, lax.rem(t + off, TP)) for off in range(1, TP)]
    peers += [(half * 8 + lax.rem(block + off, 8), t) for off in range(1, 8)]
    peers += [(partner, t), after, before]
    for peer in peers:
        pl.semaphore_signal(barrier, inc=1, device_id=peer, device_id_type=MESH)
    pl.semaphore_wait(barrier, len(peers))

    used = []

    def remote(src, dst, device):
        kind = len(used)
        cp = pltpu.make_async_remote_copy(
            src_ref=src, dst_ref=dst, send_sem=send.at[kind], recv_sem=recv.at[kind],
            device_id=device, device_id_type=MESH,
        )
        used.append(cp)
        return cp

    def go(copies):
        for cp in copies:
            cp.start()
        return copies

    def landed(copies):
        for cp in copies:
            cp.wait_recv()

    def to_group(src, dst):
        return go([
            remote(src(lax.rem(t + off, TP)), dst, (s, lax.rem(t + off, TP))) for off in range(1, TP)
        ])

    def aligned(index, size):
        return pl.ds(pl.multiple_of(index * size, size), size)

    mine = aligned(t, crows)

    row = lax.broadcasted_iota(jnp.int32, (crows, tok), 0)
    col = lax.broadcasted_iota(jnp.int32, (crows, tok), 1)
    members = jnp.where((col >= row * SHORTEN) & (col < row * SHORTEN + SHORTEN), 1.0, 0.0).astype(bf16)
    coarse_grad = jnp.dot(members, cot_ref[...], preferred_element_type=f32)
    coarse_grad_b[...] = coarse_grad.astype(bf16)
    gg[mine, :] = coarse_grad_b[...]
    grad_gather = to_group(lambda peer: coarse_grad_b, gg.at[mine, :])

    weights[0].wait()
    projected = jnp.dot(att_ref[...], out_w[...], preferred_element_type=f32)
    stream[...] = (fine_ref[...].astype(f32) + projected).astype(bf16)
    border_copy = remote(stream.at[pl.ds(tok - 16, 16), :], border, after)
    border_copy.start()
    window = jnp.where((col >= row * SHORTEN - (SHORTEN - 1)) & (col <= row * SHORTEN), 1.0, 0.0)
    coarse = jnp.dot(window.astype(bf16), stream[...], preferred_element_type=f32)
    edge_row = lax.broadcasted_iota(jnp.int32, (crows, 16), 0)
    edge_col = lax.broadcasted_iota(jnp.int32, (crows, 16), 1)
    edge = jnp.where((edge_row == 0) & (edge_col > 16 - SHORTEN) & (flat > 0), 1.0, 0.0)
    border_copy.wait_recv()
    coarse = coarse + jnp.dot(edge.astype(bf16), border[...], preferred_element_type=f32)
    coarse = coarse / SHORTEN
    rstd = lax.rsqrt(jnp.mean(coarse * coarse, axis=-1, keepdims=True) + 1e-05)
    base = coarse * rstd
    coarse_b[...] = (base * gain_ref[...]).astype(bf16)
    ng[mine, :] = coarse_b[...]
    norm_gather = to_group(lambda peer: coarse_b, ng.at[mine, :])

    landed(grad_gather)
    weights[1].wait()
    hidden_grad[...] = lax.dot_general(
        gg[...], down_w[...], contract_last, preferred_element_type=f32
    )

    def to_columns(rows_ref, turned, gathered, sem):
        for i in range(turned.shape[0]):
            turned[i] = rows_ref[:, i * HEAD : (i + 1) * HEAD].astype(f32).T.astype(bf16)
        copies = []
        for part in range(2):
            dst = gathered.at[part, :, aligned(block, group)]
            for off in range(1, 8):
                peer = lax.rem(block + off, 8)
                copies.append(remote(turned.at[part * 8 + peer], dst, (half * 8 + peer, t)))
            kept = pltpu.make_async_copy(turned.at[part * 8 + block], dst, local_sem.at[sem + part])
            kept.start()
            kept.wait()
        return go(copies)

    grad_columns = to_columns(gg, gg_t, gg_all, 4)

    landed(norm_gather)
    weights[2].wait()
    weights[3].wait()
    gate = jnp.dot(ng[...], gate_w[...], preferred_element_type=f32)
    up_v = jnp.dot(ng[...], up_w[...], preferred_element_type=f32)
    sig = jax.nn.sigmoid(gate)
    act = gate * sig
    hgu[block, 0:group] = (act * up_v).astype(bf16)
    hgu[block, group : 2 * group] = (
        hidden_grad[...] * up_v * sig * (1.0 + gate * (1.0 - sig))
    ).astype(bf16)
    hgu[block, 2 * group : 3 * group] = (hidden_grad[...] * act).astype(bf16)

    cut = 3 * group // 2
    pieces = (pl.ds(0, cut), pl.ds(cut, cut))
    above, below, across = (lax.rem(y + dy, 4) * 2 + core for dy in (1, 3, 2))

    def ring(source, piece, device):
        ref = hgu.at[source, pieces[piece], :]
        return remote(ref, ref, (device, t))

    ring_up = go([ring(block, 0, up), ring(block, 1, up)])
    ring_down = go([ring(block, 1, down), ring(block, 0, down)])
    ring_sib = go([ring(block, 0, sib), ring(block, 1, sib)])

    part = jnp.dot(hgu[block, 0:group], down_w[...], preferred_element_type=f32)
    down_out[...] = part.astype(bf16).reshape(down_out.shape)
    down_in[t] = down_out[t]
    down_sum = to_group(lambda peer: down_out.at[peer], down_in.at[t])
    part = lax.dot_general(
        hgu[block, group : 2 * group], gate_w[...], contract_last, preferred_element_type=f32
    ) + lax.dot_general(
        hgu[block, 2 * group : 3 * group], up_w[...], contract_last, preferred_element_type=f32
    )
    norm_out[...] = part.astype(bf16).reshape(norm_out.shape)
    norm_in[t] = norm_out[t]
    norm_sum = to_group(lambda peer: norm_out.at[peer], norm_in.at[t])
    norm_columns = to_columns(ng, ng_t, ng_all, 6)

    landed(ring_up[:1])
    onward = go([ring(below, 0, up), ring(below, 0, sib)])
    landed(ring_down[:1])
    onward += go([ring(above, 1, down), ring(above, 1, sib)])
    landed(ring_up[1:])
    onward += go([ring(below, 1, sib)])
    landed(ring_down[1:])
    onward += go([ring(above, 0, sib)])

    landed(down_sum)
    coarse_out = coarse + jnp.sum(down_in[...].astype(f32), axis=0)
    spread = (crows, SHORTEN, D)
    section_ref[...] = (
        (stream[...].astype(f32).reshape(spread) + coarse_out[:, None, :])
        .reshape(tok, D)
        .astype(bf16)
    )

    landed(norm_sum)
    normed_grad = jnp.sum(norm_in[...].astype(f32), axis=0)
    width = D // 8

    def fold_row(ref, value):
        for i in range(8):
            ref[i : i + 1, :] = value[:, i * width : (i + 1) * width]

    scaled = normed_grad * gain_ref[...]
    coarse_total = coarse_grad + rstd * (
        scaled - base * jnp.mean(scaled * base, axis=-1, keepdims=True)
    )
    fold_row(follow_out, coarse_total[0:1])
    follow = remote(follow_out, follow_in, before)
    follow.start()
    fold_row(gain_out, jnp.sum(normed_grad * base, axis=0, keepdims=True))
    gain_in[t] = gain_out[...]
    gain_sum = to_group(lambda peer: gain_out, gain_in.at[t])

    landed(onward[0:1] + onward[2:3])
    last = go([ring(across, 0, sib), ring(across, 1, sib)])

    follow.wait_recv()
    following = jnp.concatenate([follow_in[i : i + 1, :] for i in range(8)], axis=1)
    following = jnp.where(flat < number - 1, following, 0.0)
    ahead = jnp.concatenate([coarse_total[1:], following], axis=0)
    place = lax.broadcasted_iota(jnp.int32, spread, 1)
    contrib = jnp.where(place == 0, coarse_total[:, None, :], ahead[:, None, :])
    stream_grad_ref[...] = (
        (cot_ref[...].astype(f32).reshape(spread) + contrib / SHORTEN).reshape(tok, D).astype(bf16)
    )

    landed(gain_sum)
    gain_mid[...] = jnp.sum(gain_in[...], axis=0)
    gain_half[block] = gain_mid[...]
    gain_group = go([
        remote(gain_mid, gain_half.at[block], (half * 8 + lax.rem(block + off, 8), t))
        for off in range(1, 8)
    ])

    landed(ring_sib + onward[1:2] + onward[3:] + grad_columns + norm_columns + last)
    outs = (down_grad_ref, gate_grad_ref, up_grad_ref)

    def term(i, part):
        left = (gg_all if i == 0 else ng_all)[part]
        right = hgu[:, i * group : (i + 1) * group, :].reshape(8 * group, hid)
        return jnp.dot(left, right, preferred_element_type=f32)

    terms = []
    for i in range(3):
        term_out[i] = term(i, 1 - half).astype(bf16)
        terms += go([remote(term_out.at[i], term_in.at[i], (partner, t))])
    landed(gain_group)
    gain_far_out[...] = jnp.sum(gain_half[...], axis=0)
    gain_far = remote(gain_far_out, gain_far_in, (partner, t))
    gain_far.start()
    for i in range(3):
        outs[i][...] = term(i, half)
    gain_far.wait_recv()
    gain_grad_ref[...] = gain_far_out[...] + gain_far_in[...]
    for i in range(3):
        terms[i].wait_recv()
        outs[i][...] = outs[i][...] + term_in[i].astype(f32)

    for cp in used:
        cp.wait_send()


COPIES = 90


def section_of(attention, fine_stream, cotangent, norm_gain, out_weight, gate_weight, up_weight, down_weight):
    tok = fine_stream.shape[0]
    crows = tok // SHORTEN
    group = crows * TP
    hid = gate_weight.shape[1]
    seq = lax.axis_size("seq")
    f32, bf16 = jnp.float32, jnp.bfloat16
    vmem, anywhere = pl.BlockSpec(memory_space=pltpu.VMEM), pl.BlockSpec(memory_space=pl.ANY)
    small = (8, D // 8)
    return pl.pallas_call(
        section_kernel,
        out_shape=(
            jax.ShapeDtypeStruct((tok, D), bf16),
            jax.ShapeDtypeStruct((tok, D), bf16),
            jax.ShapeDtypeStruct((D // seq, hid), f32),
            jax.ShapeDtypeStruct((D // seq, hid), f32),
            jax.ShapeDtypeStruct((D // seq, hid), f32),
            jax.ShapeDtypeStruct(small, f32),
        ),
        in_specs=[vmem] * 4 + [anywhere] * 4,
        out_specs=(vmem,) * 6,
        scratch_shapes=[
            pltpu.VMEM(out_weight.shape, bf16),
            pltpu.VMEM(gate_weight.shape, bf16),
            pltpu.VMEM(up_weight.shape, bf16),
            pltpu.VMEM(down_weight.shape, bf16),
            pltpu.VMEM((tok, D), bf16),
            pltpu.VMEM((16, D), bf16),
            pltpu.VMEM((crows, D), bf16),
            pltpu.VMEM((crows, D), bf16),
            pltpu.VMEM((group, D), bf16),
            pltpu.VMEM((group, D), bf16),
            pltpu.VMEM((group, hid), f32),
            pltpu.VMEM((seq, HEAD, group), bf16),
            pltpu.VMEM((seq, HEAD, group), bf16),
            pltpu.VMEM((2, HEAD, 8 * group), bf16),
            pltpu.VMEM((2, HEAD, 8 * group), bf16),
            pltpu.VMEM((8, 3 * group, hid), bf16),
            pltpu.VMEM((TP, crows, D), bf16),
            pltpu.VMEM((TP, crows, D), bf16),
            pltpu.VMEM((TP, crows, D), bf16),
            pltpu.VMEM((TP, crows, D), bf16),
            pltpu.VMEM(small, f32),
            pltpu.VMEM(small, f32),
            pltpu.VMEM(small, f32),
            pltpu.VMEM((TP,) + small, f32),
            pltpu.VMEM(small, f32),
            pltpu.VMEM((8,) + small, f32),
            pltpu.VMEM(small, f32),
            pltpu.VMEM(small, f32),
            pltpu.VMEM((3, HEAD, hid), bf16),
            pltpu.VMEM((3, HEAD, hid), bf16),
            pltpu.SemaphoreType.DMA((COPIES,)),
            pltpu.SemaphoreType.DMA((COPIES,)),
            pltpu.SemaphoreType.DMA((8,)),
        ],
        compiler_params=pltpu.CompilerParams(
            collective_id=1, has_side_effects=True, vmem_limit_bytes=56 * 1024 * 1024
        ),
        name="section",
    )(
        attention, fine_stream, cotangent, norm_gain.reshape(1, D),
        out_weight, gate_weight, up_weight, down_weight,
    )


def on_device(
    fine_stream,
    queries,
    keys,
    values,
    out_weight,
    norm_gain,
    gate_weight,
    up_weight,
    down_weight,
    cotangent,
):
    attention = attention_of(queries, keys, values)
    section_out, stream_grad, gate_grad, up_grad, down_grad, gain_grad = section_of(
        attention, fine_stream, cotangent, norm_gain, out_weight, gate_weight, up_weight, down_weight
    )
    return (section_out, stream_grad, gate_grad, up_grad, down_grad.T, gain_grad.reshape(D))


def solution(mesh):
    return jax.shard_map(
        on_device,
        mesh=mesh,
        in_specs=(
            P(("seq", "tp"), None),
            P(("seq", "tp"), None),
            P(("seq", "tp"), None),
            P(("seq", "tp"), None),
            P(),
            P(),
            P(None, "tp"),
            P(None, "tp"),
            P("tp", None),
            P(("seq", "tp"), None),
        ),
        out_specs=(
            P(("seq", "tp"), None),
            P(("seq", "tp"), None),
            P("seq", "tp"),
            P("seq", "tp"),
            P("tp", "seq"),
            P(),
        ),
        check_vma=False,
    )
```

```python
import math

import jax
import jax.numpy as jnp
from jax import lax
from jax.experimental import pallas as pl
from jax.experimental.pallas import tpu as pltpu
from jax.sharding import PartitionSpec as P

D = 2048
HEAD = 128
SHORTEN = 8
MESH = pl.DeviceIdType.MESH
TP = 8
WIDE = 512
COPIES = 160

contract_last = (((1,), (1,)), ((), ()))
contract_first = (((0,), (0,)), ((), ()))
very_low = -1e30
POWER = math.log2(math.e) * HEAD ** (-0.5)


def scratch_of(tok, hid, seq):
    crows, group, rows = tok // SHORTEN, tok // SHORTEN * TP, tok * TP
    f32, bf16 = jnp.float32, jnp.bfloat16
    vmem = pltpu.VMEM
    small = (8, D // 8)
    return {
        "q_in": vmem((tok, TP * HEAD), bf16),
        "k_in": vmem((tok, TP * HEAD), bf16),
        "v_in": vmem((tok, TP * HEAD), bf16),
        "fine": vmem((tok, D), bf16),
        "cot": vmem((tok, D), bf16),
        "out_w": vmem((TP * HEAD, D), bf16),
        "gate_w": vmem((hid, D), bf16),
        "up_w": vmem((hid, D), bf16),
        "down_w": vmem((hid, D), bf16),
        "vt_src": vmem((TP, HEAD, tok), bf16),
        "q_own": vmem((rows, HEAD), bf16),
        "q_far": vmem((rows, HEAD), bf16),
        "k_all": vmem((8, rows, HEAD), bf16),
        "vt_all": vmem((8, HEAD, rows), bf16),
        "scores": vmem((2, WIDE, WIDE), f32),
        "tops": vmem((2, 1, WIDE), f32),
        "m_own": vmem((1, rows), f32),
        "l_own": vmem((1, rows), f32),
        "acc_own": vmem((HEAD, rows), f32),
        "m_far": vmem((1, rows), f32),
        "l_far": vmem((1, rows), f32),
        "acc_far": vmem((HEAD, rows), f32),
        "o_out": vmem((HEAD, rows), bf16),
        "o_in": vmem((HEAD, rows), bf16),
        "stat_out": vmem((8, rows), f32),
        "stat_in": vmem((8, rows), f32),
        "o_rows": vmem((TP, tok, HEAD), bf16),
        "att": vmem((tok, TP * HEAD), bf16),
        "stream": vmem((tok, D), bf16),
        "border": vmem((16, D), bf16),
        "coarse_b": vmem((crows, D), bf16),
        "coarse_grad": vmem((crows, D), f32),
        "coarse_grad_b": vmem((crows, D), bf16),
        "ng": vmem((group, D), bf16),
        "gg": vmem((group, D), bf16),
        "hidden_grad": vmem((group, hid), f32),
        "ng_all": vmem((2, 8 * group, HEAD), bf16),
        "gg_all": vmem((2, 8 * group, HEAD), bf16),
        "hgu": vmem((3, 8, group, hid), bf16),
        "down_out": vmem((TP, crows, D), bf16),
        "down_in": vmem((TP, crows, D), bf16),
        "norm_out": vmem((TP, crows, D), bf16),
        "norm_in": vmem((TP, crows, D), bf16),
        "follow_out": vmem(small, f32),
        "follow_in": vmem(small, f32),
        "gain_out": vmem(small, f32),
        "gain_in": vmem((TP,) + small, f32),
        "gain_mid": vmem(small, f32),
        "gain_half": vmem((8,) + small, f32),
        "gain_far_out": vmem(small, f32),
        "gain_far_in": vmem(small, f32),
        "term_out": vmem((3, hid, HEAD), bf16),
        "term_in": vmem((3, hid, HEAD), bf16),
        "send": pltpu.SemaphoreType.DMA((COPIES,)),
        "recv": pltpu.SemaphoreType.DMA((COPIES,)),
        "local": pltpu.SemaphoreType.DMA((20,)),
    }


class Space:
    pass


def section_kernel(
    names, q_hbm, k_hbm, v_hbm, fine_hbm, cot_hbm, gain_ref, out_hbm, gate_hbm, up_hbm, down_hbm,
    section_ref, stream_grad_ref, gate_grad_ref, up_grad_ref, down_grad_ref, gain_grad_ref, *scratch,
):
    r = Space()
    for name, ref in zip(names, scratch):
        setattr(r, name, ref)
    f32, bf16 = jnp.float32, jnp.bfloat16
    s, t = lax.axis_index("seq"), lax.axis_index("tp")
    half, block = s // 8, lax.rem(s, 8)
    y, core = block // 2, lax.rem(block, 2)
    sib = half * 8 + y * 2 + (1 - core)
    up = half * 8 + lax.rem(y + 1, 4) * 2 + core
    down = half * 8 + lax.rem(y + 3, 4) * 2 + core
    partner = (1 - half) * 8 + block
    number = lax.axis_size("seq") * TP
    flat = s * TP + t
    after, before = lax.rem(flat + 1, number), lax.rem(flat + number - 1, number)
    after, before = (after // TP, lax.rem(after, TP)), (before // TP, lax.rem(before, TP))
    tok = r.fine.shape[0]
    crows = tok // SHORTEN
    group = crows * TP
    hid = r.gate_w.shape[0]

    loads = {}
    for name, src in (
        ("k_in", k_hbm), ("v_in", v_hbm), ("q_in", q_hbm), ("cot", cot_hbm), ("fine", fine_hbm),
        ("out_w", out_hbm), ("down_w", down_hbm), ("gate_w", gate_hbm), ("up_w", up_hbm),
    ):
        loads[name] = pltpu.make_async_copy(src, getattr(r, name), r.local.at[len(loads)])
        loads[name].start()

    barrier = pltpu.get_barrier_semaphore()
    peers = [(s, lax.rem(t + off, TP)) for off in range(1, TP)]
    peers += [(half * 8 + lax.rem(block + off, 8), t) for off in range(1, 8)]
    peers += [(partner, t), after, before]
    for peer in peers:
        pl.semaphore_signal(barrier, inc=1, device_id=peer, device_id_type=MESH)
    for ref, value in ((r.m_own, very_low), (r.l_own, 0.0), (r.acc_own, 0.0),
                       (r.m_far, very_low), (r.l_far, 0.0), (r.acc_far, 0.0)):
        ref[...] = jnp.full(ref.shape, value, f32)
    loads["v_in"].wait()
    for h in range(TP):
        r.vt_src[h] = r.v_in[:, h * HEAD : (h + 1) * HEAD].astype(f32).T.astype(bf16)
    loads["k_in"].wait()
    loads["q_in"].wait()
    pl.semaphore_wait(barrier, len(peers))

    used, sometimes = [], []

    def remote(src, dst, device, always=True):
        kind = len(used) + len(sometimes)
        cp = pltpu.make_async_remote_copy(
            src_ref=src, dst_ref=dst, send_sem=r.send.at[kind], recv_sem=r.recv.at[kind],
            device_id=device, device_id_type=MESH,
        )
        (used if always else sometimes).append(cp)
        return cp

    def go(copies):
        for cp in copies:
            cp.start()
        return copies

    def landed(copies):
        for cp in copies:
            cp.wait_recv()

    def to_group(src, dst):
        return go([
            remote(src(lax.rem(t + off, TP)), dst, (s, lax.rem(t + off, TP))) for off in range(1, TP)
        ])

    def aligned(index, size):
        return pl.ds(pl.multiple_of(index * size, size), size)

    def lanes(index):
        return aligned(index, HEAD)

    band = aligned(t, tok)
    k_copies = to_group(lambda peer: r.k_in.at[:, lanes(peer)], r.k_all.at[block, band, :])
    v_copies = to_group(lambda peer: r.vt_src.at[peer], r.vt_all.at[block, :, band])
    q_copies = to_group(lambda peer: r.q_in.at[:, lanes(peer)], r.q_own.at[band, :])
    own = go([
        pltpu.make_async_copy(r.q_in.at[:, lanes(t)], r.q_own.at[band, :], r.local.at[9]),
        pltpu.make_async_copy(r.k_in.at[:, lanes(t)], r.k_all.at[block, band, :], r.local.at[10]),
        pltpu.make_async_copy(r.vt_src.at[t], r.vt_all.at[block, :, band], r.local.at[11]),
    ])

    mine = aligned(t, crows)
    row = lax.broadcasted_iota(jnp.int32, (crows, tok), 0)
    col = lax.broadcasted_iota(jnp.int32, (crows, tok), 1)
    members = jnp.where((col >= row * SHORTEN) & (col < row * SHORTEN + SHORTEN), 1.0, 0.0).astype(bf16)
    loads["cot"].wait()
    r.coarse_grad[...] = jnp.dot(members, r.cot[...], preferred_element_type=f32)
    r.coarse_grad_b[...] = r.coarse_grad[...].astype(bf16)
    r.gg[mine, :] = r.coarse_grad_b[...]

    for cp in own:
        cp.wait()
    k_mine, v_mine = r.k_all.at[block], r.vt_all.at[block]
    landed(k_copies)
    k_ring = go([remote(k_mine, k_mine, (device, t)) for device in (up, down, sib)])
    landed(v_copies)
    v_ring = go([remote(v_mine, v_mine, (device, t)) for device in (down, up, sib)])
    landed(q_copies)
    q_over = remote(r.q_own, r.q_far, (partner, t), always=False)

    @pl.when(half == 1)
    def _():
        q_over.start()

    grad_gather = to_group(lambda peer: r.coarse_grad_b, r.gg.at[mine, :])

    def block_of(step):
        j = step // 2
        dy = j + (j // 2) * (5 - 2 * j)
        return lax.rem(y + dy, 4) * 2 + lax.rem(core + step, 2)

    def score(q_all, key_block, piece, slot):
        kk, u = piece
        st = lax.dot_general(
            r.k_all[key_block, kk * WIDE : (kk + 1) * WIDE], q_all[u * WIDE : (u + 1) * WIDE],
            contract_last, preferred_element_type=f32,
        )
        if slot is None:
            return st
        r.scores[slot] = st
        r.tops[slot] = jnp.max(st, axis=0, keepdims=True)

    def absorb(state, st, top, key_block, piece):
        m_all, l_all, acc_all = state
        kk, u = piece
        cols = slice(u * WIDE, (u + 1) * WIDE)
        older = m_all[:, cols]
        fresh = jnp.maximum(older, top)
        weights = jnp.exp2((st - fresh) * POWER)
        factor = jnp.exp2((older - fresh) * POWER)
        m_all[:, cols] = fresh
        l_all[:, cols] = l_all[:, cols] * factor + jnp.sum(weights, axis=0, keepdims=True)
        acc_all[:, cols] = acc_all[:, cols] * factor + jnp.dot(
            r.vt_all[key_block, :, kk * WIDE : (kk + 1) * WIDE], weights.astype(bf16),
            preferred_element_type=f32,
        )

    pieces = [(kk, u) for kk in range(2) for u in range(2)]

    def sweep(q_all, state, first, last, index):
        score(q_all, index(first), pieces[0], 0)

        @pl.loop(first, last)
        def _(step):
            here, then = index(step), index(jnp.minimum(step + 1, last - 1))
            for i, piece in enumerate(pieces):
                if i + 1 < len(pieces):
                    score(q_all, here, pieces[i + 1], (i + 1) % 2)
                else:
                    score(q_all, then, pieces[0], (i + 1) % 2)
                absorb(state, r.scores[i % 2], r.tops[i % 2], here, piece)

    own_state = (r.m_own, r.l_own, r.acc_own)
    far_state = (r.m_far, r.l_far, r.acc_far)

    def arrived(first, last):
        @pl.when(half == 0)
        def _():
            sweep(r.q_far, far_state, first, last, block_of)

        @pl.when(half == 1)
        def _():
            @pl.loop(max(first, 1), last)
            def _(step):
                @pl.when(block_of(step) < block)
                def _():
                    sweep(r.q_own, own_state, step, step + 1, block_of)

    for piece in ((0, 0), (0, 1), (1, 1)):
        st = score(r.q_own, block, piece, None)
        if piece[0] == piece[1]:
            key_pos = lax.broadcasted_iota(jnp.int32, st.shape, 0)
            query_pos = lax.broadcasted_iota(jnp.int32, st.shape, 1)
            st = jnp.where(key_pos <= query_pos, st, very_low)
        absorb(own_state, st, jnp.max(st, axis=0, keepdims=True), block, piece)

    def to_columns(rows_ref, gathered, sem):
        copies = []
        for part in range(2):
            dst = gathered.at[part, aligned(block, group), :]
            for off in range(1, 8):
                peer = lax.rem(block + off, 8)
                copies.append(remote(rows_ref.at[:, lanes(part * 8 + peer)], dst, (half * 8 + peer, t)))
            kept = pltpu.make_async_copy(
                rows_ref.at[:, lanes(part * 8 + block)], dst, r.local.at[sem + part]
            )
            kept.start()
            kept.wait()
        return go(copies)

    landed([k_ring[2], v_ring[2]])

    @pl.when(half == 0)
    def _():
        q_over.wait_recv()

    arrived(0, 2)
    k_below, v_below = r.k_all.at[block_of(4)], r.vt_all.at[block_of(4)]
    k_above, v_above = r.k_all.at[block_of(2)], r.vt_all.at[block_of(2)]
    k_across, v_across = r.k_all.at[block_of(6)], r.vt_all.at[block_of(6)]
    landed(k_ring[:1])
    k_on = go([remote(k_below, k_below, (up, t)), remote(k_below, k_below, (sib, t))])
    landed(v_ring[:1])
    v_on = go([remote(v_above, v_above, (down, t)), remote(v_above, v_above, (sib, t))])
    landed(k_ring[1:2])
    k_on += go([remote(k_above, k_above, (sib, t))])
    landed(v_ring[1:2])
    v_on += go([remote(v_below, v_below, (sib, t))])
    arrived(2, 3)
    landed([k_on[2], v_on[1]])
    arrived(3, 4)
    landed([k_on[1], v_on[2]])
    landed(grad_gather)
    grad_columns = to_columns(r.gg, r.gg_all, 12)
    landed(k_on[:1])
    k_last = go([remote(k_across, k_across, (sib, t))])
    landed(v_on[:1])
    v_last = go([remote(v_across, v_across, (sib, t))])
    arrived(4, 7)
    landed(k_last + v_last)
    arrived(7, 8)

    o_over = remote(r.o_out, r.o_in, (partner, t), always=False)
    stat_over = remote(r.stat_out, r.stat_in, (partner, t), always=False)

    @pl.when(half == 0)
    def _():
        r.o_out[...] = (r.acc_far[...] / r.l_far[...]).astype(bf16)
        r.stat_out[0:1] = r.m_far[...]
        r.stat_out[1:2] = r.l_far[...]
        o_over.start()
        stat_over.start()
        r.o_in[...] = jnp.zeros(r.o_in.shape, bf16)
        r.stat_in[0:1] = jnp.full(r.m_far.shape, very_low, f32)
        r.stat_in[1:2] = jnp.zeros(r.l_far.shape, f32)
        sweep(r.q_own, own_state, 0, block, lambda step: step)

    @pl.when(half == 1)
    def _():
        o_over.wait_recv()
        stat_over.wait_recv()

    other_m, other_l = r.stat_in[0:1], r.stat_in[1:2]
    top = jnp.maximum(r.m_own[...], other_m)
    share = jnp.exp2((r.m_own[...] - top) * POWER)
    other = other_l * jnp.exp2((other_m - top) * POWER)
    total = r.l_own[...] * share + other
    share, other = share / total, other / total
    for h in range(TP):
        cols = slice(h * tok, (h + 1) * tok)
        mixed = r.acc_own[:, cols] * share[:, cols] + r.o_in[:, cols].astype(f32) * other[:, cols]
        r.o_rows[h] = mixed.T.astype(bf16)
    back = to_group(lambda peer: r.o_rows.at[peer], r.att.at[:, lanes(t)])
    own_back = pltpu.make_async_copy(r.o_rows.at[t], r.att.at[:, lanes(t)], r.local.at[14])
    own_back.start()
    own_back.wait()
    loads["out_w"].wait()
    loads["fine"].wait()
    landed(back)

    projected = jnp.dot(r.att[...], r.out_w[...], preferred_element_type=f32)
    r.stream[...] = (r.fine[...].astype(f32) + projected).astype(bf16)
    border_copy = remote(r.stream.at[pl.ds(tok - 16, 16), :], r.border, after)
    border_copy.start()
    window = jnp.where((col >= row * SHORTEN - (SHORTEN - 1)) & (col <= row * SHORTEN), 1.0, 0.0)
    coarse = jnp.dot(window.astype(bf16), r.stream[...], preferred_element_type=f32)
    edge_row = lax.broadcasted_iota(jnp.int32, (crows, 16), 0)
    edge_col = lax.broadcasted_iota(jnp.int32, (crows, 16), 1)
    edge = jnp.where((edge_row == 0) & (edge_col > 16 - SHORTEN) & (flat > 0), 1.0, 0.0)
    border_copy.wait_recv()
    coarse = coarse + jnp.dot(edge.astype(bf16), r.border[...], preferred_element_type=f32)
    coarse = coarse / SHORTEN
    rstd = lax.rsqrt(jnp.mean(coarse * coarse, axis=-1, keepdims=True) + 1e-05)
    base = coarse * rstd
    r.coarse_b[...] = (base * gain_ref[...]).astype(bf16)
    r.ng[mine, :] = r.coarse_b[...]
    norm_gather = to_group(lambda peer: r.coarse_b, r.ng.at[mine, :])

    loads["down_w"].wait()
    r.hidden_grad[...] = lax.dot_general(
        r.gg[...], r.down_w[...], contract_last, preferred_element_type=f32
    )
    loads["gate_w"].wait()
    loads["up_w"].wait()

    landed(norm_gather)
    gate = lax.dot_general(r.ng[...], r.gate_w[...], contract_last, preferred_element_type=f32)
    up_v = lax.dot_general(r.ng[...], r.up_w[...], contract_last, preferred_element_type=f32)
    sig = jax.nn.sigmoid(gate)
    act = gate * sig
    above, below, across = (lax.rem(y + dy, 4) * 2 + core for dy in (1, 3, 2))
    cut = group // 2
    parts = (pl.ds(0, cut), pl.ds(cut, cut), pl.ds(0, group))

    def ring(i, source, piece, device):
        ref = r.hgu.at[i, source, parts[piece], :]
        return remote(ref, ref, (device, t))

    def around(i):
        return (
            go([ring(i, block, 0, up), ring(i, block, 1, up)]),
            go([ring(i, block, 1, down), ring(i, block, 0, down)]),
            go([ring(i, block, 2, sib)]),
        )

    rings = []
    r.hgu[0, block] = (act * up_v).astype(bf16)
    rings.append(around(0))
    r.hgu[1, block] = (
        r.hidden_grad[...] * up_v * sig * (1.0 + gate * (1.0 - sig))
    ).astype(bf16)
    rings.append(around(1))
    r.hgu[2, block] = (r.hidden_grad[...] * act).astype(bf16)
    rings.append(around(2))

    part = jnp.dot(r.hgu[0, block], r.down_w[...], preferred_element_type=f32)
    r.down_out[...] = part.astype(bf16).reshape(r.down_out.shape)
    r.down_in[t] = r.down_out[t]
    down_sum = to_group(lambda peer: r.down_out.at[peer], r.down_in.at[t])
    part = jnp.dot(r.hgu[1, block], r.gate_w[...], preferred_element_type=f32) + jnp.dot(
        r.hgu[2, block], r.up_w[...], preferred_element_type=f32
    )
    r.norm_out[...] = part.astype(bf16).reshape(r.norm_out.shape)
    r.norm_in[t] = r.norm_out[t]
    norm_sum = to_group(lambda peer: r.norm_out.at[peer], r.norm_in.at[t])
    norm_columns = to_columns(r.ng, r.ng_all, 15)

    def pass_on(i):
        ring_up, ring_down, _ = rings[i]
        landed(ring_up[:1])
        first = go([ring(i, below, 0, up)])
        landed(ring_down[:1])
        first += go([ring(i, above, 1, down)])
        landed(ring_up[1:])
        rest = go([ring(i, below, 2, sib)])
        landed(ring_down[1:])
        rest += go([ring(i, above, 2, sib)])
        return first, rest

    def pass_last(i):
        landed(on[i][0])
        return go([ring(i, across, 2, sib)])

    on, last = [pass_on(0)], []

    landed(down_sum)
    coarse_out = coarse + jnp.sum(r.down_in[...].astype(f32), axis=0)
    spread = (crows, SHORTEN, D)
    section_ref[...] = (
        (r.stream[...].astype(f32).reshape(spread) + coarse_out[:, None, :])
        .reshape(tok, D)
        .astype(bf16)
    )
    on.append(pass_on(1))
    last.append(pass_last(0))

    landed(norm_sum)
    normed_grad = jnp.sum(r.norm_in[...].astype(f32), axis=0)
    width = D // 8

    def fold_row(ref, value):
        for i in range(8):
            ref[i : i + 1, :] = value[:, i * width : (i + 1) * width]

    def flat_row(ref):
        return jnp.concatenate([ref[i : i + 1, :] for i in range(8)], axis=1)

    scaled = normed_grad * gain_ref[...]
    coarse_total = r.coarse_grad[...] + rstd * (
        scaled - base * jnp.mean(scaled * base, axis=-1, keepdims=True)
    )
    fold_row(r.follow_out, coarse_total[0:1])
    follow = remote(r.follow_out, r.follow_in, before)
    follow.start()
    fold_row(r.gain_out, jnp.sum(normed_grad * base, axis=0, keepdims=True))
    r.gain_in[t] = r.gain_out[...]
    gain_sum = to_group(lambda peer: r.gain_out, r.gain_in.at[t])

    on.append(pass_on(2))
    last.append(pass_last(1))

    follow.wait_recv()
    following = jnp.where(flat < number - 1, flat_row(r.follow_in), 0.0)
    ahead = jnp.concatenate([coarse_total[1:], following], axis=0)
    place = lax.broadcasted_iota(jnp.int32, spread, 1)
    contrib = jnp.where(place == 0, coarse_total[:, None, :], ahead[:, None, :])
    stream_grad_ref[...] = (
        (r.cot[...].astype(f32).reshape(spread) + contrib / SHORTEN).reshape(tok, D).astype(bf16)
    )
    last.append(pass_last(2))

    landed(gain_sum)
    r.gain_mid[...] = jnp.sum(r.gain_in[...], axis=0)
    r.gain_half[block] = r.gain_mid[...]
    gain_group = go([
        remote(r.gain_mid, r.gain_half.at[block], (half * 8 + lax.rem(block + off, 8), t))
        for off in range(1, 8)
    ])

    landed(grad_columns + norm_columns)
    outs = (down_grad_ref, gate_grad_ref, up_grad_ref)

    def term(i, part):
        right = (r.gg_all if i == 0 else r.ng_all)[part]
        left = r.hgu[i].reshape(8 * group, hid)
        return lax.dot_general(left, right, contract_first, preferred_element_type=f32)

    terms = []
    for i in range(3):
        landed(rings[i][2] + on[i][1] + last[i])
        r.term_out[i] = term(i, 1 - half).astype(bf16)
        terms += go([remote(r.term_out.at[i], r.term_in.at[i], (partner, t))])
    landed(gain_group)
    r.gain_far_out[...] = jnp.sum(r.gain_half[...], axis=0)
    gain_far = remote(r.gain_far_out, r.gain_far_in, (partner, t))
    gain_far.start()
    for i in range(3):
        outs[i][...] = term(i, half)
    gain_far.wait_recv()
    gain_grad_ref[...] = flat_row(r.gain_far_out) + flat_row(r.gain_far_in)
    for i in range(3):
        terms[i].wait_recv()
        outs[i][...] = outs[i][...] + r.term_in[i].astype(f32)

    for cp in used:
        cp.wait_send()

    @pl.when(half == 1)
    def _():
        q_over.wait_send()

    @pl.when(half == 0)
    def _():
        o_over.wait_send()
        stat_over.wait_send()


def hand_over_kernel(*refs):
    count = len(refs) // 2
    copies = [
        pltpu.make_async_copy(src, dst, refs[-1].at[i])
        for i, (src, dst) in enumerate(zip(refs[:count], refs[count:-1]))
    ]
    for cp in copies:
        cp.start()
    for cp in copies:
        cp.wait()


def on_device(
    fine_stream,
    queries,
    keys,
    values,
    out_weight,
    norm_gain,
    gate_weight,
    up_weight,
    down_weight,
    cotangent,
):
    tok = fine_stream.shape[0]
    hid = gate_weight.shape[1]
    seq = lax.axis_size("seq")
    f32, bf16 = jnp.float32, jnp.bfloat16
    vmem, anywhere = pl.BlockSpec(memory_space=pltpu.VMEM), pl.BlockSpec(memory_space=pl.ANY)
    scratch = scratch_of(tok, hid, seq)
    shapes = (
        jax.ShapeDtypeStruct((tok, D), bf16),
        jax.ShapeDtypeStruct((tok, D), bf16),
        jax.ShapeDtypeStruct((hid, D // seq), f32),
        jax.ShapeDtypeStruct((hid, D // seq), f32),
        jax.ShapeDtypeStruct((hid, D // seq), f32),
        jax.ShapeDtypeStruct((1, D), f32),
    )
    outs = pl.pallas_call(
        lambda *refs: section_kernel(tuple(scratch), *refs),
        out_shape=shapes,
        in_specs=[anywhere] * 5 + [vmem] + [anywhere] * 4,
        out_specs=(vmem,) * 6,
        scratch_shapes=list(scratch.values()),
        compiler_params=pltpu.CompilerParams(
            collective_id=0, has_side_effects=True, vmem_limit_bytes=60 * 1024 * 1024
        ),
        name="section",
    )(
        queries, keys, values, fine_stream, cotangent, norm_gain.reshape(1, D),
        out_weight, gate_weight.T, up_weight.T, down_weight,
    )
    section_out, stream_grad, gate_grad, up_grad, down_grad, gain_grad = pl.pallas_call(
        hand_over_kernel,
        out_shape=shapes,
        in_specs=[anywhere] * 6,
        out_specs=(anywhere,) * 6,
        scratch_shapes=[pltpu.SemaphoreType.DMA((6,))],
        name="hand_over",
    )(*outs)
    return (section_out, stream_grad, gate_grad.T, up_grad.T, down_grad, gain_grad.reshape(D))


def solution(mesh):
    return jax.shard_map(
        on_device,
        mesh=mesh,
        in_specs=(
            P(("seq", "tp"), None),
            P(("seq", "tp"), None),
            P(("seq", "tp"), None),
            P(("seq", "tp"), None),
            P(),
            P(),
            P(None, "tp"),
            P(None, "tp"),
            P("tp", None),
            P(("seq", "tp"), None),
        ),
        out_specs=(
            P(("seq", "tp"), None),
            P(("seq", "tp"), None),
            P("seq", "tp"),
            P("seq", "tp"),
            P("tp", "seq"),
            P(),
        ),
        check_vma=False,
    )
```

```python
import math

import jax
import jax.numpy as jnp
from jax import lax
from jax.experimental import pallas as pl
from jax.experimental.pallas import tpu as pltpu
from jax.sharding import PartitionSpec as P

D = 2048
HEAD = 128
SHORTEN = 8
MESH = pl.DeviceIdType.MESH
TP = 8
WIDE = 512
COPIES = 160

contract_last = (((1,), (1,)), ((), ()))
contract_first = (((0,), (0,)), ((), ()))
very_low = -1e30
POWER = math.log2(math.e) * HEAD ** (-0.5)


def scratch_of(tok, hid, seq):
    crows, group, rows = tok // SHORTEN, tok // SHORTEN * TP, tok * TP
    f32, bf16 = jnp.float32, jnp.bfloat16
    vmem = pltpu.VMEM
    small = (8, D // 8)
    return {
        "q_in": vmem((tok, TP * HEAD), bf16),
        "k_in": vmem((tok, TP * HEAD), bf16),
        "v_in": vmem((tok, TP * HEAD), bf16),
        "fine": vmem((tok, D), bf16),
        "cot": vmem((tok, D), bf16),
        "out_w": vmem((TP * HEAD, D), bf16),
        "gate_w": vmem((hid, D), bf16),
        "up_w": vmem((hid, D), bf16),
        "down_w": vmem((hid, D), bf16),
        "vt_src": vmem((TP, HEAD, tok), bf16),
        "q_own": vmem((rows, HEAD), bf16),
        "q_far": vmem((rows, HEAD), bf16),
        "k_all": vmem((8, rows, HEAD), bf16),
        "vt_all": vmem((8, HEAD, rows), bf16),
        "scores": vmem((2, WIDE, WIDE), f32),
        "tops": vmem((2, 1, WIDE), f32),
        "m_own": vmem((1, rows), f32),
        "l_own": vmem((1, rows), f32),
        "acc_own": vmem((HEAD, rows), f32),
        "m_far": vmem((1, rows), f32),
        "l_far": vmem((1, rows), f32),
        "acc_far": vmem((HEAD, rows), f32),
        "o_out": vmem((HEAD, rows), bf16),
        "o_in": vmem((HEAD, rows), bf16),
        "stat_out": vmem((8, rows), f32),
        "stat_in": vmem((8, rows), f32),
        "o_rows": vmem((TP, tok, HEAD), bf16),
        "att": vmem((tok, TP * HEAD), bf16),
        "stream": vmem((tok, D), bf16),
        "border": vmem((16, D), bf16),
        "coarse_b": vmem((crows, D), bf16),
        "coarse_grad": vmem((crows, D), f32),
        "coarse_grad_b": vmem((crows, D), bf16),
        "ng": vmem((group, D), bf16),
        "gg": vmem((group, D), bf16),
        "hidden_grad": vmem((group, hid), f32),
        "ng_all": vmem((2, 8 * group, HEAD), bf16),
        "gg_all": vmem((2, 8 * group, HEAD), bf16),
        "hgu": vmem((3, 8, group, hid), bf16),
        "down_out": vmem((TP, crows, D), bf16),
        "down_in": vmem((TP, crows, D), bf16),
        "norm_out": vmem((TP, crows, D), bf16),
        "norm_in": vmem((TP, crows, D), bf16),
        "follow_out": vmem(small, f32),
        "follow_in": vmem(small, f32),
        "gain_out": vmem(small, f32),
        "gain_in": vmem((TP,) + small, f32),
        "gain_mid": vmem(small, f32),
        "gain_half": vmem((8,) + small, f32),
        "gain_far_out": vmem(small, f32),
        "gain_far_in": vmem(small, f32),
        "term_out": vmem((3, hid, HEAD), bf16),
        "term_in": vmem((3, hid, HEAD), bf16),
        "send": pltpu.SemaphoreType.DMA((COPIES,)),
        "recv": pltpu.SemaphoreType.DMA((COPIES,)),
        "local": pltpu.SemaphoreType.DMA((20,)),
    }


class Space:
    pass


def section_kernel(
    names, q_hbm, k_hbm, v_hbm, fine_hbm, cot_hbm, gain_ref, out_hbm, gate_hbm, up_hbm, down_hbm,
    section_ref, stream_grad_ref, gate_grad_ref, up_grad_ref, down_grad_ref, gain_grad_ref, *scratch,
):
    r = Space()
    for name, ref in zip(names, scratch):
        setattr(r, name, ref)
    f32, bf16 = jnp.float32, jnp.bfloat16
    s, t = lax.axis_index("seq"), lax.axis_index("tp")
    half, block = s // 8, lax.rem(s, 8)
    y, core = block // 2, lax.rem(block, 2)
    sib = half * 8 + y * 2 + (1 - core)
    up = half * 8 + lax.rem(y + 1, 4) * 2 + core
    down = half * 8 + lax.rem(y + 3, 4) * 2 + core
    partner = (1 - half) * 8 + block
    number = lax.axis_size("seq") * TP
    flat = s * TP + t
    after, before = lax.rem(flat + 1, number), lax.rem(flat + number - 1, number)
    after, before = (after // TP, lax.rem(after, TP)), (before // TP, lax.rem(before, TP))
    tok = r.fine.shape[0]
    crows = tok // SHORTEN
    group = crows * TP
    hid = r.gate_w.shape[0]

    loads = {}

    def load(name, src):
        loads[name] = pltpu.make_async_copy(src, getattr(r, name), r.local.at[len(loads)])
        loads[name].start()

    load("k_in", k_hbm)
    load("v_in", v_hbm)
    load("q_in", q_hbm)

    barrier = pltpu.get_barrier_semaphore()
    peers = [(s, lax.rem(t + off, TP)) for off in range(1, TP)]
    peers += [(half * 8 + lax.rem(block + off, 8), t) for off in range(1, 8)]
    peers += [(partner, t), after, before]
    for peer in peers:
        pl.semaphore_signal(barrier, inc=1, device_id=peer, device_id_type=MESH)
    for ref, value in ((r.m_own, very_low), (r.l_own, 0.0), (r.acc_own, 0.0),
                       (r.m_far, very_low), (r.l_far, 0.0), (r.acc_far, 0.0)):
        ref[...] = jnp.full(ref.shape, value, f32)
    loads["v_in"].wait()
    for h in range(TP):
        r.vt_src[h] = r.v_in[:, h * HEAD : (h + 1) * HEAD].astype(f32).T.astype(bf16)
    loads["k_in"].wait()
    loads["q_in"].wait()
    pl.semaphore_wait(barrier, len(peers))

    used, sometimes = [], []

    def remote(src, dst, device, always=True):
        kind = len(used) + len(sometimes)
        cp = pltpu.make_async_remote_copy(
            src_ref=src, dst_ref=dst, send_sem=r.send.at[kind], recv_sem=r.recv.at[kind],
            device_id=device, device_id_type=MESH,
        )
        (used if always else sometimes).append(cp)
        return cp

    def go(copies):
        for cp in copies:
            cp.start()
        return copies

    def landed(copies):
        for cp in copies:
            cp.wait_recv()

    def to_group(src, dst):
        return go([
            remote(src(lax.rem(t + off, TP)), dst, (s, lax.rem(t + off, TP))) for off in range(1, TP)
        ])

    def aligned(index, size):
        return pl.ds(pl.multiple_of(index * size, size), size)

    def lanes(index):
        return aligned(index, HEAD)

    band = aligned(t, tok)
    k_copies = to_group(lambda peer: r.k_in.at[:, lanes(peer)], r.k_all.at[block, band, :])
    v_copies = to_group(lambda peer: r.vt_src.at[peer], r.vt_all.at[block, :, band])
    q_copies = to_group(lambda peer: r.q_in.at[:, lanes(peer)], r.q_own.at[band, :])
    own = go([
        pltpu.make_async_copy(r.q_in.at[:, lanes(t)], r.q_own.at[band, :], r.local.at[9]),
        pltpu.make_async_copy(r.k_in.at[:, lanes(t)], r.k_all.at[block, band, :], r.local.at[10]),
        pltpu.make_async_copy(r.vt_src.at[t], r.vt_all.at[block, :, band], r.local.at[11]),
    ])

    load("cot", cot_hbm)

    mine = aligned(t, crows)
    row = lax.broadcasted_iota(jnp.int32, (crows, tok), 0)
    col = lax.broadcasted_iota(jnp.int32, (crows, tok), 1)
    members = jnp.where((col >= row * SHORTEN) & (col < row * SHORTEN + SHORTEN), 1.0, 0.0).astype(bf16)
    loads["cot"].wait()
    r.coarse_grad[...] = jnp.dot(members, r.cot[...], preferred_element_type=f32)
    r.coarse_grad_b[...] = r.coarse_grad[...].astype(bf16)
    r.gg[mine, :] = r.coarse_grad_b[...]

    for cp in own:
        cp.wait()
    k_mine, v_mine = r.k_all.at[block], r.vt_all.at[block]
    landed(k_copies)
    k_ring = go([remote(k_mine, k_mine, (device, t)) for device in (up, down, sib)])
    landed(v_copies)
    v_ring = go([remote(v_mine, v_mine, (device, t)) for device in (down, up, sib)])
    landed(q_copies)
    q_over = remote(r.q_own, r.q_far, (partner, t), always=False)

    @pl.when(half == 1)
    def _():
        q_over.start()

    grad_gather = to_group(lambda peer: r.coarse_grad_b, r.gg.at[mine, :])
    load("out_w", out_hbm)
    load("fine", fine_hbm)
    load("down_w", down_hbm)
    load("gate_w", gate_hbm)
    load("up_w", up_hbm)

    def block_of(step):
        j = step // 2
        dy = j + (j // 2) * (5 - 2 * j)
        return lax.rem(y + dy, 4) * 2 + lax.rem(core + step, 2)

    def score(q_all, key_block, piece, slot):
        kk, u = piece
        st = lax.dot_general(
            r.k_all[key_block, kk * WIDE : (kk + 1) * WIDE], q_all[u * WIDE : (u + 1) * WIDE],
            contract_last, preferred_element_type=f32,
        )
        if slot is None:
            return st
        r.scores[slot] = st
        r.tops[slot] = jnp.max(st, axis=0, keepdims=True)

    def absorb(state, st, top, key_block, piece):
        m_all, l_all, acc_all = state
        kk, u = piece
        cols = slice(u * WIDE, (u + 1) * WIDE)
        older = m_all[:, cols]
        fresh = jnp.maximum(older, top)
        weights = jnp.exp2((st - fresh) * POWER)
        factor = jnp.exp2((older - fresh) * POWER)
        m_all[:, cols] = fresh
        l_all[:, cols] = l_all[:, cols] * factor + jnp.sum(weights, axis=0, keepdims=True)
        acc_all[:, cols] = acc_all[:, cols] * factor + jnp.dot(
            r.vt_all[key_block, :, kk * WIDE : (kk + 1) * WIDE], weights.astype(bf16),
            preferred_element_type=f32,
        )

    pieces = [(kk, u) for kk in range(2) for u in range(2)]

    def sweep(q_all, state, first, last, index):
        score(q_all, index(first), pieces[0], 0)

        @pl.loop(first, last)
        def _(step):
            here, then = index(step), index(jnp.minimum(step + 1, last - 1))
            for i, piece in enumerate(pieces):
                if i + 1 < len(pieces):
                    score(q_all, here, pieces[i + 1], (i + 1) % 2)
                else:
                    score(q_all, then, pieces[0], (i + 1) % 2)
                absorb(state, r.scores[i % 2], r.tops[i % 2], here, piece)

    own_state = (r.m_own, r.l_own, r.acc_own)
    far_state = (r.m_far, r.l_far, r.acc_far)

    def arrived(first, last):
        @pl.when(half == 0)
        def _():
            sweep(r.q_far, far_state, first, last, block_of)

        @pl.when(half == 1)
        def _():
            @pl.loop(max(first, 1), last)
            def _(step):
                @pl.when(block_of(step) < block)
                def _():
                    sweep(r.q_own, own_state, step, step + 1, block_of)

    for piece in ((0, 0), (0, 1), (1, 1)):
        st = score(r.q_own, block, piece, None)
        if piece[0] == piece[1]:
            key_pos = lax.broadcasted_iota(jnp.int32, st.shape, 0)
            query_pos = lax.broadcasted_iota(jnp.int32, st.shape, 1)
            st = jnp.where(key_pos <= query_pos, st, very_low)
        absorb(own_state, st, jnp.max(st, axis=0, keepdims=True), block, piece)

    def to_columns(rows_ref, gathered, sem):
        copies = []
        for part in range(2):
            dst = gathered.at[part, aligned(block, group), :]
            for off in range(1, 8):
                peer = lax.rem(block + off, 8)
                copies.append(remote(rows_ref.at[:, lanes(part * 8 + peer)], dst, (half * 8 + peer, t)))
            kept = pltpu.make_async_copy(
                rows_ref.at[:, lanes(part * 8 + block)], dst, r.local.at[sem + part]
            )
            kept.start()
            kept.wait()
        return go(copies)

    landed([k_ring[2], v_ring[2]])

    @pl.when(half == 0)
    def _():
        q_over.wait_recv()

    arrived(0, 2)
    k_below, v_below = r.k_all.at[block_of(4)], r.vt_all.at[block_of(4)]
    k_above, v_above = r.k_all.at[block_of(2)], r.vt_all.at[block_of(2)]
    k_across, v_across = r.k_all.at[block_of(6)], r.vt_all.at[block_of(6)]
    landed(k_ring[:1])
    k_on = go([remote(k_below, k_below, (up, t)), remote(k_below, k_below, (sib, t))])
    landed(v_ring[:1])
    v_on = go([remote(v_above, v_above, (down, t)), remote(v_above, v_above, (sib, t))])
    landed(k_ring[1:2])
    k_on += go([remote(k_above, k_above, (sib, t))])
    landed(v_ring[1:2])
    v_on += go([remote(v_below, v_below, (sib, t))])
    arrived(2, 3)
    landed([k_on[2], v_on[1]])
    arrived(3, 4)
    landed([k_on[1], v_on[2]])
    landed(k_on[:1])
    k_last = go([remote(k_across, k_across, (sib, t))])
    landed(v_on[:1])
    v_last = go([remote(v_across, v_across, (sib, t))])
    arrived(4, 7)
    landed(k_last + v_last)
    arrived(7, 8)

    o_over = remote(r.o_out, r.o_in, (partner, t), always=False)
    stat_over = remote(r.stat_out, r.stat_in, (partner, t), always=False)

    @pl.when(half == 0)
    def _():
        r.o_out[...] = (r.acc_far[...] / r.l_far[...]).astype(bf16)
        r.stat_out[0:1] = r.m_far[...]
        r.stat_out[1:2] = r.l_far[...]
        o_over.start()
        stat_over.start()
        r.o_in[...] = jnp.zeros(r.o_in.shape, bf16)
        r.stat_in[0:1] = jnp.full(r.m_far.shape, very_low, f32)
        r.stat_in[1:2] = jnp.zeros(r.l_far.shape, f32)

    landed(grad_gather)
    grad_columns = to_columns(r.gg, r.gg_all, 12)

    @pl.when(half == 0)
    def _():
        sweep(r.q_own, own_state, 0, block, lambda step: step)

    @pl.when(half == 1)
    def _():
        o_over.wait_recv()
        stat_over.wait_recv()

    other_m, other_l = r.stat_in[0:1], r.stat_in[1:2]
    top = jnp.maximum(r.m_own[...], other_m)
    share = jnp.exp2((r.m_own[...] - top) * POWER)
    other = other_l * jnp.exp2((other_m - top) * POWER)
    total = r.l_own[...] * share + other
    share, other = share / total, other / total
    for h in range(TP):
        cols = slice(h * tok, (h + 1) * tok)
        mixed = r.acc_own[:, cols] * share[:, cols] + r.o_in[:, cols].astype(f32) * other[:, cols]
        r.o_rows[h] = mixed.T.astype(bf16)
    back = to_group(lambda peer: r.o_rows.at[peer], r.att.at[:, lanes(t)])
    own_back = pltpu.make_async_copy(r.o_rows.at[t], r.att.at[:, lanes(t)], r.local.at[14])
    own_back.start()
    own_back.wait()
    loads["out_w"].wait()
    loads["fine"].wait()
    landed(back)

    projected = jnp.dot(r.att[...], r.out_w[...], preferred_element_type=f32)
    r.stream[...] = (r.fine[...].astype(f32) + projected).astype(bf16)
    border_copy = remote(r.stream.at[pl.ds(tok - 16, 16), :], r.border, after)
    border_copy.start()
    window = jnp.where((col >= row * SHORTEN - (SHORTEN - 1)) & (col <= row * SHORTEN), 1.0, 0.0)
    coarse = jnp.dot(window.astype(bf16), r.stream[...], preferred_element_type=f32)
    edge_row = lax.broadcasted_iota(jnp.int32, (crows, 16), 0)
    edge_col = lax.broadcasted_iota(jnp.int32, (crows, 16), 1)
    edge = jnp.where((edge_row == 0) & (edge_col > 16 - SHORTEN) & (flat > 0), 1.0, 0.0)
    border_copy.wait_recv()
    coarse = coarse + jnp.dot(edge.astype(bf16), r.border[...], preferred_element_type=f32)
    coarse = coarse / SHORTEN
    rstd = lax.rsqrt(jnp.mean(coarse * coarse, axis=-1, keepdims=True) + 1e-05)
    base = coarse * rstd
    r.coarse_b[...] = (base * gain_ref[...]).astype(bf16)
    r.ng[mine, :] = r.coarse_b[...]
    norm_gather = to_group(lambda peer: r.coarse_b, r.ng.at[mine, :])

    loads["down_w"].wait()
    r.hidden_grad[...] = lax.dot_general(
        r.gg[...], r.down_w[...], contract_last, preferred_element_type=f32
    )
    loads["gate_w"].wait()
    loads["up_w"].wait()

    landed(norm_gather)
    norm_columns = to_columns(r.ng, r.ng_all, 15)
    gate = lax.dot_general(r.ng[...], r.gate_w[...], contract_last, preferred_element_type=f32)
    up_v = lax.dot_general(r.ng[...], r.up_w[...], contract_last, preferred_element_type=f32)
    sig = jax.nn.sigmoid(gate)
    act = gate * sig
    above, below, across = (lax.rem(y + dy, 4) * 2 + core for dy in (1, 3, 2))
    cut = group // 2
    parts = (pl.ds(0, cut), pl.ds(cut, cut), pl.ds(0, group))

    def ring(i, source, piece, device):
        ref = r.hgu.at[i, source, parts[piece], :]
        return remote(ref, ref, (device, t))

    def around(i):
        return (
            go([ring(i, block, 0, up), ring(i, block, 1, up)]),
            go([ring(i, block, 1, down), ring(i, block, 0, down)]),
            go([ring(i, block, 2, sib)]),
        )

    rings = []
    r.hgu[0, block] = (act * up_v).astype(bf16)
    rings.append(around(0))
    r.hgu[1, block] = (
        r.hidden_grad[...] * up_v * sig * (1.0 + gate * (1.0 - sig))
    ).astype(bf16)
    rings.append(around(1))
    r.hgu[2, block] = (r.hidden_grad[...] * act).astype(bf16)
    rings.append(around(2))

    part = jnp.dot(r.hgu[0, block], r.down_w[...], preferred_element_type=f32)
    r.down_out[...] = part.astype(bf16).reshape(r.down_out.shape)
    r.down_in[t] = r.down_out[t]
    down_sum = to_group(lambda peer: r.down_out.at[peer], r.down_in.at[t])
    part = jnp.dot(r.hgu[1, block], r.gate_w[...], preferred_element_type=f32) + jnp.dot(
        r.hgu[2, block], r.up_w[...], preferred_element_type=f32
    )
    r.norm_out[...] = part.astype(bf16).reshape(r.norm_out.shape)
    r.norm_in[t] = r.norm_out[t]
    norm_sum = to_group(lambda peer: r.norm_out.at[peer], r.norm_in.at[t])

    def pass_on(i):
        ring_up, ring_down, _ = rings[i]
        landed(ring_up[:1])
        first = go([ring(i, below, 0, up)])
        landed(ring_down[:1])
        first += go([ring(i, above, 1, down)])
        landed(ring_up[1:])
        rest = go([ring(i, below, 2, sib)])
        landed(ring_down[1:])
        rest += go([ring(i, above, 2, sib)])
        return first, rest

    def pass_last(i):
        landed(on[i][0])
        return go([ring(i, across, 2, sib)])

    on, last = [pass_on(0)], []

    landed(down_sum)
    coarse_out = coarse + jnp.sum(r.down_in[...].astype(f32), axis=0)
    spread = (crows, SHORTEN, D)
    section_ref[...] = (
        (r.stream[...].astype(f32).reshape(spread) + coarse_out[:, None, :])
        .reshape(tok, D)
        .astype(bf16)
    )
    on.append(pass_on(1))
    last.append(pass_last(0))

    landed(norm_sum)
    normed_grad = jnp.sum(r.norm_in[...].astype(f32), axis=0)
    width = D // 8

    def fold_row(ref, value):
        for i in range(8):
            ref[i : i + 1, :] = value[:, i * width : (i + 1) * width]

    def flat_row(ref):
        return jnp.concatenate([ref[i : i + 1, :] for i in range(8)], axis=1)

    scaled = normed_grad * gain_ref[...]
    coarse_total = r.coarse_grad[...] + rstd * (
        scaled - base * jnp.mean(scaled * base, axis=-1, keepdims=True)
    )
    fold_row(r.follow_out, coarse_total[0:1])
    follow = remote(r.follow_out, r.follow_in, before)
    follow.start()
    fold_row(r.gain_out, jnp.sum(normed_grad * base, axis=0, keepdims=True))
    r.gain_in[t] = r.gain_out[...]
    gain_sum = to_group(lambda peer: r.gain_out, r.gain_in.at[t])

    on.append(pass_on(2))
    last.append(pass_last(1))

    follow.wait_recv()
    following = jnp.where(flat < number - 1, flat_row(r.follow_in), 0.0)
    ahead = jnp.concatenate([coarse_total[1:], following], axis=0)
    place = lax.broadcasted_iota(jnp.int32, spread, 1)
    contrib = jnp.where(place == 0, coarse_total[:, None, :], ahead[:, None, :])
    stream_grad_ref[...] = (
        (r.cot[...].astype(f32).reshape(spread) + contrib / SHORTEN).reshape(tok, D).astype(bf16)
    )
    last.append(pass_last(2))

    landed(gain_sum)
    r.gain_mid[...] = jnp.sum(r.gain_in[...], axis=0)
    r.gain_half[block] = r.gain_mid[...]
    gain_group = go([
        remote(r.gain_mid, r.gain_half.at[block], (half * 8 + lax.rem(block + off, 8), t))
        for off in range(1, 8)
    ])

    landed(grad_columns + norm_columns)
    outs = (down_grad_ref, gate_grad_ref, up_grad_ref)

    def term(i, part):
        right = (r.gg_all if i == 0 else r.ng_all)[part]
        left = r.hgu[i].reshape(8 * group, hid)
        return lax.dot_general(left, right, contract_first, preferred_element_type=f32)

    terms = []
    for i in range(3):
        landed(rings[i][2] + on[i][1] + last[i])
        r.term_out[i] = term(i, 1 - half).astype(bf16)
        terms += go([remote(r.term_out.at[i], r.term_in.at[i], (partner, t))])
    landed(gain_group)
    r.gain_far_out[...] = jnp.sum(r.gain_half[...], axis=0)
    gain_far = remote(r.gain_far_out, r.gain_far_in, (partner, t))
    gain_far.start()
    for i in range(3):
        outs[i][...] = term(i, half)
    gain_far.wait_recv()
    gain_grad_ref[...] = flat_row(r.gain_far_out) + flat_row(r.gain_far_in)
    for i in range(3):
        terms[i].wait_recv()
        outs[i][...] = outs[i][...] + r.term_in[i].astype(f32)

    for cp in used:
        cp.wait_send()

    @pl.when(half == 1)
    def _():
        q_over.wait_send()

    @pl.when(half == 0)
    def _():
        o_over.wait_send()
        stat_over.wait_send()


def hand_over_kernel(*refs):
    count = (len(refs) - 2) // 3
    ins, outs, held = refs[:count], refs[count : 2 * count], refs[2 * count : 3 * count]
    arrive, leave = refs[-2:]
    first = [pltpu.make_async_copy(a, b, arrive.at[i]) for i, (a, b) in enumerate(zip(ins, held))]
    second = [pltpu.make_async_copy(a, b, leave.at[i]) for i, (a, b) in enumerate(zip(held, outs))]
    for cp in first:
        cp.start()
    for one, two in zip(first, second):
        one.wait()
        two.start()
    for cp in second:
        cp.wait()


def on_device(
    fine_stream,
    queries,
    keys,
    values,
    out_weight,
    norm_gain,
    gate_weight,
    up_weight,
    down_weight,
    cotangent,
):
    tok = fine_stream.shape[0]
    hid = gate_weight.shape[1]
    seq = lax.axis_size("seq")
    f32, bf16 = jnp.float32, jnp.bfloat16
    vmem, hbm = pl.BlockSpec(memory_space=pltpu.VMEM), pl.BlockSpec(memory_space=pltpu.HBM)
    scratch = scratch_of(tok, hid, seq)
    shapes = (
        jax.ShapeDtypeStruct((tok, D), bf16),
        jax.ShapeDtypeStruct((tok, D), bf16),
        jax.ShapeDtypeStruct((hid, D // seq), f32),
        jax.ShapeDtypeStruct((hid, D // seq), f32),
        jax.ShapeDtypeStruct((hid, D // seq), f32),
        jax.ShapeDtypeStruct((1, D), f32),
    )
    outs = pl.pallas_call(
        lambda *refs: section_kernel(tuple(scratch), *refs),
        out_shape=shapes,
        in_specs=[hbm] * 5 + [vmem] + [hbm] * 4,
        out_specs=(vmem,) * 6,
        scratch_shapes=list(scratch.values()),
        compiler_params=pltpu.CompilerParams(
            collective_id=0, has_side_effects=True, vmem_limit_bytes=60 * 1024 * 1024
        ),
        name="section",
    )(
        queries, keys, values, fine_stream, cotangent, norm_gain.reshape(1, D),
        out_weight, gate_weight.T, up_weight.T, down_weight,
    )
    section_out, stream_grad, gate_grad, up_grad, down_grad, gain_grad = pl.pallas_call(
        hand_over_kernel,
        out_shape=shapes,
        in_specs=[hbm] * 6,
        out_specs=(hbm,) * 6,
        scratch_shapes=[pltpu.VMEM(shape.shape, shape.dtype) for shape in shapes]
        + [pltpu.SemaphoreType.DMA((6,)), pltpu.SemaphoreType.DMA((6,))],
        compiler_params=pltpu.CompilerParams(vmem_limit_bytes=60 * 1024 * 1024),
        name="hand_over",
    )(*outs)
    return (section_out, stream_grad, gate_grad.T, up_grad.T, down_grad, gain_grad.reshape(D))


def solution(mesh):
    return jax.shard_map(
        on_device,
        mesh=mesh,
        in_specs=(
            P(("seq", "tp"), None),
            P(("seq", "tp"), None),
            P(("seq", "tp"), None),
            P(("seq", "tp"), None),
            P(),
            P(),
            P(None, "tp"),
            P(None, "tp"),
            P("tp", None),
            P(("seq", "tp"), None),
        ),
        out_specs=(
            P(("seq", "tp"), None),
            P(("seq", "tp"), None),
            P("seq", "tp"),
            P("seq", "tp"),
            P("tp", "seq"),
            P(),
        ),
        check_vma=False,
    )
```

```python
import math

import jax
import jax.numpy as jnp
from jax import lax
from jax.experimental import pallas as pl
from jax.experimental.pallas import tpu as pltpu
from jax.sharding import PartitionSpec as P

D = 2048
HEAD = 128
SHORTEN = 8
MESH = pl.DeviceIdType.MESH
TP = 8
WIDE = 512
COPIES = 190

contract_last = (((1,), (1,)), ((), ()))
contract_first = (((0,), (0,)), ((), ()))
very_low = -1e30
POWER = math.log2(math.e) * HEAD ** (-0.5)


def scratch_of(tok, hid, seq):
    crows, group, rows = tok // SHORTEN, tok // SHORTEN * TP, tok * TP
    f32, bf16 = jnp.float32, jnp.bfloat16
    vmem = pltpu.VMEM
    small = (8, D // 8)
    return {
        "q_in": vmem((tok, TP * HEAD), bf16),
        "k_in": vmem((tok, TP * HEAD), bf16),
        "v_in": vmem((tok, TP * HEAD), bf16),
        "fine": vmem((tok, D), bf16),
        "cot": vmem((tok, D), bf16),
        "out_w": vmem((TP * HEAD, D), bf16),
        "gate_w": vmem((hid, D), bf16),
        "up_w": vmem((hid, D), bf16),
        "down_w": vmem((hid, D), bf16),
        "vt_src": vmem((TP, HEAD, tok), bf16),
        "q_own": vmem((rows, HEAD), bf16),
        "q_far": vmem((rows, HEAD), bf16),
        "k_all": vmem((8, rows, HEAD), bf16),
        "vt_all": vmem((8, HEAD, rows), bf16),
        "scores": vmem((2, WIDE, WIDE), f32),
        "tops": vmem((2, 1, WIDE), f32),
        "m_own": vmem((1, rows), f32),
        "l_own": vmem((1, rows), f32),
        "acc_own": vmem((HEAD, rows), f32),
        "m_far": vmem((1, rows), f32),
        "l_far": vmem((1, rows), f32),
        "acc_far": vmem((HEAD, rows), f32),
        "o_own": vmem((HEAD, rows), bf16),
        "o_far": vmem((HEAD, rows), bf16),
        "stat_own": vmem((8, rows), f32),
        "stat_far": vmem((8, rows), f32),
        "own_in": vmem((TP, HEAD, tok), bf16),
        "far_in": vmem((TP, HEAD, tok), bf16),
        "own_stat_in": vmem((TP, 8, tok), f32),
        "far_stat_in": vmem((TP, 8, tok), f32),
        "att": vmem((TP * HEAD, tok), bf16),
        "stream": vmem((tok, D), bf16),
        "border_out": vmem(small, f32),
        "border_in": vmem(small, f32),
        "coarse_b": vmem((crows, D), bf16),
        "coarse_grad": vmem((crows, D), f32),
        "coarse_grad_b": vmem((crows, D), bf16),
        "ng": vmem((group, D), bf16),
        "gg": vmem((group, D), bf16),
        "hidden_grad": vmem((group, hid), f32),
        "ng_all": vmem((8 * group, 2 * HEAD), bf16),
        "gg_all": vmem((8 * group, 2 * HEAD), bf16),
        "hgu": vmem((3, 8, group, hid), bf16),
        "down_out": vmem((TP, crows, D), bf16),
        "down_in": vmem((TP, crows, D), bf16),
        "norm_out": vmem((TP, crows, D), bf16),
        "norm_in": vmem((TP, crows, D), bf16),
        "follow_out": vmem(small, f32),
        "follow_in": vmem(small, f32),
        "gain_out": vmem(small, f32),
        "gain_in": vmem((TP,) + small, f32),
        "gain_mid": vmem(small, f32),
        "gain_half": vmem((8,) + small, f32),
        "gain_far_out": vmem(small, f32),
        "gain_far_in": vmem(small, f32),
        "term": vmem((3, hid, 2 * HEAD), f32),
        "term_out": vmem((3, hid, HEAD), bf16),
        "term_in": vmem((3, hid, HEAD), bf16),
        "send": pltpu.SemaphoreType.DMA((COPIES,)),
        "recv": pltpu.SemaphoreType.DMA((COPIES,)),
        "local": pltpu.SemaphoreType.DMA((20,)),
    }


class Space:
    pass


def section_kernel(
    names, q_hbm, k_hbm, v_hbm, fine_hbm, cot_hbm, gain_ref, out_hbm, gate_hbm, up_hbm, down_hbm,
    section_ref, stream_grad_ref, gate_grad_ref, up_grad_ref, down_grad_ref, gain_grad_ref, *scratch,
):
    r = Space()
    for name, ref in zip(names, scratch):
        setattr(r, name, ref)
    f32, bf16 = jnp.float32, jnp.bfloat16
    s, t = lax.axis_index("seq"), lax.axis_index("tp")
    half, block = s // 8, lax.rem(s, 8)
    y, core = block // 2, lax.rem(block, 2)
    sib = half * 8 + y * 2 + (1 - core)
    up = half * 8 + lax.rem(y + 1, 4) * 2 + core
    down = half * 8 + lax.rem(y + 3, 4) * 2 + core
    partner = (1 - half) * 8 + block
    number = lax.axis_size("seq") * TP
    flat = s * TP + t
    after, before = lax.rem(flat + 1, number), lax.rem(flat + number - 1, number)
    after, before = (after // TP, lax.rem(after, TP)), (before // TP, lax.rem(before, TP))
    tok = r.fine.shape[0]
    crows = tok // SHORTEN
    group = crows * TP
    hid = r.gate_w.shape[0]

    loads = {}

    def load(name, src):
        loads[name] = pltpu.make_async_copy(src, getattr(r, name), r.local.at[len(loads)])
        loads[name].start()

    load("k_in", k_hbm)
    load("v_in", v_hbm)
    load("q_in", q_hbm)

    barrier = pltpu.get_barrier_semaphore()
    peers = [(s, lax.rem(t + off, TP)) for off in range(1, TP)]
    peers += [(half * 8 + lax.rem(block + off, 8), t) for off in range(1, 8)]
    peers += [(partner, lax.rem(t + off, TP)) for off in range(TP)] + [after, before]
    for peer in peers:
        pl.semaphore_signal(barrier, inc=1, device_id=peer, device_id_type=MESH)
    for ref, value in ((r.m_own, very_low), (r.l_own, 0.0), (r.acc_own, 0.0),
                       (r.m_far, very_low), (r.l_far, 0.0), (r.acc_far, 0.0)):
        ref[...] = jnp.full(ref.shape, value, f32)
    loads["v_in"].wait()
    for h in range(TP):
        r.vt_src[h] = r.v_in[:, h * HEAD : (h + 1) * HEAD].astype(f32).T.astype(bf16)
    loads["k_in"].wait()
    loads["q_in"].wait()
    pl.semaphore_wait(barrier, len(peers))

    used, sometimes = [], []

    def remote(src, dst, device, always=True):
        kind = len(used) + len(sometimes)
        cp = pltpu.make_async_remote_copy(
            src_ref=src, dst_ref=dst, send_sem=r.send.at[kind], recv_sem=r.recv.at[kind],
            device_id=device, device_id_type=MESH,
        )
        (used if always else sometimes).append(cp)
        return cp

    def go(copies):
        for cp in copies:
            cp.start()
        return copies

    def landed(copies):
        for cp in copies:
            cp.wait_recv()

    def to_group(src, dst):
        return go([
            remote(src(lax.rem(t + off, TP)), dst, (s, lax.rem(t + off, TP))) for off in range(1, TP)
        ])

    def aligned(index, size):
        return pl.ds(pl.multiple_of(index * size, size), size)

    def lanes(index):
        return aligned(index, HEAD)

    width = D // 8

    def fold_row(ref, value):
        for i in range(8):
            ref[i : i + 1, :] = value[:, i * width : (i + 1) * width]

    def flat_row(ref):
        return jnp.concatenate([ref[i : i + 1, :] for i in range(8)], axis=1)

    band = aligned(t, tok)
    k_copies = to_group(lambda peer: r.k_in.at[:, lanes(peer)], r.k_all.at[block, band, :])
    v_copies = to_group(lambda peer: r.vt_src.at[peer], r.vt_all.at[block, :, band])
    q_copies = to_group(lambda peer: r.q_in.at[:, lanes(peer)], r.q_own.at[band, :])
    own = go([
        pltpu.make_async_copy(r.q_in.at[:, lanes(t)], r.q_own.at[band, :], r.local.at[9]),
        pltpu.make_async_copy(r.k_in.at[:, lanes(t)], r.k_all.at[block, band, :], r.local.at[10]),
        pltpu.make_async_copy(r.vt_src.at[t], r.vt_all.at[block, :, band], r.local.at[11]),
    ])

    load("cot", cot_hbm)

    mine = aligned(t, crows)
    row = lax.broadcasted_iota(jnp.int32, (crows, tok), 0)
    col = lax.broadcasted_iota(jnp.int32, (crows, tok), 1)
    members = jnp.where((col >= row * SHORTEN) & (col < row * SHORTEN + SHORTEN), 1.0, 0.0).astype(bf16)
    loads["cot"].wait()
    r.coarse_grad[...] = jnp.dot(members, r.cot[...], preferred_element_type=f32)
    r.coarse_grad_b[...] = r.coarse_grad[...].astype(bf16)
    r.gg[mine, :] = r.coarse_grad_b[...]

    for cp in own:
        cp.wait()
    k_mine, v_mine = r.k_all.at[block], r.vt_all.at[block]
    landed(k_copies)
    k_ring = go([remote(k_mine, k_mine, (device, t)) for device in (up, down, sib)])
    landed(v_copies)
    v_ring = go([remote(v_mine, v_mine, (device, t)) for device in (down, up, sib)])
    landed(q_copies)
    q_over = remote(r.q_own, r.q_far, (partner, t), always=False)

    @pl.when(half == 1)
    def _():
        q_over.start()

    grad_gather = to_group(lambda peer: r.coarse_grad_b, r.gg.at[mine, :])
    load("out_w", out_hbm)
    load("fine", fine_hbm)
    load("down_w", down_hbm)
    load("gate_w", gate_hbm)
    load("up_w", up_hbm)

    def block_of(step):
        j = step // 2
        dy = j + (j // 2) * (5 - 2 * j)
        return lax.rem(y + dy, 4) * 2 + lax.rem(core + step, 2)

    def score(q_all, key_block, piece, slot):
        kk, u = piece
        st = lax.dot_general(
            r.k_all[key_block, kk * WIDE : (kk + 1) * WIDE], q_all[u * WIDE : (u + 1) * WIDE],
            contract_last, preferred_element_type=f32,
        )
        if slot is None:
            return st
        r.scores[slot] = st
        r.tops[slot] = jnp.max(st, axis=0, keepdims=True)

    def absorb(state, st, top, key_block, piece):
        m_all, l_all, acc_all = state
        kk, u = piece
        cols = slice(u * WIDE, (u + 1) * WIDE)
        older = m_all[:, cols]
        fresh = jnp.maximum(older, top)
        weights = jnp.exp2((st - fresh) * POWER)
        factor = jnp.exp2((older - fresh) * POWER)
        m_all[:, cols] = fresh
        l_all[:, cols] = l_all[:, cols] * factor + jnp.sum(weights, axis=0, keepdims=True)
        acc_all[:, cols] = acc_all[:, cols] * factor + jnp.dot(
            r.vt_all[key_block, :, kk * WIDE : (kk + 1) * WIDE], weights.astype(bf16),
            preferred_element_type=f32,
        )

    pieces = [(kk, u) for kk in range(2) for u in range(2)]

    def sweep(q_all, state, first, last, index):
        score(q_all, index(first), pieces[0], 0)

        @pl.loop(first, last)
        def _(step):
            here, then = index(step), index(jnp.minimum(step + 1, last - 1))
            for i, piece in enumerate(pieces):
                if i + 1 < len(pieces):
                    score(q_all, here, pieces[i + 1], (i + 1) % 2)
                else:
                    score(q_all, then, pieces[0], (i + 1) % 2)
                absorb(state, r.scores[i % 2], r.tops[i % 2], here, piece)

    own_state = (r.m_own, r.l_own, r.acc_own)
    far_state = (r.m_far, r.l_far, r.acc_far)

    def arrived(first, last):
        @pl.when(half == 0)
        def _():
            sweep(r.q_far, far_state, first, last, block_of)

        @pl.when(half == 1)
        def _():
            @pl.loop(max(first, 1), last)
            def _(step):
                @pl.when(block_of(step) < block)
                def _():
                    sweep(r.q_own, own_state, step, step + 1, block_of)

    for piece in ((0, 0), (0, 1), (1, 1)):
        st = score(r.q_own, block, piece, None)
        if piece[0] == piece[1]:
            key_pos = lax.broadcasted_iota(jnp.int32, st.shape, 0)
            query_pos = lax.broadcasted_iota(jnp.int32, st.shape, 1)
            st = jnp.where(key_pos <= query_pos, st, very_low)
        absorb(own_state, st, jnp.max(st, axis=0, keepdims=True), block, piece)

    def to_columns(rows_ref, gathered, sem):
        copies = []
        for part in range(2):
            dst = gathered.at[aligned(block, group), part * HEAD : (part + 1) * HEAD]
            for off in range(1, 8):
                peer = lax.rem(block + off, 8)
                copies.append(remote(rows_ref.at[:, lanes(part * 8 + peer)], dst, (half * 8 + peer, t)))
            kept = pltpu.make_async_copy(
                rows_ref.at[:, lanes(part * 8 + block)], dst, r.local.at[sem + part]
            )
            kept.start()
            kept.wait()
        return go(copies)

    landed([k_ring[2], v_ring[2]])

    @pl.when(half == 0)
    def _():
        q_over.wait_recv()

    arrived(0, 2)
    k_below, v_below = r.k_all.at[block_of(4)], r.vt_all.at[block_of(4)]
    k_above, v_above = r.k_all.at[block_of(2)], r.vt_all.at[block_of(2)]
    k_across, v_across = r.k_all.at[block_of(6)], r.vt_all.at[block_of(6)]
    landed(k_ring[:1])
    k_on = go([remote(k_below, k_below, (up, t)), remote(k_below, k_below, (sib, t))])
    landed(v_ring[:1])
    v_on = go([remote(v_above, v_above, (down, t)), remote(v_above, v_above, (sib, t))])
    landed(k_ring[1:2])
    k_on += go([remote(k_above, k_above, (sib, t))])
    landed(v_ring[1:2])
    v_on += go([remote(v_below, v_below, (sib, t))])
    arrived(2, 3)
    landed([k_on[2], v_on[1]])
    arrived(3, 4)
    landed([k_on[1], v_on[2]])
    landed(k_on[:1])
    k_last = go([remote(k_across, k_across, (sib, t))])
    landed(v_on[:1])
    v_last = go([remote(v_across, v_across, (sib, t))])
    arrived(4, 7)
    landed(k_last + v_last)
    arrived(7, 8)

    def normalized(state, out, stat):
        m_all, l_all, acc_all = state
        out[...] = (acc_all[...] / l_all[...]).astype(bf16)
        stat[0:1] = m_all[...]
        stat[1:2] = l_all[...]

    far_back = []
    for off in range(TP):
        peer = lax.rem(t + off, TP)
        far_back += [
            remote(r.o_far.at[:, lanes(peer)], r.far_in.at[t], (partner, peer), always=False),
            remote(r.stat_far.at[:, lanes(peer)], r.far_stat_in.at[t], (partner, peer), always=False),
        ]

    @pl.when(half == 0)
    def _():
        normalized(far_state, r.o_far, r.stat_far)
        go(far_back)
        r.far_in[...] = jnp.zeros(r.far_in.shape, bf16)
        r.far_stat_in[:, 0:1] = jnp.full((TP, 1, tok), very_low, f32)
        r.far_stat_in[:, 1:2] = jnp.zeros((TP, 1, tok), f32)
        sweep(r.q_own, own_state, 0, block, lambda step: step)

    normalized(own_state, r.o_own, r.stat_own)
    back = to_group(lambda peer: r.o_own.at[:, lanes(peer)], r.own_in.at[t])
    back += to_group(lambda peer: r.stat_own.at[:, lanes(peer)], r.own_stat_in.at[t])
    kept = go([
        pltpu.make_async_copy(r.o_own.at[:, lanes(t)], r.own_in.at[t], r.local.at[14]),
        pltpu.make_async_copy(r.stat_own.at[:, lanes(t)], r.own_stat_in.at[t], r.local.at[17]),
    ])
    landed(grad_gather)
    grad_columns = to_columns(r.gg, r.gg_all, 12)
    for cp in kept:
        cp.wait()
    loads["out_w"].wait()
    loads["fine"].wait()
    landed(back)

    @pl.when(half == 1)
    def _():
        landed(far_back)

    for h in range(TP):
        own_m, own_l = r.own_stat_in[h, 0:1], r.own_stat_in[h, 1:2]
        far_m, far_l = r.far_stat_in[h, 0:1], r.far_stat_in[h, 1:2]
        top = jnp.maximum(own_m, far_m)
        own_l = own_l * jnp.exp2((own_m - top) * POWER)
        far_l = far_l * jnp.exp2((far_m - top) * POWER)
        total = own_l + far_l
        r.att[h * HEAD : (h + 1) * HEAD] = (
            r.own_in[h].astype(f32) * (own_l / total) + r.far_in[h].astype(f32) * (far_l / total)
        ).astype(bf16)
    projected = lax.dot_general(r.att[...], r.out_w[...], contract_first, preferred_element_type=f32)
    r.stream[...] = (r.fine[...].astype(f32) + projected).astype(bf16)
    row = lax.broadcasted_iota(jnp.int32, (crows + 8, tok), 0)
    col = lax.broadcasted_iota(jnp.int32, (crows + 8, tok), 1)
    window = jnp.where((col >= row * SHORTEN - (SHORTEN - 1)) & (col <= row * SHORTEN), 1.0, 0.0)
    coarse = jnp.dot(window.astype(bf16), r.stream[...], preferred_element_type=f32)
    fold_row(r.border_out, coarse[crows : crows + 1])
    border_copy = remote(r.border_out, r.border_in, after)
    border_copy.start()
    border_copy.wait_recv()
    edge = jnp.where(flat > 0, flat_row(r.border_in), 0.0)
    first = lax.broadcasted_iota(jnp.int32, (crows, D), 0) == 0
    coarse = coarse[:crows] + jnp.where(first, edge, 0.0)
    coarse = coarse / SHORTEN
    rstd = lax.rsqrt(jnp.mean(coarse * coarse, axis=-1, keepdims=True) + 1e-05)
    base = coarse * rstd
    r.coarse_b[...] = (base * gain_ref[...]).astype(bf16)
    r.ng[mine, :] = r.coarse_b[...]
    norm_gather = to_group(lambda peer: r.coarse_b, r.ng.at[mine, :])

    loads["down_w"].wait()
    r.hidden_grad[...] = lax.dot_general(
        r.gg[...], r.down_w[...], contract_last, preferred_element_type=f32
    )
    loads["gate_w"].wait()
    loads["up_w"].wait()

    landed(norm_gather)
    norm_columns = to_columns(r.ng, r.ng_all, 15)
    gate = lax.dot_general(r.ng[...], r.gate_w[...], contract_last, preferred_element_type=f32)
    up_v = lax.dot_general(r.ng[...], r.up_w[...], contract_last, preferred_element_type=f32)
    sig = jax.nn.sigmoid(gate)
    act = gate * sig
    above, below, across = (lax.rem(y + dy, 4) * 2 + core for dy in (1, 3, 2))
    cut = group // 2
    parts = (pl.ds(0, cut), pl.ds(cut, cut), pl.ds(0, group))

    def ring(i, source, piece, device):
        ref = r.hgu.at[i, source, parts[piece], :]
        return remote(ref, ref, (device, t))

    def around(i):
        return (
            go([ring(i, block, 0, up), ring(i, block, 1, up)]),
            go([ring(i, block, 1, down), ring(i, block, 0, down)]),
            go([ring(i, block, 2, sib)]),
        )

    rings = []
    r.hgu[0, block] = (act * up_v).astype(bf16)
    rings.append(around(0))
    r.hgu[1, block] = (
        r.hidden_grad[...] * up_v * sig * (1.0 + gate * (1.0 - sig))
    ).astype(bf16)
    rings.append(around(1))
    r.hgu[2, block] = (r.hidden_grad[...] * act).astype(bf16)
    rings.append(around(2))

    part = jnp.dot(r.hgu[0, block], r.down_w[...], preferred_element_type=f32)
    r.down_out[...] = part.astype(bf16).reshape(r.down_out.shape)
    r.down_in[t] = r.down_out[t]
    down_sum = to_group(lambda peer: r.down_out.at[peer], r.down_in.at[t])
    part = jnp.dot(r.hgu[1, block], r.gate_w[...], preferred_element_type=f32) + jnp.dot(
        r.hgu[2, block], r.up_w[...], preferred_element_type=f32
    )
    r.norm_out[...] = part.astype(bf16).reshape(r.norm_out.shape)
    r.norm_in[t] = r.norm_out[t]
    norm_sum = to_group(lambda peer: r.norm_out.at[peer], r.norm_in.at[t])

    def pass_on(i):
        ring_up, ring_down, _ = rings[i]
        landed(ring_up[:1])
        first = go([ring(i, below, 0, up)])
        landed(ring_down[:1])
        first += go([ring(i, above, 1, down)])
        landed(ring_up[1:])
        rest = go([ring(i, below, 2, sib)])
        landed(ring_down[1:])
        rest += go([ring(i, above, 2, sib)])
        return first, rest

    def pass_last(i):
        landed(on[i][0])
        return go([ring(i, across, 2, sib)])

    on, last = [pass_on(0)], []

    landed(down_sum)
    coarse_out = coarse + jnp.sum(r.down_in[...].astype(f32), axis=0)
    spread = (crows, SHORTEN, D)
    section_ref[...] = (
        (r.stream[...].astype(f32).reshape(spread) + coarse_out[:, None, :])
        .reshape(tok, D)
        .astype(bf16)
    )
    on.append(pass_on(1))
    last.append(pass_last(0))

    landed(norm_sum)
    normed_grad = jnp.sum(r.norm_in[...].astype(f32), axis=0)
    scaled = normed_grad * gain_ref[...]
    coarse_total = r.coarse_grad[...] + rstd * (
        scaled - base * jnp.mean(scaled * base, axis=-1, keepdims=True)
    )
    fold_row(r.follow_out, coarse_total[0:1])
    follow = remote(r.follow_out, r.follow_in, before)
    follow.start()
    fold_row(r.gain_out, jnp.sum(normed_grad * base, axis=0, keepdims=True))
    r.gain_in[t] = r.gain_out[...]
    gain_sum = to_group(lambda peer: r.gain_out, r.gain_in.at[t])

    on.append(pass_on(2))
    last.append(pass_last(1))

    outs = (down_grad_ref, gate_grad_ref, up_grad_ref)

    def term(i):
        landed(rings[i][2] + on[i][1] + last[i])
        right = r.gg_all if i == 0 else r.ng_all
        left = r.hgu[i].reshape(8 * group, hid)
        r.term[i] = lax.dot_general(left, right[...], contract_first, preferred_element_type=f32)
        r.term_out[i] = r.term[i, :, lanes(1 - half)].astype(bf16)
        return go([remote(r.term_out.at[i], r.term_in.at[i], (partner, t))])

    landed(grad_columns)
    terms = term(0)
    last.append(pass_last(2))

    landed(gain_sum)
    r.gain_mid[...] = jnp.sum(r.gain_in[...], axis=0)
    r.gain_half[block] = r.gain_mid[...]
    gain_group = go([
        remote(r.gain_mid, r.gain_half.at[block], (half * 8 + lax.rem(block + off, 8), t))
        for off in range(1, 8)
    ])
    landed(norm_columns)
    terms += term(1)

    follow.wait_recv()
    following = jnp.where(flat < number - 1, flat_row(r.follow_in), 0.0)
    ahead = jnp.concatenate([coarse_total[1:], following], axis=0)
    place = lax.broadcasted_iota(jnp.int32, spread, 1)
    contrib = jnp.where(place == 0, coarse_total[:, None, :], ahead[:, None, :])
    stream_grad_ref[...] = (
        (r.cot[...].astype(f32).reshape(spread) + contrib / SHORTEN).reshape(tok, D).astype(bf16)
    )

    terms += term(2)
    landed(gain_group)
    r.gain_far_out[...] = jnp.sum(r.gain_half[...], axis=0)
    gain_far = remote(r.gain_far_out, r.gain_far_in, (partner, t))
    gain_far.start()
    for i in range(3):
        outs[i][...] = r.term[i, :, lanes(half)]
    gain_far.wait_recv()
    gain_grad_ref[...] = flat_row(r.gain_far_out) + flat_row(r.gain_far_in)
    for i in range(3):
        terms[i].wait_recv()
        outs[i][...] = outs[i][...] + r.term_in[i].astype(f32)

    for cp in used:
        cp.wait_send()

    @pl.when(half == 1)
    def _():
        q_over.wait_send()

    @pl.when(half == 0)
    def _():
        for cp in far_back:
            cp.wait_send()


def hand_over_kernel(*refs):
    count = (len(refs) - 2) // 3
    ins, outs, held = refs[:count], refs[count : 2 * count], refs[2 * count : 3 * count]
    arrive, leave = refs[-2:]
    first = [pltpu.make_async_copy(a, b, arrive.at[i]) for i, (a, b) in enumerate(zip(ins, held))]
    second = [pltpu.make_async_copy(a, b, leave.at[i]) for i, (a, b) in enumerate(zip(held, outs))]
    for cp in first:
        cp.start()
    for one, two in zip(first, second):
        one.wait()
        two.start()
    for cp in second:
        cp.wait()


def on_device(
    fine_stream,
    queries,
    keys,
    values,
    out_weight,
    norm_gain,
    gate_weight,
    up_weight,
    down_weight,
    cotangent,
):
    tok = fine_stream.shape[0]
    hid = gate_weight.shape[1]
    seq = lax.axis_size("seq")
    f32, bf16 = jnp.float32, jnp.bfloat16
    vmem, hbm = pl.BlockSpec(memory_space=pltpu.VMEM), pl.BlockSpec(memory_space=pltpu.HBM)
    scratch = scratch_of(tok, hid, seq)
    shapes = (
        jax.ShapeDtypeStruct((tok, D), bf16),
        jax.ShapeDtypeStruct((tok, D), bf16),
        jax.ShapeDtypeStruct((hid, D // seq), f32),
        jax.ShapeDtypeStruct((hid, D // seq), f32),
        jax.ShapeDtypeStruct((hid, D // seq), f32),
        jax.ShapeDtypeStruct((1, D), f32),
    )
    outs = pl.pallas_call(
        lambda *refs: section_kernel(tuple(scratch), *refs),
        out_shape=shapes,
        in_specs=[hbm] * 5 + [vmem] + [hbm] * 4,
        out_specs=(vmem,) * 6,
        scratch_shapes=list(scratch.values()),
        compiler_params=pltpu.CompilerParams(
            collective_id=0, has_side_effects=True, vmem_limit_bytes=60 * 1024 * 1024
        ),
        name="section",
    )(
        queries, keys, values, fine_stream, cotangent, norm_gain.reshape(1, D),
        out_weight, gate_weight.T, up_weight.T, down_weight,
    )
    section_out, stream_grad, gate_grad, up_grad, down_grad, gain_grad = pl.pallas_call(
        hand_over_kernel,
        out_shape=shapes,
        in_specs=[hbm] * 6,
        out_specs=(hbm,) * 6,
        scratch_shapes=[pltpu.VMEM(shape.shape, shape.dtype) for shape in shapes]
        + [pltpu.SemaphoreType.DMA((6,)), pltpu.SemaphoreType.DMA((6,))],
        compiler_params=pltpu.CompilerParams(vmem_limit_bytes=60 * 1024 * 1024),
        name="hand_over",
    )(*outs)
    return (section_out, stream_grad, gate_grad.T, up_grad.T, down_grad, gain_grad.reshape(D))


def solution(mesh):
    return jax.shard_map(
        on_device,
        mesh=mesh,
        in_specs=(
            P(("seq", "tp"), None),
            P(("seq", "tp"), None),
            P(("seq", "tp"), None),
            P(("seq", "tp"), None),
            P(),
            P(),
            P(None, "tp"),
            P(None, "tp"),
            P("tp", None),
            P(("seq", "tp"), None),
        ),
        out_specs=(
            P(("seq", "tp"), None),
            P(("seq", "tp"), None),
            P("seq", "tp"),
            P("seq", "tp"),
            P("tp", "seq"),
            P(),
        ),
        check_vma=False,
    )
```

```python
import math

import jax
import jax.numpy as jnp
from jax import lax
from jax.experimental import pallas as pl
from jax.experimental.pallas import tpu as pltpu
from jax.sharding import PartitionSpec as P

D = 2048
HEAD = 128
SHORTEN = 8
MESH = pl.DeviceIdType.MESH
TP = 8
WIDE = 512
COPIES = 190

contract_last = (((1,), (1,)), ((), ()))
contract_first = (((0,), (0,)), ((), ()))
very_low = -1e30
POWER = math.log2(math.e) * HEAD ** (-0.5)


def scratch_of(tok, hid, seq):
    crows, group, rows = tok // SHORTEN, tok // SHORTEN * TP, tok * TP
    f32, bf16 = jnp.float32, jnp.bfloat16
    vmem = pltpu.VMEM
    small = (8, D // 8)
    return {
        "q_in": vmem((tok, TP * HEAD), bf16),
        "k_in": vmem((tok, TP * HEAD), bf16),
        "v_in": vmem((tok, TP * HEAD), bf16),
        "fine": vmem((tok, D), bf16),
        "cot": vmem((tok, D), bf16),
        "out_w": vmem((TP * HEAD, D), bf16),
        "gate_w": vmem((hid, D), bf16),
        "up_w": vmem((hid, D), bf16),
        "down_w": vmem((hid, D), bf16),
        "vt_src": vmem((TP, HEAD, tok), bf16),
        "q_own": vmem((rows, HEAD), bf16),
        "q_far": vmem((rows, HEAD), bf16),
        "k_all": vmem((8, rows, HEAD), bf16),
        "vt_all": vmem((8, HEAD, rows), bf16),
        "scores": vmem((2, WIDE, WIDE), f32),
        "tops": vmem((2, 1, WIDE), f32),
        "m_own": vmem((1, rows), f32),
        "l_own": vmem((1, rows), f32),
        "acc_own": vmem((HEAD, rows), f32),
        "m_far": vmem((1, rows), f32),
        "l_far": vmem((1, rows), f32),
        "acc_far": vmem((HEAD, rows), f32),
        "o_own": vmem((HEAD, rows), bf16),
        "o_far": vmem((HEAD, rows), bf16),
        "stat_own": vmem((8, rows), f32),
        "stat_far": vmem((8, rows), f32),
        "own_in": vmem((TP, HEAD, tok), bf16),
        "far_in": vmem((TP, HEAD, tok), bf16),
        "own_stat_in": vmem((TP, 8, tok), f32),
        "far_stat_in": vmem((TP, 8, tok), f32),
        "att": vmem((TP * HEAD, tok), bf16),
        "stream": vmem((tok, D), bf16),
        "border_out": vmem(small, f32),
        "border_in": vmem(small, f32),
        "coarse_b": vmem((crows, D), bf16),
        "coarse_grad": vmem((crows, D), f32),
        "coarse_grad_b": vmem((crows, D), bf16),
        "ng": vmem((group, D), bf16),
        "gg": vmem((group, D), bf16),
        "hidden_grad": vmem((group, hid), f32),
        "ng_all": vmem((4 * group, 4 * HEAD), bf16),
        "gg_all": vmem((4 * group, 4 * HEAD), bf16),
        "hgu": vmem((3, 4, group, hid), bf16),
        "down_out": vmem((TP, crows, D), bf16),
        "down_in": vmem((TP, crows, D), bf16),
        "norm_out": vmem((TP, crows, D), bf16),
        "norm_in": vmem((TP, crows, D), bf16),
        "follow_out": vmem(small, f32),
        "follow_in": vmem(small, f32),
        "gain_out": vmem(small, f32),
        "gain_in": vmem((TP,) + small, f32),
        "gain_mid": vmem(small, f32),
        "gain_half": vmem((8,) + small, f32),
        "gain_far_out": vmem(small, f32),
        "gain_far_in": vmem(small, f32),
        "term": vmem((3, hid, 4 * HEAD), f32),
        "sib_out": vmem((3, 2, hid, HEAD), bf16),
        "sib_in": vmem((3, 2, hid, HEAD), bf16),
        "term_out": vmem((3, hid, HEAD), bf16),
        "term_in": vmem((3, hid, HEAD), bf16),
        "send": pltpu.SemaphoreType.DMA((COPIES,)),
        "recv": pltpu.SemaphoreType.DMA((COPIES,)),
        "local": pltpu.SemaphoreType.DMA((20,)),
    }


class Space:
    pass


def section_kernel(
    names, q_hbm, k_hbm, v_hbm, fine_hbm, cot_hbm, gain_ref, out_hbm, gate_hbm, up_hbm, down_hbm,
    section_ref, stream_grad_ref, gate_grad_ref, up_grad_ref, down_grad_ref, gain_grad_ref, *scratch,
):
    r = Space()
    for name, ref in zip(names, scratch):
        setattr(r, name, ref)
    f32, bf16 = jnp.float32, jnp.bfloat16
    s, t = lax.axis_index("seq"), lax.axis_index("tp")
    half, block = s // 8, lax.rem(s, 8)
    y, core = block // 2, lax.rem(block, 2)
    sib = half * 8 + y * 2 + (1 - core)
    up = half * 8 + lax.rem(y + 1, 4) * 2 + core
    down = half * 8 + lax.rem(y + 3, 4) * 2 + core
    partner = (1 - half) * 8 + block
    number = lax.axis_size("seq") * TP
    flat = s * TP + t
    after, before = lax.rem(flat + 1, number), lax.rem(flat + number - 1, number)
    after, before = (after // TP, lax.rem(after, TP)), (before // TP, lax.rem(before, TP))
    tok = r.fine.shape[0]
    crows = tok // SHORTEN
    group = crows * TP
    hid = r.gate_w.shape[0]

    loads = {}

    def load(name, src):
        loads[name] = pltpu.make_async_copy(src, getattr(r, name), r.local.at[len(loads)])
        loads[name].start()

    load("k_in", k_hbm)
    load("v_in", v_hbm)
    load("q_in", q_hbm)

    barrier = pltpu.get_barrier_semaphore()
    peers = [(s, lax.rem(t + off, TP)) for off in range(1, TP)]
    peers += [(half * 8 + lax.rem(block + off, 8), t) for off in range(1, 8)]
    peers += [(partner, lax.rem(t + off, TP)) for off in range(TP)] + [after, before]
    for peer in peers:
        pl.semaphore_signal(barrier, inc=1, device_id=peer, device_id_type=MESH)
    for ref, value in ((r.m_own, very_low), (r.l_own, 0.0), (r.acc_own, 0.0),
                       (r.m_far, very_low), (r.l_far, 0.0), (r.acc_far, 0.0)):
        ref[...] = jnp.full(ref.shape, value, f32)
    loads["v_in"].wait()
    for h in range(TP):
        r.vt_src[h] = r.v_in[:, h * HEAD : (h + 1) * HEAD].astype(f32).T.astype(bf16)
    loads["k_in"].wait()
    loads["q_in"].wait()
    pl.semaphore_wait(barrier, len(peers))

    used, sometimes = [], []

    def remote(src, dst, device, always=True):
        kind = len(used) + len(sometimes)
        cp = pltpu.make_async_remote_copy(
            src_ref=src, dst_ref=dst, send_sem=r.send.at[kind], recv_sem=r.recv.at[kind],
            device_id=device, device_id_type=MESH,
        )
        (used if always else sometimes).append(cp)
        return cp

    def go(copies):
        for cp in copies:
            cp.start()
        return copies

    def landed(copies):
        for cp in copies:
            cp.wait_recv()

    def to_group(src, dst):
        return go([
            remote(src(lax.rem(t + off, TP)), dst, (s, lax.rem(t + off, TP))) for off in range(1, TP)
        ])

    def aligned(index, size):
        return pl.ds(pl.multiple_of(index * size, size), size)

    def lanes(index):
        return aligned(index, HEAD)

    width = D // 8

    def fold_row(ref, value):
        for i in range(8):
            ref[i : i + 1, :] = value[:, i * width : (i + 1) * width]

    def flat_row(ref):
        return jnp.concatenate([ref[i : i + 1, :] for i in range(8)], axis=1)

    band = aligned(t, tok)
    k_copies = to_group(lambda peer: r.k_in.at[:, lanes(peer)], r.k_all.at[block, band, :])
    v_copies = to_group(lambda peer: r.vt_src.at[peer], r.vt_all.at[block, :, band])
    q_copies = to_group(lambda peer: r.q_in.at[:, lanes(peer)], r.q_own.at[band, :])
    own = go([
        pltpu.make_async_copy(r.q_in.at[:, lanes(t)], r.q_own.at[band, :], r.local.at[9]),
        pltpu.make_async_copy(r.k_in.at[:, lanes(t)], r.k_all.at[block, band, :], r.local.at[10]),
        pltpu.make_async_copy(r.vt_src.at[t], r.vt_all.at[block, :, band], r.local.at[11]),
    ])

    load("cot", cot_hbm)

    mine = aligned(t, crows)
    row = lax.broadcasted_iota(jnp.int32, (crows, tok), 0)
    col = lax.broadcasted_iota(jnp.int32, (crows, tok), 1)
    members = jnp.where((col >= row * SHORTEN) & (col < row * SHORTEN + SHORTEN), 1.0, 0.0).astype(bf16)
    loads["cot"].wait()
    r.coarse_grad[...] = jnp.dot(members, r.cot[...], preferred_element_type=f32)
    r.coarse_grad_b[...] = r.coarse_grad[...].astype(bf16)
    r.gg[mine, :] = r.coarse_grad_b[...]

    for cp in own:
        cp.wait()
    k_mine, v_mine = r.k_all.at[block], r.vt_all.at[block]
    landed(k_copies)
    k_ring = go([remote(k_mine, k_mine, (device, t)) for device in (up, down, sib)])
    landed(v_copies)
    v_ring = go([remote(v_mine, v_mine, (device, t)) for device in (down, up, sib)])
    landed(q_copies)
    q_over = remote(r.q_own, r.q_far, (partner, t), always=False)

    @pl.when(half == 1)
    def _():
        q_over.start()

    grad_gather = to_group(lambda peer: r.coarse_grad_b, r.gg.at[mine, :])
    load("out_w", out_hbm)
    load("fine", fine_hbm)
    load("down_w", down_hbm)
    load("gate_w", gate_hbm)
    load("up_w", up_hbm)

    def block_of(step):
        j = step // 2
        dy = j + (j // 2) * (5 - 2 * j)
        return lax.rem(y + dy, 4) * 2 + lax.rem(core + step, 2)

    def score(q_all, key_block, piece, slot):
        kk, u = piece
        st = lax.dot_general(
            r.k_all[key_block, kk * WIDE : (kk + 1) * WIDE], q_all[u * WIDE : (u + 1) * WIDE],
            contract_last, preferred_element_type=f32,
        )
        if slot is None:
            return st
        r.scores[slot] = st
        r.tops[slot] = jnp.max(st, axis=0, keepdims=True)

    def absorb(state, st, top, key_block, piece):
        m_all, l_all, acc_all = state
        kk, u = piece
        cols = slice(u * WIDE, (u + 1) * WIDE)
        older = m_all[:, cols]
        fresh = jnp.maximum(older, top)
        weights = jnp.exp2((st - fresh) * POWER)
        factor = jnp.exp2((older - fresh) * POWER)
        m_all[:, cols] = fresh
        l_all[:, cols] = l_all[:, cols] * factor + jnp.sum(weights, axis=0, keepdims=True)
        acc_all[:, cols] = acc_all[:, cols] * factor + jnp.dot(
            r.vt_all[key_block, :, kk * WIDE : (kk + 1) * WIDE], weights.astype(bf16),
            preferred_element_type=f32,
        )

    pieces = [(kk, u) for kk in range(2) for u in range(2)]

    def sweep(q_all, state, first, last, index):
        score(q_all, index(first), pieces[0], 0)

        @pl.loop(first, last)
        def _(step):
            here, then = index(step), index(jnp.minimum(step + 1, last - 1))
            for i, piece in enumerate(pieces):
                if i + 1 < len(pieces):
                    score(q_all, here, pieces[i + 1], (i + 1) % 2)
                else:
                    score(q_all, then, pieces[0], (i + 1) % 2)
                absorb(state, r.scores[i % 2], r.tops[i % 2], here, piece)

    own_state = (r.m_own, r.l_own, r.acc_own)
    far_state = (r.m_far, r.l_far, r.acc_far)

    def own_steps(first, last):
        @pl.loop(first, last)
        def _(step):
            @pl.when(block_of(step) < block)
            def _():
                sweep(r.q_own, own_state, step, step + 1, block_of)

    def arrived(first, last, later=False):
        @pl.when(half == 0)
        def _():
            sweep(r.q_far, far_state, first, last, block_of)

        if not later:
            own_steps(max(first, 1), last)

    for piece in ((0, 0), (0, 1), (1, 1)):
        st = score(r.q_own, block, piece, None)
        if piece[0] == piece[1]:
            key_pos = lax.broadcasted_iota(jnp.int32, st.shape, 0)
            query_pos = lax.broadcasted_iota(jnp.int32, st.shape, 1)
            st = jnp.where(key_pos <= query_pos, st, very_low)
        absorb(own_state, st, jnp.max(st, axis=0, keepdims=True), block, piece)

    def to_columns(rows_ref, gathered, sem):
        copies, kept = [], []
        for part in range(2):
            dst = gathered.at[aligned(y, group), part * 2 * HEAD : (part + 1) * 2 * HEAD]

            def columns(y_index):
                return rows_ref.at[:, aligned(part * 4 + y_index, 2 * HEAD)]

            for off in range(1, 4):
                peer = lax.rem(y + off, 4)
                copies.append(remote(columns(peer), dst, (half * 8 + peer * 2 + core, t)))
            kept.append(pltpu.make_async_copy(columns(y), dst, r.local.at[sem + part]))
        go(copies)
        for cp in go(kept):
            cp.wait()
        return copies

    landed([k_ring[2], v_ring[2]])

    @pl.when(half == 0)
    def _():
        q_over.wait_recv()

    arrived(0, 2)
    k_below, v_below = r.k_all.at[block_of(4)], r.vt_all.at[block_of(4)]
    k_above, v_above = r.k_all.at[block_of(2)], r.vt_all.at[block_of(2)]
    k_across, v_across = r.k_all.at[block_of(6)], r.vt_all.at[block_of(6)]
    landed(k_ring[:1])
    k_on = go([remote(k_below, k_below, (up, t)), remote(k_below, k_below, (sib, t))])
    landed(v_ring[:1])
    v_on = go([remote(v_above, v_above, (down, t)), remote(v_above, v_above, (sib, t))])
    landed(k_ring[1:2])
    k_on += go([remote(k_above, k_above, (sib, t))])
    landed(v_ring[1:2])
    v_on += go([remote(v_below, v_below, (sib, t))])
    arrived(2, 3)
    landed([k_on[2], v_on[1]])
    arrived(3, 4)
    landed([k_on[1], v_on[2]])
    landed(k_on[:1])
    k_last = go([remote(k_across, k_across, (sib, t))])
    landed(v_on[:1])
    v_last = go([remote(v_across, v_across, (sib, t))])
    arrived(4, 7, later=True)
    landed(k_last + v_last)
    arrived(7, 8, later=True)

    def normalized(state, out, stat):
        m_all, l_all, acc_all = state
        out[...] = (acc_all[...] / l_all[...]).astype(bf16)
        stat[0:1] = m_all[...]
        stat[1:2] = l_all[...]

    far_back = []
    for off in range(TP):
        peer = lax.rem(t + off, TP)
        far_back += [
            remote(r.o_far.at[:, lanes(peer)], r.far_in.at[t], (partner, peer), always=False),
            remote(r.stat_far.at[:, lanes(peer)], r.far_stat_in.at[t], (partner, peer), always=False),
        ]

    @pl.when(half == 0)
    def _():
        normalized(far_state, r.o_far, r.stat_far)
        go(far_back)
        r.far_in[...] = jnp.zeros(r.far_in.shape, bf16)
        r.far_stat_in[:, 0:1] = jnp.full((TP, 1, tok), very_low, f32)
        r.far_stat_in[:, 1:2] = jnp.zeros((TP, 1, tok), f32)

    own_steps(4, 8)
    normalized(own_state, r.o_own, r.stat_own)
    back = to_group(lambda peer: r.o_own.at[:, lanes(peer)], r.own_in.at[t])
    back += to_group(lambda peer: r.stat_own.at[:, lanes(peer)], r.own_stat_in.at[t])
    kept = go([
        pltpu.make_async_copy(r.o_own.at[:, lanes(t)], r.own_in.at[t], r.local.at[14]),
        pltpu.make_async_copy(r.stat_own.at[:, lanes(t)], r.own_stat_in.at[t], r.local.at[17]),
    ])
    landed(grad_gather)
    grad_columns = to_columns(r.gg, r.gg_all, 12)
    for cp in kept:
        cp.wait()
    loads["out_w"].wait()
    loads["fine"].wait()
    landed(back)

    @pl.when(half == 1)
    def _():
        landed(far_back)

    for h in range(TP):
        own_m, own_l = r.own_stat_in[h, 0:1], r.own_stat_in[h, 1:2]
        far_m, far_l = r.far_stat_in[h, 0:1], r.far_stat_in[h, 1:2]
        top = jnp.maximum(own_m, far_m)
        own_l = own_l * jnp.exp2((own_m - top) * POWER)
        far_l = far_l * jnp.exp2((far_m - top) * POWER)
        total = own_l + far_l
        r.att[h * HEAD : (h + 1) * HEAD] = (
            r.own_in[h].astype(f32) * (own_l / total) + r.far_in[h].astype(f32) * (far_l / total)
        ).astype(bf16)
    projected = lax.dot_general(r.att[...], r.out_w[...], contract_first, preferred_element_type=f32)
    r.stream[...] = (r.fine[...].astype(f32) + projected).astype(bf16)
    row = lax.broadcasted_iota(jnp.int32, (crows + 8, tok), 0)
    col = lax.broadcasted_iota(jnp.int32, (crows + 8, tok), 1)
    window = jnp.where((col >= row * SHORTEN - (SHORTEN - 1)) & (col <= row * SHORTEN), 1.0, 0.0)
    coarse = jnp.dot(window.astype(bf16), r.stream[...], preferred_element_type=f32)
    fold_row(r.border_out, coarse[crows : crows + 1])
    border_copy = remote(r.border_out, r.border_in, after)
    border_copy.start()
    border_copy.wait_recv()
    edge = jnp.where(flat > 0, flat_row(r.border_in), 0.0)
    first = lax.broadcasted_iota(jnp.int32, (crows, D), 0) == 0
    coarse = coarse[:crows] + jnp.where(first, edge, 0.0)
    coarse = coarse / SHORTEN
    rstd = lax.rsqrt(jnp.mean(coarse * coarse, axis=-1, keepdims=True) + 1e-05)
    base = coarse * rstd
    r.coarse_b[...] = (base * gain_ref[...]).astype(bf16)
    r.ng[mine, :] = r.coarse_b[...]
    norm_gather = to_group(lambda peer: r.coarse_b, r.ng.at[mine, :])

    loads["down_w"].wait()
    r.hidden_grad[...] = lax.dot_general(
        r.gg[...], r.down_w[...], contract_last, preferred_element_type=f32
    )
    loads["gate_w"].wait()
    loads["up_w"].wait()

    landed(norm_gather)
    norm_columns = to_columns(r.ng, r.ng_all, 15)
    gate = lax.dot_general(r.ng[...], r.gate_w[...], contract_last, preferred_element_type=f32)
    up_v = lax.dot_general(r.ng[...], r.up_w[...], contract_last, preferred_element_type=f32)
    sig = jax.nn.sigmoid(gate)
    act = gate * sig
    above, below, across = (lax.rem(y + dy, 4) for dy in (1, 3, 2))
    cut = group // 2
    parts = (pl.ds(0, cut), pl.ds(cut, cut))

    def ring(i, source, piece, device):
        ref = r.hgu.at[i, source, parts[piece], :]
        return remote(ref, ref, (device, t))

    def around(i):
        return (
            go([ring(i, y, 0, up), ring(i, y, 1, up)]),
            go([ring(i, y, 1, down), ring(i, y, 0, down)]),
        )

    rings = []
    r.hgu[0, y] = (act * up_v).astype(bf16)
    rings.append(around(0))
    r.hgu[1, y] = (
        r.hidden_grad[...] * up_v * sig * (1.0 + gate * (1.0 - sig))
    ).astype(bf16)
    rings.append(around(1))
    r.hgu[2, y] = (r.hidden_grad[...] * act).astype(bf16)
    rings.append(around(2))

    part = jnp.dot(r.hgu[0, y], r.down_w[...], preferred_element_type=f32)
    r.down_out[...] = part.astype(bf16).reshape(r.down_out.shape)
    r.down_in[t] = r.down_out[t]
    down_sum = to_group(lambda peer: r.down_out.at[peer], r.down_in.at[t])
    part = jnp.dot(r.hgu[1, y], r.gate_w[...], preferred_element_type=f32) + jnp.dot(
        r.hgu[2, y], r.up_w[...], preferred_element_type=f32
    )
    r.norm_out[...] = part.astype(bf16).reshape(r.norm_out.shape)
    r.norm_in[t] = r.norm_out[t]
    norm_sum = to_group(lambda peer: r.norm_out.at[peer], r.norm_in.at[t])

    def pass_on(i):
        ring_up, ring_down = rings[i]
        landed(ring_up[:1])
        first = go([ring(i, below, 0, up)])
        landed(ring_down[:1])
        return first + go([ring(i, above, 1, down)])

    on = [pass_on(0)]

    landed(down_sum)
    coarse_out = coarse + jnp.sum(r.down_in[...].astype(f32), axis=0)
    spread = (crows, SHORTEN, D)
    section_ref[...] = (
        (r.stream[...].astype(f32).reshape(spread) + coarse_out[:, None, :])
        .reshape(tok, D)
        .astype(bf16)
    )
    on.append(pass_on(1))

    landed(norm_sum)
    normed_grad = jnp.sum(r.norm_in[...].astype(f32), axis=0)
    scaled = normed_grad * gain_ref[...]
    coarse_total = r.coarse_grad[...] + rstd * (
        scaled - base * jnp.mean(scaled * base, axis=-1, keepdims=True)
    )
    fold_row(r.follow_out, coarse_total[0:1])
    follow = remote(r.follow_out, r.follow_in, before)
    follow.start()
    fold_row(r.gain_out, jnp.sum(normed_grad * base, axis=0, keepdims=True))
    r.gain_in[t] = r.gain_out[...]
    gain_sum = to_group(lambda peer: r.gain_out, r.gain_in.at[t])

    on.append(pass_on(2))

    outs = (down_grad_ref, gate_grad_ref, up_grad_ref)

    def term(i):
        landed(rings[i][0][1:] + rings[i][1][1:] + on[i])
        right = r.gg_all if i == 0 else r.ng_all
        left = r.hgu[i].reshape(4 * group, hid)
        r.term[i] = lax.dot_general(left, right[...], contract_first, preferred_element_type=f32)
        for p in range(2):
            r.sib_out[i, p] = r.term[i, :, lanes(2 * p + 1 - core)].astype(bf16)
        return go([remote(r.sib_out.at[i], r.sib_in.at[i], (sib, t))])

    def join(i):
        landed(to_sib[i : i + 1])
        r.term_out[i] = (
            r.term[i, :, lanes(2 * (1 - half) + core)] + r.sib_in[i, 1 - half].astype(f32)
        ).astype(bf16)
        copies = go([remote(r.term_out.at[i], r.term_in.at[i], (partner, t))])
        outs[i][...] = r.term[i, :, lanes(2 * half + core)] + r.sib_in[i, half].astype(f32)
        return copies

    landed(grad_columns)
    to_sib = term(0)

    landed(gain_sum)
    r.gain_mid[...] = jnp.sum(r.gain_in[...], axis=0)
    r.gain_half[block] = r.gain_mid[...]
    gain_group = go([
        remote(r.gain_mid, r.gain_half.at[block], (half * 8 + lax.rem(block + off, 8), t))
        for off in range(1, 8)
    ])
    landed(norm_columns)
    to_sib += term(1)
    terms = join(0)

    follow.wait_recv()
    following = jnp.where(flat < number - 1, flat_row(r.follow_in), 0.0)
    ahead = jnp.concatenate([coarse_total[1:], following], axis=0)
    place = lax.broadcasted_iota(jnp.int32, spread, 1)
    contrib = jnp.where(place == 0, coarse_total[:, None, :], ahead[:, None, :])
    stream_grad_ref[...] = (
        (r.cot[...].astype(f32).reshape(spread) + contrib / SHORTEN).reshape(tok, D).astype(bf16)
    )

    to_sib += term(2)
    terms += join(1)
    landed(gain_group)
    r.gain_far_out[...] = jnp.sum(r.gain_half[...], axis=0)
    gain_far = remote(r.gain_far_out, r.gain_far_in, (partner, t))
    gain_far.start()
    terms += join(2)
    gain_far.wait_recv()
    gain_grad_ref[...] = flat_row(r.gain_far_out) + flat_row(r.gain_far_in)
    for i in range(3):
        terms[i].wait_recv()
        outs[i][...] = outs[i][...] + r.term_in[i].astype(f32)

    for cp in used:
        cp.wait_send()

    @pl.when(half == 1)
    def _():
        q_over.wait_send()

    @pl.when(half == 0)
    def _():
        for cp in far_back:
            cp.wait_send()


def hand_over_kernel(*refs):
    count = (len(refs) - 2) // 3
    ins, outs, held = refs[:count], refs[count : 2 * count], refs[2 * count : 3 * count]
    arrive, leave = refs[-2:]
    first = [pltpu.make_async_copy(a, b, arrive.at[i]) for i, (a, b) in enumerate(zip(ins, held))]
    second = [pltpu.make_async_copy(a, b, leave.at[i]) for i, (a, b) in enumerate(zip(held, outs))]
    for cp in first:
        cp.start()
    for one, two in zip(first, second):
        one.wait()
        two.start()
    for cp in second:
        cp.wait()


def on_device(
    fine_stream,
    queries,
    keys,
    values,
    out_weight,
    norm_gain,
    gate_weight,
    up_weight,
    down_weight,
    cotangent,
):
    tok = fine_stream.shape[0]
    hid = gate_weight.shape[1]
    seq = lax.axis_size("seq")
    f32, bf16 = jnp.float32, jnp.bfloat16
    vmem, hbm = pl.BlockSpec(memory_space=pltpu.VMEM), pl.BlockSpec(memory_space=pltpu.HBM)
    scratch = scratch_of(tok, hid, seq)
    shapes = (
        jax.ShapeDtypeStruct((tok, D), bf16),
        jax.ShapeDtypeStruct((tok, D), bf16),
        jax.ShapeDtypeStruct((hid, D // seq), f32),
        jax.ShapeDtypeStruct((hid, D // seq), f32),
        jax.ShapeDtypeStruct((hid, D // seq), f32),
        jax.ShapeDtypeStruct((1, D), f32),
    )
    outs = pl.pallas_call(
        lambda *refs: section_kernel(tuple(scratch), *refs),
        out_shape=shapes,
        in_specs=[hbm] * 5 + [vmem] + [hbm] * 4,
        out_specs=(vmem,) * 6,
        scratch_shapes=list(scratch.values()),
        compiler_params=pltpu.CompilerParams(
            collective_id=0, has_side_effects=True, vmem_limit_bytes=60 * 1024 * 1024
        ),
        name="section",
    )(
        queries, keys, values, fine_stream, cotangent, norm_gain.reshape(1, D),
        out_weight, gate_weight.T, up_weight.T, down_weight,
    )
    section_out, stream_grad, gate_grad, up_grad, down_grad, gain_grad = pl.pallas_call(
        hand_over_kernel,
        out_shape=shapes,
        in_specs=[hbm] * 6,
        out_specs=(hbm,) * 6,
        scratch_shapes=[pltpu.VMEM(shape.shape, shape.dtype) for shape in shapes]
        + [pltpu.SemaphoreType.DMA((6,)), pltpu.SemaphoreType.DMA((6,))],
        compiler_params=pltpu.CompilerParams(vmem_limit_bytes=60 * 1024 * 1024),
        name="hand_over",
    )(*outs)
    return (section_out, stream_grad, gate_grad.T, up_grad.T, down_grad, gain_grad.reshape(D))


def solution(mesh):
    return jax.shard_map(
        on_device,
        mesh=mesh,
        in_specs=(
            P(("seq", "tp"), None),
            P(("seq", "tp"), None),
            P(("seq", "tp"), None),
            P(("seq", "tp"), None),
            P(),
            P(),
            P(None, "tp"),
            P(None, "tp"),
            P("tp", None),
            P(("seq", "tp"), None),
        ),
        out_specs=(
            P(("seq", "tp"), None),
            P(("seq", "tp"), None),
            P("seq", "tp"),
            P("seq", "tp"),
            P("tp", "seq"),
            P(),
        ),
        check_vma=False,
    )
```

```python
import math

import jax
import jax.numpy as jnp
from jax import lax
from jax.experimental import pallas as pl
from jax.experimental.pallas import tpu as pltpu
from jax.sharding import PartitionSpec as P

D = 2048
HEAD = 128
SHORTEN = 8
MESH = pl.DeviceIdType.MESH
TP = 8
WIDE = 512
COPIES = 200

contract_last = (((1,), (1,)), ((), ()))
contract_first = (((0,), (0,)), ((), ()))
very_low = -1e30
POWER = math.log2(math.e) * HEAD ** (-0.5)


def scratch_of(tok, hid, seq):
    crows, group, rows = tok // SHORTEN, tok // SHORTEN * TP, tok * TP
    f32, bf16 = jnp.float32, jnp.bfloat16
    vmem = pltpu.VMEM
    small = (8, D // 8)
    return {
        "q_in": vmem((tok, TP * HEAD), bf16),
        "k_in": vmem((tok, TP * HEAD), bf16),
        "v_in": vmem((tok, TP * HEAD), bf16),
        "fine": vmem((tok, D), bf16),
        "cot": vmem((tok, D), bf16),
        "out_w": vmem((TP * HEAD, D), bf16),
        "gate_w": vmem((hid, D), bf16),
        "up_w": vmem((hid, D), bf16),
        "down_w": vmem((hid, D), bf16),
        "vt_src": vmem((TP, HEAD, tok), bf16),
        "q_own": vmem((rows, HEAD), bf16),
        "q_far": vmem((rows, HEAD), bf16),
        "k_all": vmem((8, rows, HEAD), bf16),
        "vt_all": vmem((8, HEAD, rows), bf16),
        "scores": vmem((2, WIDE, WIDE), f32),
        "tops": vmem((2, 1, WIDE), f32),
        "m_own": vmem((1, rows), f32),
        "l_own": vmem((1, rows), f32),
        "acc_own": vmem((HEAD, rows), f32),
        "m_far": vmem((1, rows), f32),
        "l_far": vmem((1, rows), f32),
        "acc_far": vmem((HEAD, rows), f32),
        "o_own": vmem((HEAD, rows), bf16),
        "o_far": vmem((HEAD, rows), bf16),
        "stat_own": vmem((8, rows), f32),
        "stat_far": vmem((8, rows), f32),
        "own_in": vmem((TP, HEAD, tok), bf16),
        "far_in": vmem((TP, HEAD, tok), bf16),
        "own_stat_in": vmem((TP, 8, tok), f32),
        "far_stat_in": vmem((TP, 8, tok), f32),
        "att": vmem((TP * HEAD, tok), bf16),
        "stream": vmem((tok, D), bf16),
        "edge_out": vmem(small, f32),
        "edge_in": vmem(small, f32),
        "fine_rows": vmem((crows, D), f32),
        "fine_pool": vmem((crows, D), bf16),
        "fine_all": vmem((group, D), bf16),
        "pool_out": vmem((crows, TP * HEAD), bf16),
        "pool_all": vmem((TP, crows, TP * HEAD), bf16),
        "rim_out": vmem((TP, HEAD), f32),
        "rim_in": vmem((TP, TP, HEAD), f32),
        "rim_prev": vmem((TP, HEAD), f32),
        "coarse_all": vmem((group, D), f32),
        "coarse_grad": vmem((crows, D), f32),
        "coarse_grad_b": vmem((crows, D), bf16),
        "ng": vmem((group, D), bf16),
        "gg": vmem((group, D), bf16),
        "hidden_grad": vmem((group, hid), f32),
        "ng_all": vmem((4 * group, 4 * HEAD), bf16),
        "gg_all": vmem((4 * group, 4 * HEAD), bf16),
        "hgu": vmem((3, 4, group, hid), bf16),
        "down_out": vmem((TP, crows, D), bf16),
        "down_in": vmem((TP, crows, D), bf16),
        "norm_out": vmem((TP, crows, D), bf16),
        "norm_in": vmem((TP, crows, D), bf16),
        "follow_out": vmem(small, f32),
        "follow_in": vmem(small, f32),
        "gain_out": vmem(small, f32),
        "gain_in": vmem((TP,) + small, f32),
        "gain_mid": vmem(small, f32),
        "gain_half": vmem((8,) + small, f32),
        "gain_far_out": vmem(small, f32),
        "gain_far_in": vmem(small, f32),
        "term": vmem((3, hid, 4 * HEAD), f32),
        "sib_out": vmem((3, 2, hid, HEAD), bf16),
        "sib_in": vmem((3, 2, hid, HEAD), bf16),
        "term_out": vmem((3, hid, HEAD), bf16),
        "term_in": vmem((3, hid, HEAD), bf16),
        "send": pltpu.SemaphoreType.DMA((COPIES,)),
        "recv": pltpu.SemaphoreType.DMA((COPIES,)),
        "local": pltpu.SemaphoreType.DMA((20,)),
    }


class Space:
    pass


def section_kernel(
    names, q_hbm, k_hbm, v_hbm, fine_hbm, cot_hbm, gain_ref, out_hbm, gate_hbm, up_hbm, down_hbm,
    section_ref, stream_grad_ref, gate_grad_ref, up_grad_ref, down_grad_ref, gain_grad_ref, *scratch,
):
    r = Space()
    for name, ref in zip(names, scratch):
        setattr(r, name, ref)
    f32, bf16 = jnp.float32, jnp.bfloat16
    s, t = lax.axis_index("seq"), lax.axis_index("tp")
    half, block = s // 8, lax.rem(s, 8)
    y, core = block // 2, lax.rem(block, 2)
    sib = half * 8 + y * 2 + (1 - core)
    up = half * 8 + lax.rem(y + 1, 4) * 2 + core
    down = half * 8 + lax.rem(y + 3, 4) * 2 + core
    partner = (1 - half) * 8 + block
    number = lax.axis_size("seq") * TP
    flat = s * TP + t
    after, before = lax.rem(flat + 1, number), lax.rem(flat + number - 1, number)
    after, before = (after // TP, lax.rem(after, TP)), (before // TP, lax.rem(before, TP))
    tok = r.fine.shape[0]
    crows = tok // SHORTEN
    group = crows * TP
    hid = r.gate_w.shape[0]

    loads = {}

    def load(name, src):
        loads[name] = pltpu.make_async_copy(src, getattr(r, name), r.local.at[len(loads)])
        loads[name].start()

    load("k_in", k_hbm)
    load("v_in", v_hbm)
    load("q_in", q_hbm)

    barrier = pltpu.get_barrier_semaphore()
    peers = [(s, lax.rem(t + off, TP)) for off in range(1, TP)]
    peers += [(half * 8 + lax.rem(block + off, 8), t) for off in range(1, 8)]
    peers += [(partner, lax.rem(t + off, TP)) for off in range(TP)] + [after, before]
    for peer in peers + [(lax.rem(s + 15, 16), TP - 1)]:
        pl.semaphore_signal(barrier, inc=1, device_id=peer, device_id_type=MESH)
    for ref, value in ((r.m_own, very_low), (r.l_own, 0.0), (r.acc_own, 0.0),
                       (r.m_far, very_low), (r.l_far, 0.0), (r.acc_far, 0.0)):
        ref[...] = jnp.full(ref.shape, value, f32)
    loads["v_in"].wait()
    for h in range(TP):
        r.vt_src[h] = r.v_in[:, h * HEAD : (h + 1) * HEAD].astype(f32).T.astype(bf16)
    loads["k_in"].wait()
    loads["q_in"].wait()
    pl.semaphore_wait(barrier, len(peers) + TP * (t // (TP - 1)))

    used, sometimes = [], []

    def remote(src, dst, device, always=True, arrival=None):
        kind = len(used) + len(sometimes)
        arrival = kind if arrival is None else arrival
        cp = pltpu.make_async_remote_copy(
            src_ref=src, dst_ref=dst, send_sem=r.send.at[kind], recv_sem=r.recv.at[arrival],
            device_id=device, device_id_type=MESH,
        )
        (used if always else sometimes).append(cp)
        return cp

    def go(copies):
        for cp in copies:
            cp.start()
        return copies

    def landed(copies):
        for cp in copies:
            cp.wait_recv()

    def to_group(src, dst):
        return go([
            remote(src(lax.rem(t + off, TP)), dst, (s, lax.rem(t + off, TP))) for off in range(1, TP)
        ])

    def aligned(index, size):
        return pl.ds(pl.multiple_of(index * size, size), size)

    def lanes(index):
        return aligned(index, HEAD)

    width = D // 8

    def fold_row(ref, value):
        for i in range(8):
            ref[i : i + 1, :] = value[:, i * width : (i + 1) * width]

    def flat_row(ref):
        return jnp.concatenate([ref[i : i + 1, :] for i in range(8)], axis=1)

    band = aligned(t, tok)
    k_copies = to_group(lambda peer: r.k_in.at[:, lanes(peer)], r.k_all.at[block, band, :])
    v_copies = to_group(lambda peer: r.vt_src.at[peer], r.vt_all.at[block, :, band])
    q_copies = to_group(lambda peer: r.q_in.at[:, lanes(peer)], r.q_own.at[band, :])
    own = go([
        pltpu.make_async_copy(r.q_in.at[:, lanes(t)], r.q_own.at[band, :], r.local.at[9]),
        pltpu.make_async_copy(r.k_in.at[:, lanes(t)], r.k_all.at[block, band, :], r.local.at[10]),
        pltpu.make_async_copy(r.vt_src.at[t], r.vt_all.at[block, :, band], r.local.at[11]),
    ])

    load("cot", cot_hbm)
    load("fine", fine_hbm)

    mine = aligned(t, crows)
    row = lax.broadcasted_iota(jnp.int32, (crows, tok), 0)
    col = lax.broadcasted_iota(jnp.int32, (crows, tok), 1)
    members = jnp.where((col >= row * SHORTEN) & (col < row * SHORTEN + SHORTEN), 1.0, 0.0).astype(bf16)
    loads["cot"].wait()
    r.coarse_grad[...] = jnp.dot(members, r.cot[...], preferred_element_type=f32)
    r.coarse_grad_b[...] = r.coarse_grad[...].astype(bf16)
    r.gg[mine, :] = r.coarse_grad_b[...]

    for cp in own:
        cp.wait()
    k_mine, v_mine = r.k_all.at[block], r.vt_all.at[block]
    landed(k_copies)
    k_ring = go([remote(k_mine, k_mine, (device, t)) for device in (up, down, sib)])
    landed(v_copies)
    v_ring = go([remote(v_mine, v_mine, (device, t)) for device in (down, up, sib)])
    landed(q_copies)
    q_over = remote(r.q_own, r.q_far, (partner, t), always=False)

    @pl.when(half == 1)
    def _():
        q_over.start()

    grad_gather = to_group(lambda peer: r.coarse_grad_b, r.gg.at[mine, :])
    load("out_w", out_hbm)
    load("down_w", down_hbm)
    load("gate_w", gate_hbm)
    load("up_w", up_hbm)

    row = lax.broadcasted_iota(jnp.int32, (crows + 8, tok), 0)
    col = lax.broadcasted_iota(jnp.int32, (crows + 8, tok), 1)
    window = jnp.where((col >= row * SHORTEN - (SHORTEN - 1)) & (col <= row * SHORTEN), 1.0, 0.0)
    window = window.astype(bf16)
    first_row = lax.broadcasted_iota(jnp.int32, (crows, 1), 0) == 0
    loads["fine"].wait()
    pooled = jnp.dot(window, r.fine[...], preferred_element_type=f32)
    r.fine_rows[...] = pooled[:crows]
    fold_row(r.edge_out, pooled[crows : crows + 1])
    edge_copy = remote(r.edge_out, r.edge_in, after)
    edge_copy.start()

    def block_of(step):
        j = step // 2
        dy = j + (j // 2) * (5 - 2 * j)
        return lax.rem(y + dy, 4) * 2 + lax.rem(core + step, 2)

    def score(q_all, key_block, piece, slot):
        kk, u = piece
        st = lax.dot_general(
            r.k_all[key_block, kk * WIDE : (kk + 1) * WIDE], q_all[u * WIDE : (u + 1) * WIDE],
            contract_last, preferred_element_type=f32,
        )
        if slot is None:
            return st
        r.scores[slot] = st
        r.tops[slot] = jnp.max(st, axis=0, keepdims=True)

    def absorb(state, st, top, key_block, piece):
        m_all, l_all, acc_all = state
        kk, u = piece
        cols = slice(u * WIDE, (u + 1) * WIDE)
        older = m_all[:, cols]
        fresh = jnp.maximum(older, top)
        weights = jnp.exp2((st - fresh) * POWER)
        factor = jnp.exp2((older - fresh) * POWER)
        m_all[:, cols] = fresh
        l_all[:, cols] = l_all[:, cols] * factor + jnp.sum(weights, axis=0, keepdims=True)
        acc_all[:, cols] = acc_all[:, cols] * factor + jnp.dot(
            r.vt_all[key_block, :, kk * WIDE : (kk + 1) * WIDE], weights.astype(bf16),
            preferred_element_type=f32,
        )

    pieces = [(kk, u) for kk in range(2) for u in range(2)]

    def sweep(q_all, state, first, last, index):
        score(q_all, index(first), pieces[0], 0)

        @pl.loop(first, last)
        def _(step):
            here, then = index(step), index(jnp.minimum(step + 1, last - 1))
            for i, piece in enumerate(pieces):
                if i + 1 < len(pieces):
                    score(q_all, here, pieces[i + 1], (i + 1) % 2)
                else:
                    score(q_all, then, pieces[0], (i + 1) % 2)
                absorb(state, r.scores[i % 2], r.tops[i % 2], here, piece)

    own_state = (r.m_own, r.l_own, r.acc_own)
    far_state = (r.m_far, r.l_far, r.acc_far)

    def own_steps(first, last):
        @pl.loop(first, last)
        def _(step):
            @pl.when(block_of(step) < block)
            def _():
                sweep(r.q_own, own_state, step, step + 1, block_of)

    def arrived(first, last, later=False):
        @pl.when(half == 0)
        def _():
            sweep(r.q_far, far_state, first, last, block_of)

        if not later:
            own_steps(max(first, 1), last)

    for piece in ((0, 0), (0, 1), (1, 1)):
        st = score(r.q_own, block, piece, None)
        if piece[0] == piece[1]:
            key_pos = lax.broadcasted_iota(jnp.int32, st.shape, 0)
            query_pos = lax.broadcasted_iota(jnp.int32, st.shape, 1)
            st = jnp.where(key_pos <= query_pos, st, very_low)
        absorb(own_state, st, jnp.max(st, axis=0, keepdims=True), block, piece)

    def to_columns(rows_ref, gathered, sem):
        copies, kept = [], []
        for part in range(2):
            dst = gathered.at[aligned(y, group), part * 2 * HEAD : (part + 1) * 2 * HEAD]

            def columns(y_index):
                return rows_ref.at[:, aligned(part * 4 + y_index, 2 * HEAD)]

            for off in range(1, 4):
                peer = lax.rem(y + off, 4)
                copies.append(remote(columns(peer), dst, (half * 8 + peer * 2 + core, t)))
            kept.append(pltpu.make_async_copy(columns(y), dst, r.local.at[sem + part]))
        go(copies)
        for cp in go(kept):
            cp.wait()
        return copies

    landed([k_ring[2], v_ring[2]])

    @pl.when(half == 0)
    def _():
        q_over.wait_recv()

    arrived(0, 2)
    k_below, v_below = r.k_all.at[block_of(4)], r.vt_all.at[block_of(4)]
    k_above, v_above = r.k_all.at[block_of(2)], r.vt_all.at[block_of(2)]
    k_across, v_across = r.k_all.at[block_of(6)], r.vt_all.at[block_of(6)]
    landed(k_ring[:1])
    k_on = go([remote(k_below, k_below, (up, t)), remote(k_below, k_below, (sib, t))])
    landed(v_ring[:1])
    v_on = go([remote(v_above, v_above, (down, t)), remote(v_above, v_above, (sib, t))])
    landed(k_ring[1:2])
    k_on += go([remote(k_above, k_above, (sib, t))])
    landed(v_ring[1:2])
    v_on += go([remote(v_below, v_below, (sib, t))])
    arrived(2, 3)
    landed([k_on[2], v_on[1]])
    arrived(3, 4)
    landed([k_on[1], v_on[2]])
    landed(k_on[:1])
    k_last = go([remote(k_across, k_across, (sib, t))])
    landed(v_on[:1])
    v_last = go([remote(v_across, v_across, (sib, t))])
    arrived(4, 7, later=True)
    edge_copy.wait_recv()
    edge = jnp.where(flat > 0, flat_row(r.edge_in), 0.0)
    r.fine_pool[...] = (r.fine_rows[...] + jnp.where(first_row, edge, 0.0)).astype(bf16)
    r.fine_all[mine, :] = r.fine_pool[...]
    fine_gather = to_group(lambda peer: r.fine_pool, r.fine_all.at[mine, :])
    landed(k_last + v_last)
    arrived(7, 8, later=True)

    def normalized(state, out, stat):
        m_all, l_all, acc_all = state
        out[...] = (acc_all[...] / l_all[...]).astype(bf16)
        stat[0:1] = m_all[...]
        stat[1:2] = l_all[...]

    far_back = []
    for off in range(TP):
        peer = lax.rem(t + off, TP)
        far_back += [
            remote(r.o_far.at[:, lanes(peer)], r.far_in.at[t], (partner, peer), always=False),
            remote(r.stat_far.at[:, lanes(peer)], r.far_stat_in.at[t], (partner, peer), always=False),
        ]

    @pl.when(half == 0)
    def _():
        normalized(far_state, r.o_far, r.stat_far)
        go(far_back)
        r.far_in[...] = jnp.zeros(r.far_in.shape, bf16)
        r.far_stat_in[:, 0:1] = jnp.full((TP, 1, tok), very_low, f32)
        r.far_stat_in[:, 1:2] = jnp.zeros((TP, 1, tok), f32)

    own_steps(4, 8)
    normalized(own_state, r.o_own, r.stat_own)
    back = to_group(lambda peer: r.o_own.at[:, lanes(peer)], r.own_in.at[t])
    back += to_group(lambda peer: r.stat_own.at[:, lanes(peer)], r.own_stat_in.at[t])
    kept = go([
        pltpu.make_async_copy(r.o_own.at[:, lanes(t)], r.own_in.at[t], r.local.at[14]),
        pltpu.make_async_copy(r.stat_own.at[:, lanes(t)], r.own_stat_in.at[t], r.local.at[17]),
    ])
    landed(grad_gather)
    grad_columns = to_columns(r.gg, r.gg_all, 12)
    for cp in kept:
        cp.wait()
    loads["out_w"].wait()
    landed(back)

    @pl.when(half == 1)
    def _():
        landed(far_back)

    for h in range(TP):
        own_m, own_l = r.own_stat_in[h, 0:1], r.own_stat_in[h, 1:2]
        far_m, far_l = r.far_stat_in[h, 0:1], r.far_stat_in[h, 1:2]
        top = jnp.maximum(own_m, far_m)
        own_l = own_l * jnp.exp2((own_m - top) * POWER)
        far_l = far_l * jnp.exp2((far_m - top) * POWER)
        total = own_l + far_l
        r.att[h * HEAD : (h + 1) * HEAD] = (
            r.own_in[h].astype(f32) * (own_l / total) + r.far_in[h].astype(f32) * (far_l / total)
        ).astype(bf16)
    pooled = lax.dot_general(window, r.att[...], contract_last, preferred_element_type=f32)
    r.pool_out[...] = pooled[:crows].astype(bf16)
    r.pool_all[t] = r.pool_out[...]
    for i in range(TP):
        r.rim_out[i : i + 1, :] = pooled[crows : crows + 1, i * HEAD : (i + 1) * HEAD]
    r.rim_in[t] = r.rim_out[...]
    pool_gather = to_group(lambda peer: r.pool_out, r.pool_all.at[t])
    pool_gather += to_group(lambda peer: r.rim_out, r.rim_in.at[t])
    rim_kind = len(used) + len(sometimes)
    rim_next = [
        remote(r.rim_out, r.rim_prev, (lax.rem(s + 1, 16), lax.rem(t + off, TP)), always=False,
               arrival=rim_kind)
        for off in range(TP)
    ]

    @pl.when(t == TP - 1)
    def _():
        go(rim_next)

    loads["down_w"].wait()
    r.hidden_grad[...] = lax.dot_general(
        r.gg[...], r.down_w[...], contract_last, preferred_element_type=f32
    )
    loads["gate_w"].wait()
    loads["up_w"].wait()
    landed(fine_gather + pool_gather + rim_next[:1])
    for i in range(TP):
        source = r.rim_prev if i == 0 else r.rim_in.at[i - 1]
        rim = jnp.concatenate([source[h : h + 1, :] for h in range(TP)], axis=1)
        if i == 0:
            rim = jnp.where(s > 0, rim, 0.0)
        r.pool_all[i] = (r.pool_all[i].astype(f32) + jnp.where(first_row, rim, 0.0)).astype(bf16)
    coarse_all = jnp.dot(
        r.pool_all[...].reshape(group, TP * HEAD), r.out_w[...], preferred_element_type=f32
    )
    coarse_all = (coarse_all + r.fine_all[...].astype(f32)) / SHORTEN
    r.coarse_all[...] = coarse_all
    rstd_all = lax.rsqrt(jnp.mean(coarse_all * coarse_all, axis=-1, keepdims=True) + 1e-05)
    r.ng[...] = (coarse_all * rstd_all * gain_ref[...]).astype(bf16)
    coarse = r.coarse_all[mine, :]
    rstd = lax.rsqrt(jnp.mean(coarse * coarse, axis=-1, keepdims=True) + 1e-05)
    base = coarse * rstd

    norm_columns = to_columns(r.ng, r.ng_all, 15)
    gate = lax.dot_general(r.ng[...], r.gate_w[...], contract_last, preferred_element_type=f32)
    up_v = lax.dot_general(r.ng[...], r.up_w[...], contract_last, preferred_element_type=f32)
    sig = jax.nn.sigmoid(gate)
    act = gate * sig
    above, below, across = (lax.rem(y + dy, 4) for dy in (1, 3, 2))
    cut = group // 2
    parts = (pl.ds(0, cut), pl.ds(cut, cut))

    def ring(i, source, piece, device):
        ref = r.hgu.at[i, source, parts[piece], :]
        return remote(ref, ref, (device, t))

    def around(i):
        return (
            go([ring(i, y, 0, up), ring(i, y, 1, up)]),
            go([ring(i, y, 1, down), ring(i, y, 0, down)]),
        )

    rings = []
    r.hgu[0, y] = (act * up_v).astype(bf16)
    rings.append(around(0))
    r.hgu[1, y] = (
        r.hidden_grad[...] * up_v * sig * (1.0 + gate * (1.0 - sig))
    ).astype(bf16)
    rings.append(around(1))
    r.hgu[2, y] = (r.hidden_grad[...] * act).astype(bf16)
    rings.append(around(2))

    part = jnp.dot(r.hgu[0, y], r.down_w[...], preferred_element_type=f32)
    r.down_out[...] = part.astype(bf16).reshape(r.down_out.shape)
    r.down_in[t] = r.down_out[t]
    down_sum = to_group(lambda peer: r.down_out.at[peer], r.down_in.at[t])
    part = jnp.dot(r.hgu[1, y], r.gate_w[...], preferred_element_type=f32) + jnp.dot(
        r.hgu[2, y], r.up_w[...], preferred_element_type=f32
    )
    r.norm_out[...] = part.astype(bf16).reshape(r.norm_out.shape)
    r.norm_in[t] = r.norm_out[t]
    norm_sum = to_group(lambda peer: r.norm_out.at[peer], r.norm_in.at[t])
    fold_row(r.gain_out, jnp.sum(part * (r.coarse_all[...] * rstd_all), axis=0, keepdims=True))
    r.gain_in[t] = r.gain_out[...]
    gain_sum = to_group(lambda peer: r.gain_out, r.gain_in.at[t])

    projected = lax.dot_general(r.att[...], r.out_w[...], contract_first, preferred_element_type=f32)
    r.stream[...] = (r.fine[...].astype(f32) + projected).astype(bf16)

    def pass_on(i):
        ring_up, ring_down = rings[i]
        landed(ring_up[:1])
        first = go([ring(i, below, 0, up)])
        landed(ring_down[:1])
        return first + go([ring(i, above, 1, down)])

    on = [pass_on(0)]

    landed(gain_sum)
    r.gain_mid[...] = jnp.sum(r.gain_in[...], axis=0)
    r.gain_half[block] = r.gain_mid[...]
    gain_group = go([
        remote(r.gain_mid, r.gain_half.at[block], (half * 8 + lax.rem(block + off, 8), t))
        for off in range(1, 8)
    ])

    landed(down_sum)
    coarse_out = coarse + jnp.sum(r.down_in[...].astype(f32), axis=0)
    spread = (crows, SHORTEN, D)
    section_ref[...] = (
        (r.stream[...].astype(f32).reshape(spread) + coarse_out[:, None, :])
        .reshape(tok, D)
        .astype(bf16)
    )
    on.append(pass_on(1))

    landed(norm_sum)
    normed_grad = jnp.sum(r.norm_in[...].astype(f32), axis=0)
    scaled = normed_grad * gain_ref[...]
    coarse_total = r.coarse_grad[...] + rstd * (
        scaled - base * jnp.mean(scaled * base, axis=-1, keepdims=True)
    )
    fold_row(r.follow_out, coarse_total[0:1])
    follow = remote(r.follow_out, r.follow_in, before)
    follow.start()

    on.append(pass_on(2))

    outs = (down_grad_ref, gate_grad_ref, up_grad_ref)

    def term(i):
        landed(rings[i][0][1:] + rings[i][1][1:] + on[i])
        right = r.gg_all if i == 0 else r.ng_all
        left = r.hgu[i].reshape(4 * group, hid)
        r.term[i] = lax.dot_general(left, right[...], contract_first, preferred_element_type=f32)
        for p in range(2):
            r.sib_out[i, p] = r.term[i, :, lanes(2 * p + 1 - core)].astype(bf16)
        return go([remote(r.sib_out.at[i], r.sib_in.at[i], (sib, t))])

    def join(i):
        landed(to_sib[i : i + 1])
        r.term_out[i] = (
            r.term[i, :, lanes(2 * (1 - half) + core)] + r.sib_in[i, 1 - half].astype(f32)
        ).astype(bf16)
        copies = go([remote(r.term_out.at[i], r.term_in.at[i], (partner, t))])
        outs[i][...] = r.term[i, :, lanes(2 * half + core)] + r.sib_in[i, half].astype(f32)
        return copies

    landed(grad_columns)
    to_sib = term(0)

    landed(norm_columns)
    to_sib += term(1)
    terms = join(0)

    follow.wait_recv()
    following = jnp.where(flat < number - 1, flat_row(r.follow_in), 0.0)
    ahead = jnp.concatenate([coarse_total[1:], following], axis=0)
    place = lax.broadcasted_iota(jnp.int32, spread, 1)
    contrib = jnp.where(place == 0, coarse_total[:, None, :], ahead[:, None, :])
    stream_grad_ref[...] = (
        (r.cot[...].astype(f32).reshape(spread) + contrib / SHORTEN).reshape(tok, D).astype(bf16)
    )

    to_sib += term(2)
    terms += join(1)
    landed(gain_group)
    r.gain_far_out[...] = jnp.sum(r.gain_half[...], axis=0)
    gain_far = remote(r.gain_far_out, r.gain_far_in, (partner, t))
    gain_far.start()
    terms += join(2)
    gain_far.wait_recv()
    gain_grad_ref[...] = flat_row(r.gain_far_out) + flat_row(r.gain_far_in)
    for i in range(3):
        terms[i].wait_recv()
        outs[i][...] = outs[i][...] + r.term_in[i].astype(f32)

    for cp in used:
        cp.wait_send()

    @pl.when(t == TP - 1)
    def _():
        for cp in rim_next:
            cp.wait_send()

    @pl.when(half == 1)
    def _():
        q_over.wait_send()

    @pl.when(half == 0)
    def _():
        for cp in far_back:
            cp.wait_send()


def hand_over_kernel(*refs):
    count = (len(refs) - 2) // 3
    ins, outs, held = refs[:count], refs[count : 2 * count], refs[2 * count : 3 * count]
    arrive, leave = refs[-2:]
    first = [pltpu.make_async_copy(a, b, arrive.at[i]) for i, (a, b) in enumerate(zip(ins, held))]
    second = [pltpu.make_async_copy(a, b, leave.at[i]) for i, (a, b) in enumerate(zip(held, outs))]
    for cp in first:
        cp.start()
    for one, two in zip(first, second):
        one.wait()
        two.start()
    for cp in second:
        cp.wait()


def on_device(
    fine_stream,
    queries,
    keys,
    values,
    out_weight,
    norm_gain,
    gate_weight,
    up_weight,
    down_weight,
    cotangent,
):
    tok = fine_stream.shape[0]
    hid = gate_weight.shape[1]
    seq = lax.axis_size("seq")
    f32, bf16 = jnp.float32, jnp.bfloat16
    vmem, hbm = pl.BlockSpec(memory_space=pltpu.VMEM), pl.BlockSpec(memory_space=pltpu.HBM)
    scratch = scratch_of(tok, hid, seq)
    shapes = (
        jax.ShapeDtypeStruct((tok, D), bf16),
        jax.ShapeDtypeStruct((tok, D), bf16),
        jax.ShapeDtypeStruct((hid, D // seq), f32),
        jax.ShapeDtypeStruct((hid, D // seq), f32),
        jax.ShapeDtypeStruct((hid, D // seq), f32),
        jax.ShapeDtypeStruct((1, D), f32),
    )
    outs = pl.pallas_call(
        lambda *refs: section_kernel(tuple(scratch), *refs),
        out_shape=shapes,
        in_specs=[hbm] * 5 + [vmem] + [hbm] * 4,
        out_specs=(vmem,) * 6,
        scratch_shapes=list(scratch.values()),
        compiler_params=pltpu.CompilerParams(
            collective_id=0, has_side_effects=True, vmem_limit_bytes=60 * 1024 * 1024
        ),
        name="section",
    )(
        queries, keys, values, fine_stream, cotangent, norm_gain.reshape(1, D),
        out_weight, gate_weight.T, up_weight.T, down_weight,
    )
    section_out, stream_grad, gate_grad, up_grad, down_grad, gain_grad = pl.pallas_call(
        hand_over_kernel,
        out_shape=shapes,
        in_specs=[hbm] * 6,
        out_specs=(hbm,) * 6,
        scratch_shapes=[pltpu.VMEM(shape.shape, shape.dtype) for shape in shapes]
        + [pltpu.SemaphoreType.DMA((6,)), pltpu.SemaphoreType.DMA((6,))],
        compiler_params=pltpu.CompilerParams(vmem_limit_bytes=60 * 1024 * 1024),
        name="hand_over",
    )(*outs)
    return (section_out, stream_grad, gate_grad.T, up_grad.T, down_grad, gain_grad.reshape(D))


def solution(mesh):
    return jax.shard_map(
        on_device,
        mesh=mesh,
        in_specs=(
            P(("seq", "tp"), None),
            P(("seq", "tp"), None),
            P(("seq", "tp"), None),
            P(("seq", "tp"), None),
            P(),
            P(),
            P(None, "tp"),
            P(None, "tp"),
            P("tp", None),
            P(("seq", "tp"), None),
        ),
        out_specs=(
            P(("seq", "tp"), None),
            P(("seq", "tp"), None),
            P("seq", "tp"),
            P("seq", "tp"),
            P("tp", "seq"),
            P(),
        ),
        check_vma=False,
    )
```

```python
import math

import jax
import jax.numpy as jnp
from jax import lax
from jax.experimental import pallas as pl
from jax.experimental.pallas import tpu as pltpu
from jax.sharding import PartitionSpec as P

D = 2048
HEAD = 128
SHORTEN = 8
MESH = pl.DeviceIdType.MESH
TP = 8
WIDE = 512
COPIES = 210

contract_last = (((1,), (1,)), ((), ()))
contract_first = (((0,), (0,)), ((), ()))
very_low = -1e30
POWER = math.log2(math.e) * HEAD ** (-0.5)


def scratch_of(tok, hid, seq):
    crows, group, rows = tok // SHORTEN, tok // SHORTEN * TP, tok * TP
    f32, bf16 = jnp.float32, jnp.bfloat16
    vmem = pltpu.VMEM
    small = (8, D // 8)
    return {
        "q_in": vmem((tok, TP * HEAD), bf16),
        "k_in": vmem((tok, TP * HEAD), bf16),
        "v_in": vmem((tok, TP * HEAD), bf16),
        "fine": vmem((tok, D), bf16),
        "cot": vmem((tok, D), bf16),
        "out_w": vmem((TP * HEAD, D), bf16),
        "gate_w": vmem((hid, D), bf16),
        "up_w": vmem((hid, D), bf16),
        "down_w": vmem((hid, D), bf16),
        "vt_src": vmem((TP, HEAD, tok), bf16),
        "q_own": vmem((rows, HEAD), bf16),
        "q_far": vmem((rows, HEAD), bf16),
        "q_work": vmem((rows, HEAD), bf16),
        "k_all": vmem((8, rows, HEAD), bf16),
        "vt_all": vmem((8, HEAD, rows), bf16),
        "scores": vmem((2, WIDE, WIDE), f32),
        "tops": vmem((2, 1, WIDE), f32),
        "m_own": vmem((1, rows), f32),
        "l_own": vmem((1, rows), f32),
        "acc_own": vmem((HEAD, rows), f32),
        "m_far": vmem((1, rows), f32),
        "l_far": vmem((1, rows), f32),
        "acc_far": vmem((HEAD, rows), f32),
        "o_own": vmem((HEAD, rows), bf16),
        "o_far": vmem((HEAD, rows), bf16),
        "stat_own": vmem((8, rows), f32),
        "stat_far": vmem((8, rows), f32),
        "own_in": vmem((TP, HEAD, tok), bf16),
        "far_in": vmem((TP, HEAD, tok), bf16),
        "own_stat_in": vmem((TP, 8, tok), f32),
        "far_stat_in": vmem((TP, 8, tok), f32),
        "att": vmem((TP * HEAD, tok), bf16),
        "stream": vmem((tok, D), bf16),
        "edge_out": vmem(small, f32),
        "edge_in": vmem(small, f32),
        "fine_rows": vmem((crows, D), f32),
        "fine_pool": vmem((crows, D), bf16),
        "fine_all": vmem((group, D), bf16),
        "pool_out": vmem((crows, TP * HEAD), bf16),
        "pool_all": vmem((TP, crows, TP * HEAD), bf16),
        "rim_out": vmem((TP, HEAD), f32),
        "rim_in": vmem((TP, TP, HEAD), f32),
        "rim_prev": vmem((TP, HEAD), f32),
        "coarse_all": vmem((group, D), f32),
        "coarse_grad": vmem((crows, D), f32),
        "coarse_grad_b": vmem((crows, D), bf16),
        "ng": vmem((group, D), bf16),
        "gg": vmem((group, D), bf16),
        "hidden_grad": vmem((group, hid), f32),
        "ng_all": vmem((4 * group, 4 * HEAD), bf16),
        "gg_all": vmem((4 * group, 4 * HEAD), bf16),
        "hgu": vmem((3, 4, group, hid), bf16),
        "down_out": vmem((TP, crows, D), bf16),
        "down_in": vmem((TP, crows, D), bf16),
        "norm_out": vmem((TP, crows, D), bf16),
        "norm_in": vmem((TP, crows, D), bf16),
        "follow_out": vmem(small, f32),
        "follow_in": vmem(small, f32),
        "gain_out": vmem(small, f32),
        "gain_in": vmem((TP,) + small, f32),
        "gain_mid": vmem(small, f32),
        "gain_half": vmem((8,) + small, f32),
        "gain_far_out": vmem(small, f32),
        "gain_far_in": vmem(small, f32),
        "term": vmem((3, hid, 4 * HEAD), f32),
        "sib_out": vmem((3, 2, hid, HEAD), bf16),
        "sib_in": vmem((3, 2, hid, HEAD), bf16),
        "term_out": vmem((3, hid, HEAD), bf16),
        "term_in": vmem((3, hid, HEAD), bf16),
        "send": pltpu.SemaphoreType.DMA((COPIES,)),
        "recv": pltpu.SemaphoreType.DMA((COPIES,)),
        "local": pltpu.SemaphoreType.DMA((20,)),
    }


class Space:
    pass


def section_kernel(
    names, q_hbm, k_hbm, v_hbm, fine_hbm, cot_hbm, gain_ref, out_hbm, gate_hbm, up_hbm, down_hbm,
    section_ref, stream_grad_ref, gate_grad_ref, up_grad_ref, down_grad_ref, gain_grad_ref, *scratch,
):
    r = Space()
    for name, ref in zip(names, scratch):
        setattr(r, name, ref)
    f32, bf16 = jnp.float32, jnp.bfloat16
    s, t = lax.axis_index("seq"), lax.axis_index("tp")
    half, block = s // 8, lax.rem(s, 8)
    y, core = block // 2, lax.rem(block, 2)
    sib = half * 8 + y * 2 + (1 - core)
    up = half * 8 + lax.rem(y + 1, 4) * 2 + core
    down = half * 8 + lax.rem(y + 3, 4) * 2 + core
    partner = (1 - half) * 8 + block
    mirror_block = (3 - y) * 2 + core
    mirror = half * 8 + mirror_block
    number = lax.axis_size("seq") * TP
    flat = s * TP + t
    after, before = lax.rem(flat + 1, number), lax.rem(flat + number - 1, number)
    after, before = (after // TP, lax.rem(after, TP)), (before // TP, lax.rem(before, TP))
    tok = r.fine.shape[0]
    crows = tok // SHORTEN
    group = crows * TP
    hid = r.gate_w.shape[0]

    loads = {}

    def load(name, src):
        loads[name] = pltpu.make_async_copy(src, getattr(r, name), r.local.at[len(loads)])
        loads[name].start()

    load("k_in", k_hbm)
    load("v_in", v_hbm)
    load("q_in", q_hbm)

    barrier = pltpu.get_barrier_semaphore()
    peers = [(s, lax.rem(t + off, TP)) for off in range(1, TP)]
    peers += [(half * 8 + lax.rem(block + off, 8), t) for off in range(1, 8)]
    peers += [(partner, lax.rem(t + off, TP)) for off in range(TP)] + [after, before]
    for peer in peers + [(lax.rem(s + 15, 16), TP - 1)]:
        pl.semaphore_signal(barrier, inc=1, device_id=peer, device_id_type=MESH)

    @pl.when(t >= TP // 2)
    def _():
        for h in range(TP):
            pl.semaphore_signal(barrier, inc=1, device_id=(mirror, h), device_id_type=MESH)

    for ref, value in ((r.m_own, very_low), (r.l_own, 0.0), (r.acc_own, 0.0),
                       (r.m_far, very_low), (r.l_far, 0.0), (r.acc_far, 0.0)):
        ref[...] = jnp.full(ref.shape, value, f32)
    loads["v_in"].wait()
    for h in range(TP):
        r.vt_src[h] = r.v_in[:, h * HEAD : (h + 1) * HEAD].astype(f32).T.astype(bf16)
    loads["k_in"].wait()
    loads["q_in"].wait()
    pl.semaphore_wait(barrier, len(peers) + TP // 2 + TP * (t // (TP - 1)))

    used, sometimes = [], []

    def remote(src, dst, device, always=True, arrival=None):
        kind = len(used) + len(sometimes)
        arrival = kind if arrival is None else arrival
        cp = pltpu.make_async_remote_copy(
            src_ref=src, dst_ref=dst, send_sem=r.send.at[kind], recv_sem=r.recv.at[arrival],
            device_id=device, device_id_type=MESH,
        )
        (used if always else sometimes).append(cp)
        return cp

    def go(copies):
        for cp in copies:
            cp.start()
        return copies

    def landed(copies):
        for cp in copies:
            cp.wait_recv()

    def to_group(src, dst):
        return go([
            remote(src(lax.rem(t + off, TP)), dst, (s, lax.rem(t + off, TP))) for off in range(1, TP)
        ])

    def aligned(index, size):
        return pl.ds(pl.multiple_of(index * size, size), size)

    def lanes(index):
        return aligned(index, HEAD)

    width = D // 8

    def fold_row(ref, value):
        for i in range(8):
            ref[i : i + 1, :] = value[:, i * width : (i + 1) * width]

    def flat_row(ref):
        return jnp.concatenate([ref[i : i + 1, :] for i in range(8)], axis=1)

    band = aligned(t, tok)
    k_copies = to_group(lambda peer: r.k_in.at[:, lanes(peer)], r.k_all.at[block, band, :])
    v_copies = to_group(lambda peer: r.vt_src.at[peer], r.vt_all.at[block, :, band])
    q_copies = to_group(lambda peer: r.q_in.at[:, lanes(peer)], r.q_own.at[band, :])
    own = go([
        pltpu.make_async_copy(r.q_in.at[:, lanes(t)], r.q_own.at[band, :], r.local.at[9]),
        pltpu.make_async_copy(r.k_in.at[:, lanes(t)], r.k_all.at[block, band, :], r.local.at[10]),
        pltpu.make_async_copy(r.vt_src.at[t], r.vt_all.at[block, :, band], r.local.at[11]),
    ])

    load("cot", cot_hbm)
    load("fine", fine_hbm)

    mine = aligned(t, crows)
    row = lax.broadcasted_iota(jnp.int32, (crows, tok), 0)
    col = lax.broadcasted_iota(jnp.int32, (crows, tok), 1)
    members = jnp.where((col >= row * SHORTEN) & (col < row * SHORTEN + SHORTEN), 1.0, 0.0).astype(bf16)
    loads["cot"].wait()
    r.coarse_grad[...] = jnp.dot(members, r.cot[...], preferred_element_type=f32)
    r.coarse_grad_b[...] = r.coarse_grad[...].astype(bf16)
    r.gg[mine, :] = r.coarse_grad_b[...]

    for cp in own:
        cp.wait()
    k_mine, v_mine = r.k_all.at[block], r.vt_all.at[block]
    landed(k_copies)
    k_ring = go([remote(k_mine, k_mine, (device, t)) for device in (up, down, sib)])
    landed(v_copies)
    v_ring = go([remote(v_mine, v_mine, (device, t)) for device in (down, up, sib)])
    landed(q_copies)
    low, high = pl.ds(0, WIDE), pl.ds(WIDE, WIDE)
    q_swap = remote(r.q_own.at[high, :], r.q_work.at[high, :], (mirror, t))
    q_swap.start()
    r.q_work[low, :] = r.q_own[low, :]
    q_over = remote(r.q_own, r.q_far, (partner, t), always=False)

    @pl.when(half == 1)
    def _():
        q_over.start()

    grad_gather = to_group(lambda peer: r.coarse_grad_b, r.gg.at[mine, :])
    load("out_w", out_hbm)
    load("down_w", down_hbm)
    load("gate_w", gate_hbm)
    load("up_w", up_hbm)

    row = lax.broadcasted_iota(jnp.int32, (crows + 8, tok), 0)
    col = lax.broadcasted_iota(jnp.int32, (crows + 8, tok), 1)
    window = jnp.where((col >= row * SHORTEN - (SHORTEN - 1)) & (col <= row * SHORTEN), 1.0, 0.0)
    window = window.astype(bf16)
    first_row = lax.broadcasted_iota(jnp.int32, (crows, 1), 0) == 0
    loads["fine"].wait()
    pooled = jnp.dot(window, r.fine[...], preferred_element_type=f32)
    r.fine_rows[...] = pooled[:crows]
    fold_row(r.edge_out, pooled[crows : crows + 1])
    edge_copy = remote(r.edge_out, r.edge_in, after)
    edge_copy.start()

    def block_of(step):
        j = step // 2
        dy = j + (j // 2) * (5 - 2 * j)
        return lax.rem(y + dy, 4) * 2 + lax.rem(core + step, 2)

    def score(q_all, key_block, piece, slot):
        kk, u = piece
        st = lax.dot_general(
            r.k_all[key_block, kk * WIDE : (kk + 1) * WIDE], q_all[u * WIDE : (u + 1) * WIDE],
            contract_last, preferred_element_type=f32,
        )
        if slot is None:
            return st
        r.scores[slot] = st
        r.tops[slot] = jnp.max(st, axis=0, keepdims=True)

    def absorb(state, st, top, key_block, piece):
        m_all, l_all, acc_all = state
        kk, u = piece
        cols = slice(u * WIDE, (u + 1) * WIDE)
        older = m_all[:, cols]
        fresh = jnp.maximum(older, top)
        weights = jnp.exp2((st - fresh) * POWER)
        factor = jnp.exp2((older - fresh) * POWER)
        m_all[:, cols] = fresh
        l_all[:, cols] = l_all[:, cols] * factor + jnp.sum(weights, axis=0, keepdims=True)
        acc_all[:, cols] = acc_all[:, cols] * factor + jnp.dot(
            r.vt_all[key_block, :, kk * WIDE : (kk + 1) * WIDE], weights.astype(bf16),
            preferred_element_type=f32,
        )

    def sweep(q_all, state, first, last, index, columns=(0, 1)):
        pieces = [(kk, u) for kk in range(2) for u in columns]
        score(q_all, index(first), pieces[0], 0)

        @pl.loop(first, last)
        def _(step):
            here, then = index(step), index(jnp.minimum(step + 1, last - 1))
            for i, piece in enumerate(pieces):
                if i + 1 < len(pieces):
                    score(q_all, here, pieces[i + 1], (i + 1) % 2)
                else:
                    score(q_all, then, pieces[0], (i + 1) % 2)
                absorb(state, r.scores[i % 2], r.tops[i % 2], here, piece)

    own_state = (r.m_own, r.l_own, r.acc_own)
    far_state = (r.m_far, r.l_far, r.acc_far)

    def arrived(first, last):
        @pl.when(half == 0)
        def _():
            sweep(r.q_far, far_state, first, last, block_of)

    def fold_own(key_block, piece, diagonal):
        st = score(r.q_work, key_block, piece, None)
        if diagonal:
            key_pos = lax.broadcasted_iota(jnp.int32, st.shape, 0)
            query_pos = lax.broadcasted_iota(jnp.int32, st.shape, 1)
            st = jnp.where(key_pos <= query_pos, st, very_low)
        absorb(own_state, st, jnp.max(st, axis=0, keepdims=True), key_block, piece)

    fold_own(block, (0, 0), True)

    def to_columns(rows_ref, gathered, sem):
        copies, kept = [], []
        for part in range(2):
            dst = gathered.at[aligned(y, group), part * 2 * HEAD : (part + 1) * 2 * HEAD]

            def columns(y_index):
                return rows_ref.at[:, aligned(part * 4 + y_index, 2 * HEAD)]

            for off in range(1, 4):
                peer = lax.rem(y + off, 4)
                copies.append(remote(columns(peer), dst, (half * 8 + peer * 2 + core, t)))
            kept.append(pltpu.make_async_copy(columns(y), dst, r.local.at[sem + part]))
        go(copies)
        for cp in go(kept):
            cp.wait()
        return copies

    landed([k_ring[2], v_ring[2]])

    @pl.when(half == 0)
    def _():
        q_over.wait_recv()

    arrived(0, 2)
    k_below, v_below = r.k_all.at[block_of(4)], r.vt_all.at[block_of(4)]
    k_above, v_above = r.k_all.at[block_of(2)], r.vt_all.at[block_of(2)]
    k_across, v_across = r.k_all.at[block_of(6)], r.vt_all.at[block_of(6)]
    landed(k_ring[:1])
    k_on = go([remote(k_below, k_below, (up, t)), remote(k_below, k_below, (sib, t))])
    landed(v_ring[:1])
    v_on = go([remote(v_above, v_above, (down, t)), remote(v_above, v_above, (sib, t))])
    landed(k_ring[1:2])
    k_on += go([remote(k_above, k_above, (sib, t))])
    landed(v_ring[1:2])
    v_on += go([remote(v_below, v_below, (sib, t))])
    arrived(2, 3)
    landed([k_on[2], v_on[1]])
    arrived(3, 4)
    landed([k_on[1], v_on[2]])
    landed(k_on[:1])
    k_last = go([remote(k_across, k_across, (sib, t))])
    landed(v_on[:1])
    v_last = go([remote(v_across, v_across, (sib, t))])
    arrived(4, 7)
    edge_copy.wait_recv()
    edge = jnp.where(flat > 0, flat_row(r.edge_in), 0.0)
    r.fine_pool[...] = (r.fine_rows[...] + jnp.where(first_row, edge, 0.0)).astype(bf16)
    r.fine_all[mine, :] = r.fine_pool[...]
    fine_gather = to_group(lambda peer: r.fine_pool, r.fine_all.at[mine, :])
    landed(k_last + v_last)
    arrived(7, 8)

    def normalized(state, out, stat):
        m_all, l_all, acc_all = state
        out[...] = (acc_all[...] / l_all[...]).astype(bf16)
        stat[0:1] = m_all[...]
        stat[1:2] = l_all[...]

    far_back = []
    for off in range(TP):
        peer = lax.rem(t + off, TP)
        far_back += [
            remote(r.o_far.at[:, lanes(peer)], r.far_in.at[t], (partner, peer), always=False),
            remote(r.stat_far.at[:, lanes(peer)], r.far_stat_in.at[t], (partner, peer), always=False),
        ]

    @pl.when(half == 0)
    def _():
        normalized(far_state, r.o_far, r.stat_far)
        go(far_back)
        r.far_in[...] = jnp.zeros(r.far_in.shape, bf16)
        r.far_stat_in[:, 0:1] = jnp.full((TP, 1, tok), very_low, f32)
        r.far_stat_in[:, 1:2] = jnp.zeros((TP, 1, tok), f32)

    q_swap.wait_recv()
    sweep(r.q_work, own_state, 0, block, lambda step: step, (0,))
    sweep(r.q_work, own_state, 0, mirror_block, lambda step: step, (1,))
    fold_own(mirror_block, (0, 1), False)
    fold_own(mirror_block, (1, 1), True)
    normalized(own_state, r.o_own, r.stat_own)

    def row_owner(peer):
        return (s + (peer // (TP // 2)) * (mirror - s), peer)

    back = []
    for off in range(1, TP):
        peer = lax.rem(t + off, TP)
        back += [
            remote(r.o_own.at[:, lanes(peer)], r.own_in.at[t], row_owner(peer)),
            remote(r.stat_own.at[:, lanes(peer)], r.own_stat_in.at[t], row_owner(peer)),
        ]
    go(back)
    swapped = [
        remote(r.o_own.at[:, lanes(t)], r.own_in.at[t], (mirror, t), always=False),
        remote(r.stat_own.at[:, lanes(t)], r.own_stat_in.at[t], (mirror, t), always=False),
    ]

    @pl.when(t < TP // 2)
    def _():
        kept = go([
            pltpu.make_async_copy(r.o_own.at[:, lanes(t)], r.own_in.at[t], r.local.at[14]),
            pltpu.make_async_copy(r.stat_own.at[:, lanes(t)], r.own_stat_in.at[t], r.local.at[17]),
        ])
        for cp in kept:
            cp.wait()

    @pl.when(t >= TP // 2)
    def _():
        go(swapped)

    landed(grad_gather)
    grad_columns = to_columns(r.gg, r.gg_all, 12)
    loads["out_w"].wait()
    landed(back)

    @pl.when(t >= TP // 2)
    def _():
        landed(swapped)

    @pl.when(half == 1)
    def _():
        landed(far_back)

    for h in range(TP):
        own_m, own_l = r.own_stat_in[h, 0:1], r.own_stat_in[h, 1:2]
        far_m, far_l = r.far_stat_in[h, 0:1], r.far_stat_in[h, 1:2]
        top = jnp.maximum(own_m, far_m)
        own_l = own_l * jnp.exp2((own_m - top) * POWER)
        far_l = far_l * jnp.exp2((far_m - top) * POWER)
        total = own_l + far_l
        r.att[h * HEAD : (h + 1) * HEAD] = (
            r.own_in[h].astype(f32) * (own_l / total) + r.far_in[h].astype(f32) * (far_l / total)
        ).astype(bf16)
    pooled = lax.dot_general(window, r.att[...], contract_last, preferred_element_type=f32)
    r.pool_out[...] = pooled[:crows].astype(bf16)
    r.pool_all[t] = r.pool_out[...]
    for i in range(TP):
        r.rim_out[i : i + 1, :] = pooled[crows : crows + 1, i * HEAD : (i + 1) * HEAD]
    r.rim_in[t] = r.rim_out[...]
    pool_gather = to_group(lambda peer: r.pool_out, r.pool_all.at[t])
    pool_gather += to_group(lambda peer: r.rim_out, r.rim_in.at[t])
    rim_kind = len(used) + len(sometimes)
    rim_next = [
        remote(r.rim_out, r.rim_prev, (lax.rem(s + 1, 16), lax.rem(t + off, TP)), always=False,
               arrival=rim_kind)
        for off in range(TP)
    ]

    @pl.when(t == TP - 1)
    def _():
        go(rim_next)

    loads["down_w"].wait()
    r.hidden_grad[...] = lax.dot_general(
        r.gg[...], r.down_w[...], contract_last, preferred_element_type=f32
    )
    loads["gate_w"].wait()
    loads["up_w"].wait()
    landed(fine_gather + pool_gather + rim_next[:1])
    for i in range(TP):
        source = r.rim_prev if i == 0 else r.rim_in.at[i - 1]
        rim = jnp.concatenate([source[h : h + 1, :] for h in range(TP)], axis=1)
        if i == 0:
            rim = jnp.where(s > 0, rim, 0.0)
        r.pool_all[i] = (r.pool_all[i].astype(f32) + jnp.where(first_row, rim, 0.0)).astype(bf16)
    coarse_all = jnp.dot(
        r.pool_all[...].reshape(group, TP * HEAD), r.out_w[...], preferred_element_type=f32
    )
    coarse_all = (coarse_all + r.fine_all[...].astype(f32)) / SHORTEN
    r.coarse_all[...] = coarse_all
    rstd_all = lax.rsqrt(jnp.mean(coarse_all * coarse_all, axis=-1, keepdims=True) + 1e-05)
    r.ng[...] = (coarse_all * rstd_all * gain_ref[...]).astype(bf16)
    coarse = r.coarse_all[mine, :]
    rstd = lax.rsqrt(jnp.mean(coarse * coarse, axis=-1, keepdims=True) + 1e-05)
    base = coarse * rstd

    norm_columns = to_columns(r.ng, r.ng_all, 15)
    gate = lax.dot_general(r.ng[...], r.gate_w[...], contract_last, preferred_element_type=f32)
    up_v = lax.dot_general(r.ng[...], r.up_w[...], contract_last, preferred_element_type=f32)
    sig = jax.nn.sigmoid(gate)
    act = gate * sig
    above, below, across = (lax.rem(y + dy, 4) for dy in (1, 3, 2))
    cut = group // 2
    parts = (pl.ds(0, cut), pl.ds(cut, cut))

    def ring(i, source, piece, device):
        ref = r.hgu.at[i, source, parts[piece], :]
        return remote(ref, ref, (device, t))

    def around(i):
        return (
            go([ring(i, y, 0, up), ring(i, y, 1, up)]),
            go([ring(i, y, 1, down), ring(i, y, 0, down)]),
        )

    rings = []
    r.hgu[0, y] = (act * up_v).astype(bf16)
    rings.append(around(0))
    r.hgu[1, y] = (
        r.hidden_grad[...] * up_v * sig * (1.0 + gate * (1.0 - sig))
    ).astype(bf16)
    rings.append(around(1))
    r.hgu[2, y] = (r.hidden_grad[...] * act).astype(bf16)
    rings.append(around(2))

    part = jnp.dot(r.hgu[0, y], r.down_w[...], preferred_element_type=f32)
    r.down_out[...] = part.astype(bf16).reshape(r.down_out.shape)
    r.down_in[t] = r.down_out[t]
    down_sum = to_group(lambda peer: r.down_out.at[peer], r.down_in.at[t])
    part = jnp.dot(r.hgu[1, y], r.gate_w[...], preferred_element_type=f32) + jnp.dot(
        r.hgu[2, y], r.up_w[...], preferred_element_type=f32
    )
    r.norm_out[...] = part.astype(bf16).reshape(r.norm_out.shape)
    r.norm_in[t] = r.norm_out[t]
    norm_sum = to_group(lambda peer: r.norm_out.at[peer], r.norm_in.at[t])
    fold_row(r.gain_out, jnp.sum(part * (r.coarse_all[...] * rstd_all), axis=0, keepdims=True))
    r.gain_in[t] = r.gain_out[...]
    gain_sum = to_group(lambda peer: r.gain_out, r.gain_in.at[t])

    projected = lax.dot_general(r.att[...], r.out_w[...], contract_first, preferred_element_type=f32)
    r.stream[...] = (r.fine[...].astype(f32) + projected).astype(bf16)

    def pass_on(i):
        ring_up, ring_down = rings[i]
        landed(ring_up[:1])
        first = go([ring(i, below, 0, up)])
        landed(ring_down[:1])
        return first + go([ring(i, above, 1, down)])

    on = [pass_on(0)]

    landed(gain_sum)
    r.gain_mid[...] = jnp.sum(r.gain_in[...], axis=0)
    r.gain_half[block] = r.gain_mid[...]
    gain_group = go([
        remote(r.gain_mid, r.gain_half.at[block], (half * 8 + lax.rem(block + off, 8), t))
        for off in range(1, 8)
    ])

    landed(down_sum)
    coarse_out = coarse + jnp.sum(r.down_in[...].astype(f32), axis=0)
    spread = (crows, SHORTEN, D)
    section_ref[...] = (
        (r.stream[...].astype(f32).reshape(spread) + coarse_out[:, None, :])
        .reshape(tok, D)
        .astype(bf16)
    )
    on.append(pass_on(1))

    landed(norm_sum)
    normed_grad = jnp.sum(r.norm_in[...].astype(f32), axis=0)
    scaled = normed_grad * gain_ref[...]
    coarse_total = r.coarse_grad[...] + rstd * (
        scaled - base * jnp.mean(scaled * base, axis=-1, keepdims=True)
    )
    fold_row(r.follow_out, coarse_total[0:1])
    follow = remote(r.follow_out, r.follow_in, before)
    follow.start()

    on.append(pass_on(2))

    outs = (down_grad_ref, gate_grad_ref, up_grad_ref)

    def term(i):
        landed(rings[i][0][1:] + rings[i][1][1:] + on[i])
        right = r.gg_all if i == 0 else r.ng_all
        left = r.hgu[i].reshape(4 * group, hid)
        r.term[i] = lax.dot_general(left, right[...], contract_first, preferred_element_type=f32)
        for p in range(2):
            r.sib_out[i, p] = r.term[i, :, lanes(2 * p + 1 - core)].astype(bf16)
        return go([remote(r.sib_out.at[i], r.sib_in.at[i], (sib, t))])

    def join(i):
        landed(to_sib[i : i + 1])
        r.term_out[i] = (
            r.term[i, :, lanes(2 * (1 - half) + core)] + r.sib_in[i, 1 - half].astype(f32)
        ).astype(bf16)
        copies = go([remote(r.term_out.at[i], r.term_in.at[i], (partner, t))])
        outs[i][...] = r.term[i, :, lanes(2 * half + core)] + r.sib_in[i, half].astype(f32)
        return copies

    landed(grad_columns)
    to_sib = term(0)

    landed(norm_columns)
    to_sib += term(1)
    terms = join(0)

    follow.wait_recv()
    following = jnp.where(flat < number - 1, flat_row(r.follow_in), 0.0)
    ahead = jnp.concatenate([coarse_total[1:], following], axis=0)
    place = lax.broadcasted_iota(jnp.int32, spread, 1)
    contrib = jnp.where(place == 0, coarse_total[:, None, :], ahead[:, None, :])
    stream_grad_ref[...] = (
        (r.cot[...].astype(f32).reshape(spread) + contrib / SHORTEN).reshape(tok, D).astype(bf16)
    )

    to_sib += term(2)
    terms += join(1)
    landed(gain_group)
    r.gain_far_out[...] = jnp.sum(r.gain_half[...], axis=0)
    gain_far = remote(r.gain_far_out, r.gain_far_in, (partner, t))
    gain_far.start()
    terms += join(2)
    gain_far.wait_recv()
    gain_grad_ref[...] = flat_row(r.gain_far_out) + flat_row(r.gain_far_in)
    for i in range(3):
        terms[i].wait_recv()
        outs[i][...] = outs[i][...] + r.term_in[i].astype(f32)

    for cp in used:
        cp.wait_send()

    @pl.when(t == TP - 1)
    def _():
        for cp in rim_next:
            cp.wait_send()

    @pl.when(t >= TP // 2)
    def _():
        for cp in swapped:
            cp.wait_send()

    @pl.when(half == 1)
    def _():
        q_over.wait_send()

    @pl.when(half == 0)
    def _():
        for cp in far_back:
            cp.wait_send()


def hand_over_kernel(*refs):
    count = (len(refs) - 2) // 3
    ins, outs, held = refs[:count], refs[count : 2 * count], refs[2 * count : 3 * count]
    arrive, leave = refs[-2:]
    first = [pltpu.make_async_copy(a, b, arrive.at[i]) for i, (a, b) in enumerate(zip(ins, held))]
    second = [pltpu.make_async_copy(a, b, leave.at[i]) for i, (a, b) in enumerate(zip(held, outs))]
    for cp in first:
        cp.start()
    for one, two in zip(first, second):
        one.wait()
        two.start()
    for cp in second:
        cp.wait()


def on_device(
    fine_stream,
    queries,
    keys,
    values,
    out_weight,
    norm_gain,
    gate_weight,
    up_weight,
    down_weight,
    cotangent,
):
    tok = fine_stream.shape[0]
    hid = gate_weight.shape[1]
    seq = lax.axis_size("seq")
    f32, bf16 = jnp.float32, jnp.bfloat16
    vmem, hbm = pl.BlockSpec(memory_space=pltpu.VMEM), pl.BlockSpec(memory_space=pltpu.HBM)
    scratch = scratch_of(tok, hid, seq)
    shapes = (
        jax.ShapeDtypeStruct((tok, D), bf16),
        jax.ShapeDtypeStruct((tok, D), bf16),
        jax.ShapeDtypeStruct((hid, D // seq), f32),
        jax.ShapeDtypeStruct((hid, D // seq), f32),
        jax.ShapeDtypeStruct((hid, D // seq), f32),
        jax.ShapeDtypeStruct((1, D), f32),
    )
    outs = pl.pallas_call(
        lambda *refs: section_kernel(tuple(scratch), *refs),
        out_shape=shapes,
        in_specs=[hbm] * 5 + [vmem] + [hbm] * 4,
        out_specs=(vmem,) * 6,
        scratch_shapes=list(scratch.values()),
        compiler_params=pltpu.CompilerParams(
            collective_id=0, has_side_effects=True, vmem_limit_bytes=60 * 1024 * 1024
        ),
        name="section",
    )(
        queries, keys, values, fine_stream, cotangent, norm_gain.reshape(1, D),
        out_weight, gate_weight.T, up_weight.T, down_weight,
    )
    section_out, stream_grad, gate_grad, up_grad, down_grad, gain_grad = pl.pallas_call(
        hand_over_kernel,
        out_shape=shapes,
        in_specs=[hbm] * 6,
        out_specs=(hbm,) * 6,
        scratch_shapes=[pltpu.VMEM(shape.shape, shape.dtype) for shape in shapes]
        + [pltpu.SemaphoreType.DMA((6,)), pltpu.SemaphoreType.DMA((6,))],
        compiler_params=pltpu.CompilerParams(vmem_limit_bytes=60 * 1024 * 1024),
        name="hand_over",
    )(*outs)
    return (section_out, stream_grad, gate_grad.T, up_grad.T, down_grad, gain_grad.reshape(D))


def solution(mesh):
    return jax.shard_map(
        on_device,
        mesh=mesh,
        in_specs=(
            P(("seq", "tp"), None),
            P(("seq", "tp"), None),
            P(("seq", "tp"), None),
            P(("seq", "tp"), None),
            P(),
            P(),
            P(None, "tp"),
            P(None, "tp"),
            P("tp", None),
            P(("seq", "tp"), None),
        ),
        out_specs=(
            P(("seq", "tp"), None),
            P(("seq", "tp"), None),
            P("seq", "tp"),
            P("seq", "tp"),
            P("tp", "seq"),
            P(),
        ),
        check_vma=False,
    )
```

```python
import math

import jax
import jax.numpy as jnp
from jax import lax
from jax.experimental import pallas as pl
from jax.experimental.pallas import tpu as pltpu
from jax.sharding import PartitionSpec as P

D = 2048
HEAD = 128
SHORTEN = 8
MESH = pl.DeviceIdType.MESH
TP = 8
WIDE = 512
COPIES = 200

contract_last = (((1,), (1,)), ((), ()))
contract_first = (((0,), (0,)), ((), ()))
very_low = -1e30
POWER = math.log2(math.e) * HEAD ** (-0.5)


def scratch_of(tok, hid, seq):
    crows, group, rows = tok // SHORTEN, tok // SHORTEN * TP, tok * TP
    f32, bf16 = jnp.float32, jnp.bfloat16
    vmem = pltpu.VMEM
    small = (8, D // 8)
    return {
        "q_in": vmem((tok, TP * HEAD), bf16),
        "k_in": vmem((tok, TP * HEAD), bf16),
        "v_in": vmem((tok, TP * HEAD), bf16),
        "fine": vmem((tok, D), bf16),
        "cot": vmem((tok, D), bf16),
        "out_w": vmem((TP * HEAD, D), bf16),
        "gate_w": vmem((hid, D), bf16),
        "up_w": vmem((hid, D), bf16),
        "down_w": vmem((hid, D), bf16),
        "vt_src": vmem((TP, HEAD, tok), bf16),
        "q_own": vmem((rows, HEAD), bf16),
        "q_far": vmem((rows, HEAD), bf16),
        "k_all": vmem((8, rows, HEAD), bf16),
        "vt_all": vmem((8, HEAD, rows), bf16),
        "scores": vmem((2, WIDE, WIDE), f32),
        "tops": vmem((2, 1, WIDE), f32),
        "m_own": vmem((1, rows), f32),
        "l_own": vmem((1, rows), f32),
        "acc_own": vmem((HEAD, rows), f32),
        "m_far": vmem((1, rows), f32),
        "l_far": vmem((1, rows), f32),
        "acc_far": vmem((HEAD, rows), f32),
        "o_own": vmem((HEAD, rows), bf16),
        "o_far": vmem((HEAD, rows), bf16),
        "stat_own": vmem((8, rows), f32),
        "stat_far": vmem((8, rows), f32),
        "own_in": vmem((TP, HEAD, tok), bf16),
        "far_in": vmem((TP, HEAD, tok), bf16),
        "own_stat_in": vmem((TP, 8, tok), f32),
        "far_stat_in": vmem((TP, 8, tok), f32),
        "att": vmem((TP * HEAD, tok), bf16),
        "stream": vmem((tok, D), bf16),
        "edge_out": vmem(small, f32),
        "edge_in": vmem(small, f32),
        "fine_rows": vmem((crows, D), f32),
        "fine_pool": vmem((crows, D), bf16),
        "fine_all": vmem((group, D), bf16),
        "pool_out": vmem((crows, TP * HEAD), bf16),
        "pool_all": vmem((TP, crows, TP * HEAD), bf16),
        "rim_out": vmem((TP, HEAD), f32),
        "rim_in": vmem((TP, TP, HEAD), f32),
        "rim_prev": vmem((TP, HEAD), f32),
        "coarse_all": vmem((group, D), f32),
        "coarse_grad": vmem((crows, D), f32),
        "coarse_grad_b": vmem((crows, D), bf16),
        "ng": vmem((group, D), bf16),
        "gg": vmem((group, D), bf16),
        "hidden_grad": vmem((group, hid), f32),
        "ng_all": vmem((4 * group, 4 * HEAD), bf16),
        "gg_all": vmem((4 * group, 4 * HEAD), bf16),
        "hgu": vmem((3, 4, group, hid), bf16),
        "down_out": vmem((TP, crows, D), bf16),
        "down_in": vmem((TP, crows, D), bf16),
        "norm_out": vmem((TP, crows, D), bf16),
        "norm_in": vmem((TP, crows, D), bf16),
        "follow_out": vmem(small, f32),
        "follow_in": vmem(small, f32),
        "gain_out": vmem(small, f32),
        "gain_in": vmem((TP,) + small, f32),
        "gain_mid": vmem(small, f32),
        "gain_half": vmem((8,) + small, f32),
        "gain_far_out": vmem(small, f32),
        "gain_far_in": vmem(small, f32),
        "term": vmem((3, hid, 4 * HEAD), f32),
        "sib_out": vmem((3, 2, hid, HEAD), bf16),
        "sib_in": vmem((3, 2, hid, HEAD), bf16),
        "term_out": vmem((3, hid, HEAD), bf16),
        "term_in": vmem((3, hid, HEAD), bf16),
        "send": pltpu.SemaphoreType.DMA((COPIES,)),
        "recv": pltpu.SemaphoreType.DMA((COPIES,)),
        "local": pltpu.SemaphoreType.DMA((20,)),
    }


class Space:
    pass


def section_kernel(
    names, q_hbm, k_hbm, v_hbm, fine_hbm, cot_hbm, gain_ref, out_hbm, gate_hbm, up_hbm, down_hbm,
    section_ref, stream_grad_ref, gate_grad_ref, up_grad_ref, down_grad_ref, gain_grad_ref, *scratch,
):
    r = Space()
    for name, ref in zip(names, scratch):
        setattr(r, name, ref)
    f32, bf16 = jnp.float32, jnp.bfloat16
    s, t = lax.axis_index("seq"), lax.axis_index("tp")
    half, block = s // 8, lax.rem(s, 8)
    y, core = block // 2, lax.rem(block, 2)
    sib = half * 8 + y * 2 + (1 - core)
    up = half * 8 + lax.rem(y + 1, 4) * 2 + core
    down = half * 8 + lax.rem(y + 3, 4) * 2 + core
    partner = (1 - half) * 8 + block
    number = lax.axis_size("seq") * TP
    flat = s * TP + t
    after, before = lax.rem(flat + 1, number), lax.rem(flat + number - 1, number)
    after, before = (after // TP, lax.rem(after, TP)), (before // TP, lax.rem(before, TP))
    tok = r.fine.shape[0]
    crows = tok // SHORTEN
    group = crows * TP
    hid = r.gate_w.shape[0]

    loads = {}

    def load(name, src):
        loads[name] = pltpu.make_async_copy(src, getattr(r, name), r.local.at[len(loads)])
        loads[name].start()

    load("k_in", k_hbm)
    load("v_in", v_hbm)
    load("q_in", q_hbm)

    barrier = pltpu.get_barrier_semaphore()
    peers = [(s, lax.rem(t + off, TP)) for off in range(1, TP)]
    peers += [(half * 8 + lax.rem(block + off, 8), t) for off in range(1, 8)]
    peers += [(partner, lax.rem(t + off, TP)) for off in range(TP)] + [after, before]
    for peer in peers + [(lax.rem(s + 15, 16), TP - 1)]:
        pl.semaphore_signal(barrier, inc=1, device_id=peer, device_id_type=MESH)
    for ref, value in ((r.m_own, very_low), (r.l_own, 0.0), (r.acc_own, 0.0),
                       (r.m_far, very_low), (r.l_far, 0.0), (r.acc_far, 0.0)):
        ref[...] = jnp.full(ref.shape, value, f32)
    loads["v_in"].wait()
    for h in range(TP):
        r.vt_src[h] = r.v_in[:, h * HEAD : (h + 1) * HEAD].astype(f32).T.astype(bf16)
    loads["k_in"].wait()
    loads["q_in"].wait()
    pl.semaphore_wait(barrier, len(peers) + TP * (t // (TP - 1)))

    used, sometimes = [], []

    def remote(src, dst, device, always=True, arrival=None):
        kind = len(used) + len(sometimes)
        arrival = kind if arrival is None else arrival
        cp = pltpu.make_async_remote_copy(
            src_ref=src, dst_ref=dst, send_sem=r.send.at[kind], recv_sem=r.recv.at[arrival],
            device_id=device, device_id_type=MESH,
        )
        (used if always else sometimes).append(cp)
        return cp

    def go(copies):
        for cp in copies:
            cp.start()
        return copies

    def landed(copies):
        for cp in copies:
            cp.wait_recv()

    def to_group(src, dst):
        return go([
            remote(src(lax.rem(t + off, TP)), dst, (s, lax.rem(t + off, TP))) for off in range(1, TP)
        ])

    def aligned(index, size):
        return pl.ds(pl.multiple_of(index * size, size), size)

    def lanes(index):
        return aligned(index, HEAD)

    width = D // 8

    def fold_row(ref, value):
        for i in range(8):
            ref[i : i + 1, :] = value[:, i * width : (i + 1) * width]

    def flat_row(ref):
        return jnp.concatenate([ref[i : i + 1, :] for i in range(8)], axis=1)

    band = aligned(t, tok)
    k_copies = to_group(lambda peer: r.k_in.at[:, lanes(peer)], r.k_all.at[block, band, :])
    v_copies = to_group(lambda peer: r.vt_src.at[peer], r.vt_all.at[block, :, band])
    q_copies = to_group(lambda peer: r.q_in.at[:, lanes(peer)], r.q_own.at[band, :])
    own = go([
        pltpu.make_async_copy(r.q_in.at[:, lanes(t)], r.q_own.at[band, :], r.local.at[9]),
        pltpu.make_async_copy(r.k_in.at[:, lanes(t)], r.k_all.at[block, band, :], r.local.at[10]),
        pltpu.make_async_copy(r.vt_src.at[t], r.vt_all.at[block, :, band], r.local.at[11]),
    ])

    load("cot", cot_hbm)
    load("fine", fine_hbm)

    mine = aligned(t, crows)
    row = lax.broadcasted_iota(jnp.int32, (crows, tok), 0)
    col = lax.broadcasted_iota(jnp.int32, (crows, tok), 1)
    members = jnp.where((col >= row * SHORTEN) & (col < row * SHORTEN + SHORTEN), 1.0, 0.0).astype(bf16)
    loads["cot"].wait()
    r.coarse_grad[...] = jnp.dot(members, r.cot[...], preferred_element_type=f32)
    r.coarse_grad_b[...] = r.coarse_grad[...].astype(bf16)
    r.gg[mine, :] = r.coarse_grad_b[...]

    for cp in own:
        cp.wait()
    k_mine, v_mine = r.k_all.at[block], r.vt_all.at[block]
    landed(k_copies)
    k_ring = go([remote(k_mine, k_mine, (device, t)) for device in (up, down, sib)])
    landed(v_copies)
    v_ring = go([remote(v_mine, v_mine, (device, t)) for device in (down, up, sib)])
    landed(q_copies)
    q_over = remote(r.q_own, r.q_far, (partner, t), always=False)

    @pl.when(half == 1)
    def _():
        q_over.start()

    grad_gather = to_group(lambda peer: r.coarse_grad_b, r.gg.at[mine, :])
    load("out_w", out_hbm)
    load("down_w", down_hbm)
    load("gate_w", gate_hbm)
    load("up_w", up_hbm)

    row = lax.broadcasted_iota(jnp.int32, (crows + 8, tok), 0)
    col = lax.broadcasted_iota(jnp.int32, (crows + 8, tok), 1)
    window = jnp.where((col >= row * SHORTEN - (SHORTEN - 1)) & (col <= row * SHORTEN), 1.0, 0.0)
    window = window.astype(bf16)
    first_row = lax.broadcasted_iota(jnp.int32, (crows, 1), 0) == 0
    loads["fine"].wait()
    pooled = jnp.dot(window, r.fine[...], preferred_element_type=f32)
    r.fine_rows[...] = pooled[:crows]
    fold_row(r.edge_out, pooled[crows : crows + 1])
    edge_copy = remote(r.edge_out, r.edge_in, after)
    edge_copy.start()

    def block_of(step):
        j = step // 2
        dy = j + (j // 2) * (5 - 2 * j)
        return lax.rem(y + dy, 4) * 2 + lax.rem(core + step, 2)

    def score(q_all, key_block, piece, slot):
        kk, u = piece
        st = lax.dot_general(
            r.k_all[key_block, kk * WIDE : (kk + 1) * WIDE], q_all[u * WIDE : (u + 1) * WIDE],
            contract_last, preferred_element_type=f32,
        )
        if slot is None:
            return st
        r.scores[slot] = st
        r.tops[slot] = jnp.max(st, axis=0, keepdims=True)

    def absorb(state, st, top, key_block, piece):
        m_all, l_all, acc_all = state
        kk, u = piece
        cols = slice(u * WIDE, (u + 1) * WIDE)
        older = m_all[:, cols]
        fresh = jnp.maximum(older, top)
        weights = jnp.exp2((st - fresh) * POWER)
        factor = jnp.exp2((older - fresh) * POWER)
        m_all[:, cols] = fresh
        l_all[:, cols] = l_all[:, cols] * factor + jnp.sum(weights, axis=0, keepdims=True)
        acc_all[:, cols] = acc_all[:, cols] * factor + jnp.dot(
            r.vt_all[key_block, :, kk * WIDE : (kk + 1) * WIDE], weights.astype(bf16),
            preferred_element_type=f32,
        )

    pieces = [(kk, u) for kk in range(2) for u in range(2)]

    def sweep(q_all, state, first, last, index):
        score(q_all, index(first), pieces[0], 0)

        @pl.loop(first, last)
        def _(step):
            here, then = index(step), index(jnp.minimum(step + 1, last - 1))
            for i, piece in enumerate(pieces):
                if i + 1 < len(pieces):
                    score(q_all, here, pieces[i + 1], (i + 1) % 2)
                else:
                    score(q_all, then, pieces[0], (i + 1) % 2)
                absorb(state, r.scores[i % 2], r.tops[i % 2], here, piece)

    own_state = (r.m_own, r.l_own, r.acc_own)
    far_state = (r.m_far, r.l_far, r.acc_far)

    def own_steps(first, last):
        @pl.loop(first, last)
        def _(step):
            @pl.when(block_of(step) < block)
            def _():
                sweep(r.q_own, own_state, step, step + 1, block_of)

    def arrived(first, last, later=False):
        @pl.when(half == 0)
        def _():
            sweep(r.q_far, far_state, first, last, block_of)

        if not later:
            own_steps(max(first, 1), last)

    for piece in ((0, 0), (0, 1), (1, 1)):
        st = score(r.q_own, block, piece, None)
        if piece[0] == piece[1]:
            key_pos = lax.broadcasted_iota(jnp.int32, st.shape, 0)
            query_pos = lax.broadcasted_iota(jnp.int32, st.shape, 1)
            st = jnp.where(key_pos <= query_pos, st, very_low)
        absorb(own_state, st, jnp.max(st, axis=0, keepdims=True), block, piece)

    def to_columns(rows_ref, gathered, sem):
        copies, kept = [], []
        for part in range(2):
            dst = gathered.at[aligned(y, group), part * 2 * HEAD : (part + 1) * 2 * HEAD]

            def columns(y_index):
                return rows_ref.at[:, aligned(part * 4 + y_index, 2 * HEAD)]

            for off in range(1, 4):
                peer = lax.rem(y + off, 4)
                copies.append(remote(columns(peer), dst, (half * 8 + peer * 2 + core, t)))
            kept.append(pltpu.make_async_copy(columns(y), dst, r.local.at[sem + part]))
        go(copies)
        for cp in go(kept):
            cp.wait()
        return copies

    landed([k_ring[2], v_ring[2]])

    @pl.when(half == 0)
    def _():
        q_over.wait_recv()

    arrived(0, 2)
    k_below, v_below = r.k_all.at[block_of(4)], r.vt_all.at[block_of(4)]
    k_above, v_above = r.k_all.at[block_of(2)], r.vt_all.at[block_of(2)]
    k_across, v_across = r.k_all.at[block_of(6)], r.vt_all.at[block_of(6)]
    landed(k_ring[:1])
    k_on = go([remote(k_below, k_below, (up, t)), remote(k_below, k_below, (sib, t))])
    landed(v_ring[:1])
    v_on = go([remote(v_above, v_above, (down, t)), remote(v_above, v_above, (sib, t))])
    landed(k_ring[1:2])
    k_on += go([remote(k_above, k_above, (sib, t))])
    landed(v_ring[1:2])
    v_on += go([remote(v_below, v_below, (sib, t))])
    arrived(2, 3)
    landed([k_on[2], v_on[1]])
    arrived(3, 4)
    landed([k_on[1], v_on[2]])
    landed(k_on[:1])
    k_last = go([remote(k_across, k_across, (sib, t))])
    landed(v_on[:1])
    v_last = go([remote(v_across, v_across, (sib, t))])
    arrived(4, 7, later=True)
    edge_copy.wait_recv()
    edge = jnp.where(flat > 0, flat_row(r.edge_in), 0.0)
    r.fine_pool[...] = (r.fine_rows[...] + jnp.where(first_row, edge, 0.0)).astype(bf16)
    r.fine_all[mine, :] = r.fine_pool[...]
    fine_gather = to_group(lambda peer: r.fine_pool, r.fine_all.at[mine, :])
    landed(k_last + v_last)
    arrived(7, 8, later=True)

    def normalized(state, out, stat):
        m_all, l_all, acc_all = state
        out[...] = (acc_all[...] / l_all[...]).astype(bf16)
        stat[0:1] = m_all[...]
        stat[1:2] = l_all[...]

    far_back = []
    for off in range(TP):
        peer = lax.rem(t + off, TP)
        far_back += [
            remote(r.o_far.at[:, lanes(peer)], r.far_in.at[t], (partner, peer), always=False),
            remote(r.stat_far.at[:, lanes(peer)], r.far_stat_in.at[t], (partner, peer), always=False),
        ]

    @pl.when(half == 0)
    def _():
        normalized(far_state, r.o_far, r.stat_far)
        go(far_back)
        r.far_in[...] = jnp.zeros(r.far_in.shape, bf16)
        r.far_stat_in[:, 0:1] = jnp.full((TP, 1, tok), very_low, f32)
        r.far_stat_in[:, 1:2] = jnp.zeros((TP, 1, tok), f32)

    own_steps(4, 8)
    normalized(own_state, r.o_own, r.stat_own)
    back = to_group(lambda peer: r.o_own.at[:, lanes(peer)], r.own_in.at[t])
    back += to_group(lambda peer: r.stat_own.at[:, lanes(peer)], r.own_stat_in.at[t])
    kept = go([
        pltpu.make_async_copy(r.o_own.at[:, lanes(t)], r.own_in.at[t], r.local.at[14]),
        pltpu.make_async_copy(r.stat_own.at[:, lanes(t)], r.own_stat_in.at[t], r.local.at[17]),
    ])
    landed(grad_gather)
    grad_columns = to_columns(r.gg, r.gg_all, 12)
    for cp in kept:
        cp.wait()
    loads["out_w"].wait()
    landed(back)

    @pl.when(half == 1)
    def _():
        landed(far_back)

    for h in range(TP):
        own_m, own_l = r.own_stat_in[h, 0:1], r.own_stat_in[h, 1:2]
        far_m, far_l = r.far_stat_in[h, 0:1], r.far_stat_in[h, 1:2]
        top = jnp.maximum(own_m, far_m)
        own_l = own_l * jnp.exp2((own_m - top) * POWER)
        far_l = far_l * jnp.exp2((far_m - top) * POWER)
        total = own_l + far_l
        r.att[h * HEAD : (h + 1) * HEAD] = (
            r.own_in[h].astype(f32) * (own_l / total) + r.far_in[h].astype(f32) * (far_l / total)
        ).astype(bf16)
    pooled = lax.dot_general(window, r.att[...], contract_last, preferred_element_type=f32)
    r.pool_out[...] = pooled[:crows].astype(bf16)
    r.pool_all[t] = r.pool_out[...]
    for i in range(TP):
        r.rim_out[i : i + 1, :] = pooled[crows : crows + 1, i * HEAD : (i + 1) * HEAD]
    r.rim_in[t] = r.rim_out[...]
    pool_gather = to_group(lambda peer: r.pool_out, r.pool_all.at[t])
    pool_gather += to_group(lambda peer: r.rim_out, r.rim_in.at[t])
    rim_kind = len(used) + len(sometimes)
    rim_next = [
        remote(r.rim_out, r.rim_prev, (lax.rem(s + 1, 16), lax.rem(t + off, TP)), always=False,
               arrival=rim_kind)
        for off in range(TP)
    ]

    @pl.when(t == TP - 1)
    def _():
        go(rim_next)

    loads["down_w"].wait()
    r.hidden_grad[...] = lax.dot_general(
        r.gg[...], r.down_w[...], contract_last, preferred_element_type=f32
    )
    loads["gate_w"].wait()
    loads["up_w"].wait()
    landed(fine_gather + pool_gather + rim_next[:1])
    for i in range(TP):
        source = r.rim_prev if i == 0 else r.rim_in.at[i - 1]
        rim = jnp.concatenate([source[h : h + 1, :] for h in range(TP)], axis=1)
        if i == 0:
            rim = jnp.where(s > 0, rim, 0.0)
        r.pool_all[i] = (r.pool_all[i].astype(f32) + jnp.where(first_row, rim, 0.0)).astype(bf16)
    coarse_all = jnp.dot(
        r.pool_all[...].reshape(group, TP * HEAD), r.out_w[...], preferred_element_type=f32
    )
    coarse_all = (coarse_all + r.fine_all[...].astype(f32)) / SHORTEN
    r.coarse_all[...] = coarse_all
    rstd_all = lax.rsqrt(jnp.mean(coarse_all * coarse_all, axis=-1, keepdims=True) + 1e-05)
    r.ng[...] = (coarse_all * rstd_all * gain_ref[...]).astype(bf16)
    coarse = r.coarse_all[mine, :]
    rstd = lax.rsqrt(jnp.mean(coarse * coarse, axis=-1, keepdims=True) + 1e-05)
    base = coarse * rstd

    norm_columns = to_columns(r.ng, r.ng_all, 15)
    gate = lax.dot_general(r.ng[...], r.gate_w[...], contract_last, preferred_element_type=f32)
    up_v = lax.dot_general(r.ng[...], r.up_w[...], contract_last, preferred_element_type=f32)
    sig = jax.nn.sigmoid(gate)
    act = gate * sig
    above, below, across = (lax.rem(y + dy, 4) for dy in (1, 3, 2))
    cut = group // 2
    parts = (pl.ds(0, cut), pl.ds(cut, cut))

    def ring(i, source, piece, device):
        ref = r.hgu.at[i, source, parts[piece], :]
        return remote(ref, ref, (device, t))

    def around(i):
        return (
            go([ring(i, y, 0, up), ring(i, y, 1, up)]),
            go([ring(i, y, 1, down), ring(i, y, 0, down)]),
        )

    rings = []
    r.hgu[0, y] = (act * up_v).astype(bf16)
    rings.append(around(0))
    r.hgu[1, y] = (
        r.hidden_grad[...] * up_v * sig * (1.0 + gate * (1.0 - sig))
    ).astype(bf16)
    rings.append(around(1))
    r.hgu[2, y] = (r.hidden_grad[...] * act).astype(bf16)
    rings.append(around(2))

    part = jnp.dot(r.hgu[0, y], r.down_w[...], preferred_element_type=f32)
    r.down_out[...] = part.astype(bf16).reshape(r.down_out.shape)
    r.down_in[t] = r.down_out[t]
    down_sum = to_group(lambda peer: r.down_out.at[peer], r.down_in.at[t])
    part = jnp.dot(r.hgu[1, y], r.gate_w[...], preferred_element_type=f32) + jnp.dot(
        r.hgu[2, y], r.up_w[...], preferred_element_type=f32
    )
    r.norm_out[...] = part.astype(bf16).reshape(r.norm_out.shape)
    r.norm_in[t] = r.norm_out[t]
    norm_sum = to_group(lambda peer: r.norm_out.at[peer], r.norm_in.at[t])
    fold_row(r.gain_out, jnp.sum(part * (r.coarse_all[...] * rstd_all), axis=0, keepdims=True))
    r.gain_in[t] = r.gain_out[...]
    gain_sum = to_group(lambda peer: r.gain_out, r.gain_in.at[t])

    projected = lax.dot_general(r.att[...], r.out_w[...], contract_first, preferred_element_type=f32)
    r.stream[...] = (r.fine[...].astype(f32) + projected).astype(bf16)

    def pass_on(i):
        ring_up, ring_down = rings[i]
        landed(ring_up[:1])
        first = go([ring(i, below, 0, up)])
        landed(ring_down[:1])
        return first + go([ring(i, above, 1, down)])

    on = [pass_on(0)]

    landed(gain_sum)
    r.gain_mid[...] = jnp.sum(r.gain_in[...], axis=0)
    r.gain_half[block] = r.gain_mid[...]
    gain_group = go([
        remote(r.gain_mid, r.gain_half.at[block], (half * 8 + lax.rem(block + off, 8), t))
        for off in range(1, 8)
    ])

    landed(down_sum)
    coarse_out = coarse + jnp.sum(r.down_in[...].astype(f32), axis=0)
    spread = (crows, SHORTEN, D)
    section_ref[...] = (
        (r.stream[...].astype(f32).reshape(spread) + coarse_out[:, None, :])
        .reshape(tok, D)
        .astype(bf16)
    )
    on.append(pass_on(1))

    landed(norm_sum)
    normed_grad = jnp.sum(r.norm_in[...].astype(f32), axis=0)
    scaled = normed_grad * gain_ref[...]
    coarse_total = r.coarse_grad[...] + rstd * (
        scaled - base * jnp.mean(scaled * base, axis=-1, keepdims=True)
    )
    fold_row(r.follow_out, coarse_total[0:1])
    follow = remote(r.follow_out, r.follow_in, before)
    follow.start()

    on.append(pass_on(2))

    outs = (down_grad_ref, gate_grad_ref, up_grad_ref)

    def term(i):
        landed(rings[i][0][1:] + rings[i][1][1:] + on[i])
        right = r.gg_all if i == 0 else r.ng_all
        left = r.hgu[i].reshape(4 * group, hid)
        r.term[i] = lax.dot_general(left, right[...], contract_first, preferred_element_type=f32)
        for p in range(2):
            r.sib_out[i, p] = r.term[i, :, lanes(2 * p + 1 - core)].astype(bf16)
        return go([remote(r.sib_out.at[i], r.sib_in.at[i], (sib, t))])

    def join(i):
        landed(to_sib[i : i + 1])
        r.term_out[i] = (
            r.term[i, :, lanes(2 * (1 - half) + core)] + r.sib_in[i, 1 - half].astype(f32)
        ).astype(bf16)
        copies = go([remote(r.term_out.at[i], r.term_in.at[i], (partner, t))])
        outs[i][...] = r.term[i, :, lanes(2 * half + core)] + r.sib_in[i, half].astype(f32)
        return copies

    landed(grad_columns)
    to_sib = term(0)

    landed(norm_columns)
    to_sib += term(1)
    terms = join(0)

    to_sib += term(2)
    terms += join(1)

    follow.wait_recv()
    following = jnp.where(flat < number - 1, flat_row(r.follow_in), 0.0)
    ahead = jnp.concatenate([coarse_total[1:], following], axis=0)
    place = lax.broadcasted_iota(jnp.int32, spread, 1)
    contrib = jnp.where(place == 0, coarse_total[:, None, :], ahead[:, None, :])
    stream_grad_ref[...] = (
        (r.cot[...].astype(f32).reshape(spread) + contrib / SHORTEN).reshape(tok, D).astype(bf16)
    )

    landed(gain_group)
    r.gain_far_out[...] = jnp.sum(r.gain_half[...], axis=0)
    gain_far = remote(r.gain_far_out, r.gain_far_in, (partner, t))
    gain_far.start()
    terms += join(2)
    gain_far.wait_recv()
    gain_grad_ref[...] = flat_row(r.gain_far_out) + flat_row(r.gain_far_in)
    for i in range(3):
        terms[i].wait_recv()
        outs[i][...] = outs[i][...] + r.term_in[i].astype(f32)

    for cp in used:
        cp.wait_send()

    @pl.when(t == TP - 1)
    def _():
        for cp in rim_next:
            cp.wait_send()

    @pl.when(half == 1)
    def _():
        q_over.wait_send()

    @pl.when(half == 0)
    def _():
        for cp in far_back:
            cp.wait_send()


def hand_over_kernel(*refs):
    count = (len(refs) - 2) // 3
    ins, outs, held = refs[:count], refs[count : 2 * count], refs[2 * count : 3 * count]
    arrive, leave = refs[-2:]
    first = [pltpu.make_async_copy(a, b, arrive.at[i]) for i, (a, b) in enumerate(zip(ins, held))]
    second = [pltpu.make_async_copy(a, b, leave.at[i]) for i, (a, b) in enumerate(zip(held, outs))]
    for cp in first:
        cp.start()
    for one, two in zip(first, second):
        one.wait()
        two.start()
    for cp in second:
        cp.wait()


def on_device(
    fine_stream,
    queries,
    keys,
    values,
    out_weight,
    norm_gain,
    gate_weight,
    up_weight,
    down_weight,
    cotangent,
):
    tok = fine_stream.shape[0]
    hid = gate_weight.shape[1]
    seq = lax.axis_size("seq")
    f32, bf16 = jnp.float32, jnp.bfloat16
    vmem, hbm = pl.BlockSpec(memory_space=pltpu.VMEM), pl.BlockSpec(memory_space=pltpu.HBM)
    scratch = scratch_of(tok, hid, seq)
    shapes = (
        jax.ShapeDtypeStruct((tok, D), bf16),
        jax.ShapeDtypeStruct((tok, D), bf16),
        jax.ShapeDtypeStruct((hid, D // seq), f32),
        jax.ShapeDtypeStruct((hid, D // seq), f32),
        jax.ShapeDtypeStruct((hid, D // seq), f32),
        jax.ShapeDtypeStruct((1, D), f32),
    )
    outs = pl.pallas_call(
        lambda *refs: section_kernel(tuple(scratch), *refs),
        out_shape=shapes,
        in_specs=[hbm] * 5 + [vmem] + [hbm] * 4,
        out_specs=(vmem,) * 6,
        scratch_shapes=list(scratch.values()),
        compiler_params=pltpu.CompilerParams(
            collective_id=0, has_side_effects=True, vmem_limit_bytes=60 * 1024 * 1024
        ),
        name="section",
    )(
        queries, keys, values, fine_stream, cotangent, norm_gain.reshape(1, D),
        out_weight, gate_weight.T, up_weight.T, down_weight,
    )
    section_out, stream_grad, gate_grad, up_grad, down_grad, gain_grad = pl.pallas_call(
        hand_over_kernel,
        out_shape=shapes,
        in_specs=[hbm] * 6,
        out_specs=(hbm,) * 6,
        scratch_shapes=[pltpu.VMEM(shape.shape, shape.dtype) for shape in shapes]
        + [pltpu.SemaphoreType.DMA((6,)), pltpu.SemaphoreType.DMA((6,))],
        compiler_params=pltpu.CompilerParams(vmem_limit_bytes=60 * 1024 * 1024),
        name="hand_over",
    )(*outs)
    return (section_out, stream_grad, gate_grad.T, up_grad.T, down_grad, gain_grad.reshape(D))


def solution(mesh):
    return jax.shard_map(
        on_device,
        mesh=mesh,
        in_specs=(
            P(("seq", "tp"), None),
            P(("seq", "tp"), None),
            P(("seq", "tp"), None),
            P(("seq", "tp"), None),
            P(),
            P(),
            P(None, "tp"),
            P(None, "tp"),
            P("tp", None),
            P(("seq", "tp"), None),
        ),
        out_specs=(
            P(("seq", "tp"), None),
            P(("seq", "tp"), None),
            P("seq", "tp"),
            P("seq", "tp"),
            P("tp", "seq"),
            P(),
        ),
        check_vma=False,
    )
```
